256 devices in a mesh: seq: 32 (over x, z_lo, core), tp: 8 (over y, z_hi).
Axes of the slice: x: 4, y: 4, z: 8 (z_hi: 2, z_lo: 4; z = z_hi * 4 + z_lo), core: 2. Of those that a mesh axis runs over, the one named last changes fastest.
Arguments:
- prompt: bfloat16 [32768, 8192], P(('seq', 'tp')), may hold values from -6 to 6
- kv_weight: bfloat16 [8192, 2048], P('seq', 'tp'), may hold values from -0.0625 to 0.0625
- norm_gain: bfloat16 [8192], replicated, may hold values from 0.099609375 to 1.8984375
- kv_cache: bfloat16 [3072, 128, 8, 256], P('seq', None, 'tp'), may hold values from -8 to 8
- block_table: int32 [3, 1024], P(None, 'seq'), may hold values from 0 to 95, as said below
- context_len: int32 [3], replicated, may hold values from 1 to 131072, as said below
- dest_shard: int32 [256, 1], replicated, may hold values from 0 to 31; in each aligned block of 8 rows (0 to 7, 8 to 15, ...) no two rows name the same one
- new_query: bfloat16 [4, 11, 64, 128], P(None, None, 'tp'), may hold values from -16 to 16
- new_keyval: bfloat16 [4, 11, 8, 256], P(None, None, 'tp'), may hold values from -6 to 6
- out_weight: bfloat16 [8192, 8192], P('tp', 'seq'), may hold values from -0.0625 to 0.0625
Outputs:
- landed: bfloat16 [1024, 128, 8, 256], P('seq', None, 'tp')
- decoded: bfloat16 [4, 11, 8192], P(None, None, 'seq')
The draws below stay inside these ranges and needn't reach their ends.
Inputs may be any that keep to these rules, and one draw needn't show every extreme that they name: `block_table`: the columns k * 32 to (k + 1) * 32 - 1 of all rows together name each page 0 to 95 exactly once, for every k. `context_len`: some request has a context of exactly 131072. `dest_shard`: within each aligned block of 8 rows (the prompt blocks of one index of seq) no value appears twice.
All inputs are finite; a program needn't handle non-finite values.
Results may differ from the reference program's by a relative error of at most 0.017.
Values may be sent and summed in bfloat16 or wider, within the bound.
No kernel may reach another device: no remote copies, remote signals or barrier semaphores. Data moves between devices by JAX's collectives and lax.ppermute only.
A program may use at most 128 MiB of HBM per device.

```python
import math
import jax
import jax.numpy as jnp
import numpy as np
from jax import lax

D = 8192
Q_HEADS = 64
KV_HEADS = 8
HEAD_DIM = 128
BLOCK = 128
STEPS = 4
CACHED = 3
OWN_BLOCKS = 32
SEND_BLOCKS = 8
GROUP = 8
SPAN_BLOCKS = 32
PROMPT_TOKENS = 32768
PROMPT_BLOCKS = 256
FRESH_REQS = 8
REQUESTS = 11
CONTEXT_BLOCKS = 1024
MAX_CONTEXT = 131072
PAGES_DEV = 96
PAGES = 3072


def draw_kv_cache(key, part):
    key = jax.random.fold_in(key, 11)
    earlier = jax.random.fold_in(key, 0)
    full_shape = (PAGES, BLOCK, KV_HEADS, 2 * HEAD_DIM)
    values = jnp.clip(jax.random.normal(earlier, full_shape, jnp.float32), -6.0, 6.0)
    return values.astype(jnp.bfloat16)


def draw_new_query(key, part):
    key = jax.random.fold_in(key, 12)
    earlier = jax.random.fold_in(key, 0)
    full_shape = (STEPS, REQUESTS, Q_HEADS, HEAD_DIM)
    values = jnp.clip(3.0 * jax.random.normal(earlier, full_shape, jnp.float32), -16.0, 16.0)
    return values.astype(jnp.bfloat16)


def draw_block_table(key, part):
    key = jax.random.fold_in(key, 13)
    shards = CONTEXT_BLOCKS // OWN_BLOCKS
    shard_keys = jax.random.split(key, shards)
    orders = jax.vmap(lambda single: jax.random.permutation(single, PAGES_DEV))(shard_keys)
    table = orders.reshape(shards, CACHED, OWN_BLOCKS).transpose(1, 0, 2).reshape(CACHED, CONTEXT_BLOCKS)
    return table.astype(jnp.int32)


def draw_context_len(key, part):
    key = jax.random.fold_in(key, 14)
    earlier, later = jax.random.split(key)
    lengths = jax.random.randint(earlier, (CACHED,), 1, MAX_CONTEXT + 1)
    chosen = jax.random.randint(later, (), 0, CACHED)
    return jnp.where(jnp.arange(CACHED) == chosen, MAX_CONTEXT, lengths).astype(jnp.int32)


def steps_of(own_key, extent, cuts, low, largest):
    level, own = 1.0, jax.random.fold_in(own_key, 6)
    for axis_at, shards_of in cuts:
        draws = jnp.exp(jax.random.uniform(jax.random.fold_in(own, axis_at), (shards_of,), jnp.float32, low / len(cuts), largest / len(cuts)))
        level = level * jnp.repeat(draws, extent[axis_at] // shards_of).reshape([-1 if axis == axis_at else 1 for axis in range(len(extent))])
    return level


def shared_out(rng, own, number, rows, count, top, most, slope):
    ranking = jax.random.permutation(rng, count)
    heavy_load, common = portions_of(count, rows * top, most, slope, True), portions_of(count, rows * top, most, slope, False)
    places = jnp.arange(count)

    def named(sizes, offset_by):
        used = int((sizes > 0).sum())
        fixed = max(1, used // 4)
        passed = fixed + (places - fixed + offset_by * (used - fixed)) % max(1, count - fixed)
        return jnp.zeros((count,), jnp.int32).at[ranking[jnp.where(places < fixed, places, passed)]].set(jnp.asarray(sizes, jnp.int32))

    sizes = jnp.where(number % 4 == 0, named(heavy_load, number // 4), named(common, number - number // 4 - 1))
    mixed = jax.random.permutation(jax.random.fold_in(own, 3), count)
    giver, sink = mixed[0:count // 2 * 2:2], mixed[1:count // 2 * 2:2]
    slack = jnp.minimum(sizes[giver] - 1, most - sizes[sink]) // 2
    slack = jnp.where((giver == ranking[0]) | (sink == ranking[0]) | (sizes[sink] == 0), 0, jnp.maximum(slack, 0))
    passed = jax.random.randint(jax.random.fold_in(own, 4), (count // 2,), 0, 1 << 20) % (slack + 1)
    sizes = sizes.at[giver].add(-passed).at[sink].add(passed)
    members = jnp.searchsorted(jnp.cumsum(sizes), jnp.arange(rows * top), side="right").astype(jnp.int32)
    table = members.reshape(top, rows).T
    table = table[jax.random.permutation(jax.random.fold_in(own, 1), rows)]
    offset_by = jax.random.randint(jax.random.fold_in(own, 2), (rows, 1), 0, top)
    return jnp.take_along_axis(table, (jnp.arange(top)[None, :] + offset_by) % top, axis=1)


def portions_of(count, total, limit, slope, full):
    loads = [(1 << 20) // math.isqrt(standing ** slope) + 1 for standing in range(1, count + 1)]
    largest = limit if full else min(limit, max(-(-total // count), total * loads[0] // sum(loads)))
    least = 1 if total - largest >= count - 1 else 0
    holding, spare = [largest] + [least] * (count - 1), total - largest - least * (count - 1)
    while spare > 0:
        movable = [i for i in range(1, count) if holding[i] < largest] or [i for i in range(1, count) if holding[i] < limit]
        pool, left = sum([loads[i] for i in movable]), spare
        for i in movable:
            extra = min(limit - holding[i], max(1, left * loads[i] // pool), spare)
            holding[i] = holding[i] + extra
            spare = spare - extra
    return np.array(holding)


def scatter_about(key, shape, scale, most, cuts=(), kind=jnp.bfloat16):
    level = steps_of(key, shape, cuts, -0.22, 0.18) if cuts else 1.0
    values = jax.random.normal(key, shape, jnp.float32) * scale * level
    return jnp.minimum(jnp.maximum(values, -most), most).astype(kind)


def setup_inputs(seed: int = 0) -> dict:
    keys = jax.random.split(jax.random.key(seed), 11)
    prompt = scatter_about(keys[0], (PROMPT_TOKENS, D), 1.0, 6.0, ((0, 256),))
    kv_weight = scatter_about(keys[1], (D, KV_HEADS * 2 * HEAD_DIM), D ** -0.5, 0.0625, ((0, 32), (1, 8)))
    norm_gain = jnp.clip(1.0 + 0.18 * jax.random.normal(keys[2], (D,), jnp.float32), 0.099609375, 1.8984375).astype(jnp.bfloat16)
    kv_cache = draw_kv_cache(jax.random.fold_in(keys[10], 71), 0)
    block_table = draw_block_table(jax.random.fold_in(keys[10], 71), 0)
    context_len = draw_context_len(jax.random.fold_in(keys[10], 71), 0)
    dest_shard_keys = jax.random.split(jax.random.fold_in(keys[6], 1), PROMPT_BLOCKS // SEND_BLOCKS)
    dest_shard_turns = jax.random.permutation(jax.random.fold_in(keys[6], 3), PROMPT_BLOCKS // SEND_BLOCKS)
    dest_shard = jax.vmap(lambda own, number: shared_out(jax.random.fold_in(keys[6], 2), own, number, SEND_BLOCKS, PROMPT_BLOCKS // SEND_BLOCKS, 1, 1, 2))(dest_shard_keys, dest_shard_turns).reshape((PROMPT_BLOCKS, 1))
    new_query = draw_new_query(jax.random.fold_in(keys[10], 71), 0)
    new_keyval = scatter_about(keys[8], (STEPS, REQUESTS, KV_HEADS, 2 * HEAD_DIM), 1.0, 6.0, ((2, 8),))
    out_weight = scatter_about(keys[9], (Q_HEADS * HEAD_DIM, D), (Q_HEADS * HEAD_DIM) ** -0.5, 0.0625, ((0, 8), (1, 32)))
    return dict(prompt=prompt, kv_weight=kv_weight, norm_gain=norm_gain, kv_cache=kv_cache, block_table=block_table, context_len=context_len, dest_shard=dest_shard, new_query=new_query, new_keyval=new_keyval, out_weight=out_weight)


EPSILON = 1e-05
NEGATIVE = -1e+30

def norm_rows(rows, gain):
    wide = rows.astype(jnp.float32)
    factor = lax.rsqrt(lax.optimization_barrier(jnp.mean(wide * wide, axis=-1, keepdims=True)) + EPSILON)
    return (wide * factor * gain.astype(jnp.float32)).astype(jnp.bfloat16)

def rounded(values):
    narrow = lax.optimization_barrier(values.astype(jnp.bfloat16))
    return narrow.astype(jnp.float32)

def block_stats(query_matrix, keyval, usable):
    head_feature_width = query_matrix.shape[-1]
    key_portion = keyval[:, :, :head_feature_width].astype(jnp.float32)
    value_portion = keyval[:, :, head_feature_width:].astype(jnp.float32)
    logit_scores = jnp.einsum('tmyi,umi->tmyu', query_matrix, key_portion, precision=lax.Precision.HIGHEST) * head_feature_width ** (-0.5)
    masked = jnp.where(usable, logit_scores, NEGATIVE)
    block_peak = lax.optimization_barrier(jnp.max(masked, axis=-1))
    softmax_weight = rounded(jnp.where(usable, jnp.exp(masked - block_peak[..., None]), 0.0))
    block_total = lax.optimization_barrier(jnp.sum(softmax_weight, axis=-1))
    block_running_sum = jnp.einsum('mitv,vip->mitp', softmax_weight, value_portion, precision=lax.Precision.HIGHEST)
    return (block_peak, block_total, block_running_sum)

def finish(peaks, totals, accs, fresh_parts):
    top = jnp.maximum(lax.optimization_barrier(jnp.max(peaks, axis=0)), fresh_parts[0])
    scale_blocks = jnp.exp(peaks - top[None])
    scale_fresh = jnp.exp(fresh_parts[0] - top)
    total = lax.optimization_barrier(jnp.sum(scale_blocks * totals, axis=0)) + scale_fresh * fresh_parts[1]
    acc = lax.optimization_barrier(jnp.sum(scale_blocks[..., None] * accs, axis=0)) + scale_fresh[..., None] * fresh_parts[2]
    return (acc / total[..., None]).astype(jnp.bfloat16)

def reference(prompt, kv_weight, norm_gain, kv_cache, block_table, context_len, dest_shard, new_query, new_keyval, out_weight):
    weight_wide = kv_weight.astype(jnp.float32)

    def project(rows):
        normed = norm_rows(rows, norm_gain).astype(jnp.float32)
        return jnp.dot(normed, weight_wide, precision=lax.Precision.HIGHEST).astype(jnp.bfloat16)
    keyval = lax.map(project, prompt.reshape(PROMPT_BLOCKS, BLOCK, D))
    blocks = keyval.reshape(PROMPT_BLOCKS, BLOCK, KV_HEADS, 2 * HEAD_DIM)
    sources = PROMPT_BLOCKS // SEND_BLOCKS
    by_source = blocks.reshape(sources, SEND_BLOCKS, BLOCK, KV_HEADS, 2 * HEAD_DIM)
    targets = dest_shard[:, 0].reshape(sources, SEND_BLOCKS)

    def land(target):
        chosen = (targets == target)[:, :, None, None, None]
        picked = jnp.where(chosen, by_source, jnp.zeros((), jnp.bfloat16))
        return lax.optimization_barrier(jnp.sum(picked, axis=1, dtype=jnp.float32)).astype(jnp.bfloat16)
    landed = lax.map(land, jnp.arange(sources, dtype=jnp.int32)).reshape(sources * sources, BLOCK, KV_HEADS, 2 * HEAD_DIM)
    queries_all = new_query.astype(jnp.float32).reshape(STEPS, REQUESTS, KV_HEADS, GROUP, HEAD_DIM)
    causal = (jnp.arange(STEPS)[:, None] >= jnp.arange(STEPS)[None, :])[:, None, None, :]
    everywhere = jnp.ones((1, 1, 1, BLOCK), dtype=bool)

    def old_row(row):
        query_matrix = lax.dynamic_index_in_dim(queries_all, row, 1, keepdims=False)

        def per_block(column):
            page_id = column // OWN_BLOCKS * PAGES_DEV + block_table[row, column]
            keyval_block = lax.dynamic_index_in_dim(kv_cache, page_id, 0, keepdims=False)
            position = column * BLOCK + jnp.arange(BLOCK, dtype=jnp.int32)
            usable = (position < context_len[row])[None, None, None, :]
            return block_stats(query_matrix, keyval_block, usable)
        peaks, totals, accs = lax.map(per_block, jnp.arange(CONTEXT_BLOCKS, dtype=jnp.int32))
        fresh = lax.dynamic_index_in_dim(new_keyval, row, 1, keepdims=False)
        return finish(peaks, totals, accs, block_stats(query_matrix, fresh, causal))

    def new_row(index):
        row = CACHED + index
        query_matrix = lax.dynamic_index_in_dim(queries_all, row, 1, keepdims=False)

        def per_block(column):
            keyval_block = lax.dynamic_index_in_dim(blocks, index * SPAN_BLOCKS + column, 0, keepdims=False)
            return block_stats(query_matrix, keyval_block, everywhere)
        peaks, totals, accs = lax.map(per_block, jnp.arange(SPAN_BLOCKS, dtype=jnp.int32))
        fresh = lax.dynamic_index_in_dim(new_keyval, row, 1, keepdims=False)
        return finish(peaks, totals, accs, block_stats(query_matrix, fresh, causal))
    old_out = lax.map(old_row, jnp.arange(CACHED, dtype=jnp.int32))
    new_out = lax.map(new_row, jnp.arange(FRESH_REQS, dtype=jnp.int32))
    attended = jnp.concatenate([old_out, new_out], axis=0)
    attended = jnp.transpose(attended, (1, 0, 2, 3, 4)).reshape(STEPS * REQUESTS, Q_HEADS * HEAD_DIM)
    decoded = jnp.dot(attended.astype(jnp.float32), out_weight.astype(jnp.float32), precision=lax.Precision.HIGHEST)
    decoded = decoded.astype(jnp.bfloat16).reshape(STEPS, REQUESTS, D)
    return (landed, decoded)
```

```python
import jax
import jax.numpy as jnp
from jax import lax
from jax.sharding import Mesh, PartitionSpec as P

EPSILON = 1e-05
NEGATIVE = -1e30
CHUNKS = 1
SIZES = (4, 2, 2, 2, 4, 2)
NAMES = ("x", "zp", "zq", "c", "y", "zh")
SEQ = ("x", "zp", "zq", "c")
TP = ("y", "zh")
RING = ("zh", "zp", "zq")
QUAD = ("zq", "c")
UP = [(i, (i + 1) % 4) for i in range(4)]
DOWN = [(i, (i - 1) % 4) for i in range(4)]
SWAP = [(0, 1), (1, 0)]


def norm_rows(rows, gain):
    wide = rows.astype(jnp.float32)
    factor = lax.rsqrt(jnp.mean(wide * wide, axis=-1, keepdims=True) + EPSILON)
    return (wide * factor * gain.astype(jnp.float32)).astype(jnp.bfloat16)


def spread(values, axes, count):
    copies = jnp.broadcast_to(values[None], (count,) + values.shape)
    return lax.all_to_all(copies, axes, 0, 0, tiled=True)


def paged_stats(query_matrix, keyval, usable):
    width = query_matrix.shape[-1]
    logit_scores = jnp.einsum(
        "trgd,rpbd->trgpb", query_matrix, keyval[..., :width], preferred_element_type=jnp.float32
    ) * width ** (-0.5)
    masked = jnp.where(usable, logit_scores, NEGATIVE)
    row_peak = jnp.max(masked, axis=(-1, -2))
    weight = jnp.where(usable, jnp.exp(masked - row_peak[..., None, None]), 0.0).astype(jnp.bfloat16)
    total = jnp.sum(weight.astype(jnp.float32), axis=(-1, -2))
    acc = jnp.einsum(
        "trgpb,rpbd->trgd", weight, keyval[..., width:], preferred_element_type=jnp.float32
    )
    return row_peak, total, acc


def step_stats(query_matrix, keyval):
    width = query_matrix.shape[-1]
    steps = query_matrix.shape[0]
    logit_scores = jnp.einsum(
        "trgd,urd->trgu", query_matrix, keyval[..., :width], preferred_element_type=jnp.float32
    ) * width ** (-0.5)
    usable = (jnp.arange(steps)[:, None] >= jnp.arange(steps)[None, :])[:, None, None, :]
    masked = jnp.where(usable, logit_scores, NEGATIVE)
    row_peak = jnp.max(masked, axis=-1)
    weight = jnp.where(usable, jnp.exp(masked - row_peak[..., None]), 0.0).astype(jnp.bfloat16)
    total = jnp.sum(weight.astype(jnp.float32), axis=-1)
    acc = jnp.einsum(
        "trgu,urd->trgd", weight, keyval[..., width:], preferred_element_type=jnp.float32
    )
    return row_peak, total, acc


def pack(peak, total, acc):
    rows = acc.shape[0]
    rest = jnp.zeros((rows, 126), jnp.float32)
    return jnp.concatenate([acc, peak[:, None], total[:, None], rest], axis=1)


def merge(packed, step_packed):
    parts = jnp.concatenate([packed, step_packed[None]], axis=0)
    acc, peak, total = parts[..., :128], parts[..., 128:129], parts[..., 129:130]
    factor = jnp.exp(peak - jnp.max(peak, axis=0, keepdims=True))
    return (jnp.sum(factor * acc, axis=0) / jnp.sum(factor * total, axis=0)).astype(jnp.bfloat16)


def gather_weight(kv_weight, x_at, core):
    rows, columns = kv_weight.shape
    mine = spread(kv_weight, RING, 8)
    lower = lax.ppermute(mine, "x", UP)
    upper = lax.ppermute(mine, "x", DOWN)
    across = jnp.concatenate(
        [lax.ppermute(lower[:4], "x", UP), lax.ppermute(upper[4:], "x", DOWN)], axis=0
    )
    whole = jnp.zeros((2, 4, 4, 2, rows, columns), kv_weight.dtype)
    for piece, offset in ((mine, 0), (lower, 3), (upper, 1), (across, 2)):
        at = (x_at + offset) % 4
        other = lax.ppermute(piece, "c", SWAP)
        whole = lax.dynamic_update_slice(
            whole, piece.reshape(2, 1, 4, 1, rows, columns), (0, at, 0, core, 0, 0)
        )
        whole = lax.dynamic_update_slice(
            whole, other.reshape(2, 1, 4, 1, rows, columns), (0, at, 0, 1 - core, 0, 0)
        )
    return whole.reshape(2, 32 * rows, columns)


def on_device(
    prompt,
    kv_weight,
    norm_gain,
    kv_cache,
    block_table,
    context_len,
    dest_shard,
    new_query,
    new_keyval,
    out_weight,
):
    x_at, y_at, core = lax.axis_index("x"), lax.axis_index("y"), lax.axis_index("c")
    shard = lax.axis_index(SEQ)
    quad = lax.axis_index(QUAD)
    request = shard // 4
    block_len = kv_cache.shape[1]
    width = new_query.shape[3]
    steps, requests, group = new_query.shape[:3]
    cached, own_blocks = block_table.shape

    whole = gather_weight(kv_weight, x_at, core)

    targets = lax.dynamic_index_in_dim(dest_shard.reshape(32, 4, 2), shard, 0, keepdims=False)
    order = (y_at + jnp.array([0, 3, 1, 2], jnp.int32)) % 4
    mine = jnp.take(targets, order, axis=0).T.reshape(8)
    selector = (mine[None, :] == jnp.arange(32, dtype=jnp.int32)[:, None]).astype(jnp.bfloat16)

    size = prompt.shape[0] // CHUNKS
    landed_parts, blocks_parts = [], []
    for at in range(CHUNKS):
        own = norm_rows(prompt[at * size : (at + 1) * size], norm_gain)
        lower = lax.ppermute(own, "y", UP)
        upper = lax.ppermute(own, "y", DOWN)
        across = [
            lax.ppermute(lower[: size // 2], "y", UP),
            lax.ppermute(upper[size // 2 :], "y", DOWN),
        ]
        rows = jnp.concatenate([own, lower, upper] + across, axis=0)
        keyval = jnp.stack(
            [
                jnp.dot(rows, whole[h], preferred_element_type=jnp.float32).astype(jnp.bfloat16)
                for h in range(2)
            ]
        )
        blocks = lax.all_to_all(keyval, "zh", 0, 0, tiled=True).reshape(8, size, 2 * width)
        outgoing = jnp.dot(
            selector, blocks.reshape(8, -1), preferred_element_type=jnp.float32
        ).astype(jnp.bfloat16)
        outgoing = outgoing.reshape(32, size, 2 * width)
        landed_parts.append(lax.all_to_all(outgoing, SEQ, 0, 0, tiled=True))
        blocks_parts.append(blocks)

    step_peak, step_total, step_acc = step_stats(new_query, new_keyval[:, :, 0])
    cached_blocks = jnp.take(kv_cache[:, :, 0], block_table, axis=0)
    position = ((shard * own_blocks + jnp.arange(own_blocks, dtype=jnp.int32)) * block_len)[
        :, None
    ] + jnp.arange(block_len, dtype=jnp.int32)[None, :]
    usable = position[None, :, :] < context_len[:, None, None]
    peak, total, acc = paged_stats(new_query[:, :cached], cached_blocks, usable[None, :, None])
    packed = pack(peak.reshape(96), total.reshape(96), acc.reshape(96, width))
    packed = lax.all_to_all(packed.reshape(32, 3, 256), SEQ, 0, 0, tiled=True)
    step_packed = pack(
        step_peak[:, :cached].reshape(96),
        step_total[:, :cached].reshape(96),
        step_acc[:, :cached].reshape(96, width),
    )
    step_packed = lax.dynamic_slice_in_dim(step_packed, shard * 3, 3, axis=0)
    old = spread(merge(packed, step_packed), SEQ, 32).reshape(steps, cached, group, width)

    blocks = jnp.concatenate([part.reshape(-1, 2 * width) for part in blocks_parts], axis=0)
    query = lax.dynamic_index_in_dim(new_query, cached + request, 1, keepdims=False)
    query = query.reshape(steps * group, width)
    scores = lax.dot_general(
        query, blocks[:, :width], (((1,), (1,)), ((), ())), preferred_element_type=jnp.float32
    ) * width ** (-0.5)
    peak = jnp.max(scores, axis=-1)
    weight = jnp.exp(scores - peak[:, None]).astype(jnp.bfloat16)
    total = jnp.sum(weight.astype(jnp.float32), axis=-1)
    acc = jnp.dot(weight, blocks[:, width:], preferred_element_type=jnp.float32)
    packed = pack(peak, total, acc).reshape(4, 8, 256)
    packed = lax.all_to_all(packed, QUAD, 0, 0, tiled=True)
    step_of = [
        lax.dynamic_index_in_dim(value, cached + request, 1, keepdims=False)
        for value in (step_peak, step_total, step_acc)
    ]
    step_packed = pack(step_of[0].reshape(32), step_of[1].reshape(32), step_of[2].reshape(32, width))
    step_packed = lax.dynamic_slice_in_dim(step_packed, quad * 8, 8, axis=0)
    new = spread(merge(packed, step_packed), SEQ, 32).reshape(8, steps, group, width)

    attended = jnp.concatenate([old, new.transpose(1, 0, 2, 3)], axis=1)
    flat_rows = attended.reshape(steps * requests, group * width)
    partial = jnp.dot(flat_rows, out_weight, preferred_element_type=jnp.float32).astype(jnp.bfloat16)
    partial = jnp.pad(partial, ((0, 4), (0, 0)))
    summed = jnp.sum(spread(partial, TP, 8).astype(jnp.float32), axis=0).astype(jnp.bfloat16)
    decoded = summed[: steps * requests].reshape(steps, requests, -1)

    landed = jnp.concatenate(landed_parts, axis=1)[:, :, None, :]
    return landed, decoded


def solution(mesh):
    fine = Mesh(mesh.devices.reshape(SIZES), NAMES)
    placed = (
        P(SEQ + TP, None),
        P(SEQ, TP),
        P(),
        P(SEQ, None, TP, None),
        P(None, SEQ),
        P(),
        P(),
        P(None, None, TP, None),
        P(None, None, TP, None),
        P(TP, SEQ),
    )
    return jax.shard_map(
        on_device,
        mesh=fine,
        in_specs=placed,
        out_specs=(P(SEQ, None, TP, None), P(None, None, SEQ)),
        check_vma=False,
    )
```

```python
import jax
import jax.numpy as jnp
from jax import lax
from jax.sharding import Mesh, PartitionSpec as P

EPSILON = 1e-05
NEGATIVE = -1e30
CHUNKS = 2
SIZES = (4, 2, 2, 2, 4, 2)
NAMES = ("x", "zp", "zq", "c", "y", "zh")
SEQ = ("x", "zp", "zq", "c")
TP = ("y", "zh")
RING = ("zh", "zp", "zq")
QUAD = ("zq", "c")
OCT = ("zq", "c", "zh")
UP = [(i, (i + 1) % 4) for i in range(4)]
DOWN = [(i, (i - 1) % 4) for i in range(4)]
SWAP = [(0, 1), (1, 0)]


def norm_rows(rows, gain):
    wide = rows.astype(jnp.float32)
    factor = lax.rsqrt(jnp.mean(wide * wide, axis=-1, keepdims=True) + EPSILON)
    return (wide * factor * gain.astype(jnp.float32)).astype(jnp.bfloat16)


def spread(values, axes, count):
    copies = jnp.broadcast_to(values[None], (count,) + values.shape)
    return lax.all_to_all(copies, axes, 0, 0, tiled=True)


def paged_stats(query_matrix, keyval, usable):
    width = query_matrix.shape[-1]
    logit_scores = jnp.einsum(
        "trgd,rpbd->trgpb", query_matrix, keyval[..., :width], preferred_element_type=jnp.float32
    ) * width ** (-0.5)
    masked = jnp.where(usable, logit_scores, NEGATIVE)
    row_peak = jnp.max(masked, axis=(-1, -2))
    weight = jnp.where(usable, jnp.exp(masked - row_peak[..., None, None]), 0.0).astype(jnp.bfloat16)
    total = jnp.sum(weight.astype(jnp.float32), axis=(-1, -2))
    acc = jnp.einsum(
        "trgpb,rpbd->trgd", weight, keyval[..., width:], preferred_element_type=jnp.float32
    )
    return row_peak, total, acc


def step_stats(query_matrix, keyval):
    width = query_matrix.shape[-1]
    steps = query_matrix.shape[0]
    logit_scores = jnp.einsum(
        "trgd,urd->trgu", query_matrix, keyval[..., :width], preferred_element_type=jnp.float32
    ) * width ** (-0.5)
    usable = (jnp.arange(steps)[:, None] >= jnp.arange(steps)[None, :])[:, None, None, :]
    masked = jnp.where(usable, logit_scores, NEGATIVE)
    row_peak = jnp.max(masked, axis=-1)
    weight = jnp.where(usable, jnp.exp(masked - row_peak[..., None]), 0.0).astype(jnp.bfloat16)
    total = jnp.sum(weight.astype(jnp.float32), axis=-1)
    acc = jnp.einsum(
        "trgu,urd->trgd", weight, keyval[..., width:], preferred_element_type=jnp.float32
    )
    return row_peak, total, acc


def pack(peak, total, acc):
    rows = acc.shape[0]
    rest = jnp.zeros((rows, 126), jnp.float32)
    return jnp.concatenate([acc, peak[:, None], total[:, None], rest], axis=1)


def merge(packed, step_packed):
    parts = jnp.concatenate([packed, step_packed[None]], axis=0)
    acc, peak, total = parts[..., :128], parts[..., 128:129], parts[..., 129:130]
    factor = jnp.exp(peak - jnp.max(peak, axis=0, keepdims=True))
    return (jnp.sum(factor * acc, axis=0) / jnp.sum(factor * total, axis=0)).astype(jnp.bfloat16)


def swap_parts(values, axes, count):
    me = lax.axis_index(axes)
    parts = [lax.dynamic_index_in_dim(values, me, 0, keepdims=False)]
    for bits in range(1, count):
        sent = lax.dynamic_index_in_dim(values, me ^ bits, 0, keepdims=False)
        parts.append(lax.ppermute(sent, axes, [(i, i ^ bits) for i in range(count)]))
    return parts


def collect(values, axes, count):
    others = [
        lax.ppermute(values, axes, [(i, i ^ bits) for i in range(count)])
        for bits in range(1, count)
    ]
    return [values] + others


def gather_weight(halves, x_at, core):
    rows, columns = halves[0].shape[1:]
    whole = jnp.zeros((2, 4, 4, 2, 2 * rows, columns), halves[0].dtype)
    for at, mine in enumerate(halves):
        lower = lax.ppermute(mine, "x", UP)
        upper = lax.ppermute(mine, "x", DOWN)
        across = jnp.concatenate(
            [lax.ppermute(lower[:4], "x", UP), lax.ppermute(upper[4:], "x", DOWN)], axis=0
        )
        for piece, offset in ((mine, 0), (lower, 3), (upper, 1), (across, 2)):
            to = (x_at + offset) % 4
            other = lax.ppermute(piece, "c", SWAP)
            shape = (2, 1, 4, 1, rows, columns)
            whole = lax.dynamic_update_slice(
                whole, piece.reshape(shape), (0, to, 0, core, at * rows, 0)
            )
            whole = lax.dynamic_update_slice(
                whole, other.reshape(shape), (0, to, 0, 1 - core, at * rows, 0)
            )
    return whole.reshape(2, 64 * rows, columns)


def on_device(
    prompt,
    kv_weight,
    norm_gain,
    kv_cache,
    block_table,
    context_len,
    dest_shard,
    new_query,
    new_keyval,
    out_weight,
):
    x_at, y_at, core = lax.axis_index("x"), lax.axis_index("y"), lax.axis_index("c")
    high = lax.axis_index("zh")
    shard = lax.axis_index(SEQ)
    quad = lax.axis_index(QUAD)
    request = shard // 4
    block_len = kv_cache.shape[1]
    width = new_query.shape[3]
    steps, requests, group = new_query.shape[:3]
    cached, own_blocks = block_table.shape

    half = kv_weight.shape[0] // 2
    halves = [spread(kv_weight[:half], RING, 8), spread(kv_weight[half:], RING, 8)]
    whole = gather_weight(halves, x_at, core)

    block_table, _ = lax.optimization_barrier((block_table, halves[0]))
    step_peak, step_total, step_acc = step_stats(new_query, new_keyval[:, :, 0])
    cached_blocks = jnp.take(kv_cache[:, :, 0], block_table, axis=0, mode="clip")
    position = ((shard * own_blocks + jnp.arange(own_blocks, dtype=jnp.int32)) * block_len)[
        :, None
    ] + jnp.arange(block_len, dtype=jnp.int32)[None, :]
    usable = position[None, :, :] < context_len[:, None, None]
    peak, total, acc = paged_stats(new_query[:, :cached], cached_blocks, usable[None, :, None])
    packed = pack(peak.reshape(96), total.reshape(96), acc.reshape(96, width))
    packed, _ = lax.optimization_barrier((packed, halves[1]))
    packed = lax.all_to_all(packed.reshape(32, 3, 256), SEQ, 0, 0, tiled=True)
    step_packed = pack(
        step_peak[:, :cached].reshape(96),
        step_total[:, :cached].reshape(96),
        step_acc[:, :cached].reshape(96, width),
    )
    step_packed = lax.dynamic_slice_in_dim(step_packed, shard * 3, 3, axis=0)
    old = spread(merge(packed, step_packed), SEQ, 32).reshape(steps, cached, group, width)

    targets = lax.dynamic_index_in_dim(dest_shard.reshape(32, 4, 2), shard, 0, keepdims=False)
    order = (y_at + jnp.array([0, 3, 1, 2], jnp.int32)) % 4
    mine = jnp.take(targets, order, axis=0, mode="clip").T
    mine = jnp.where(high == 0, mine, mine[::-1]).reshape(8)
    selector = (mine[None, :] == jnp.arange(32, dtype=jnp.int32)[:, None]).astype(jnp.bfloat16)

    query = lax.dynamic_index_in_dim(new_query, cached + request, 1, keepdims=False)
    query = query.reshape(steps * group, width)
    query_other = lax.ppermute(query, "zh", SWAP)

    size = prompt.shape[0] // CHUNKS
    landed_parts, own_parts, other_parts = [], [], []
    before = None
    for at in range(CHUNKS):
        rows_in = prompt[at * size : (at + 1) * size]
        own = norm_rows(rows_in, norm_gain)
        if before is not None:
            own, *_ = lax.optimization_barrier((own,) + before)
        lower = lax.ppermute(own, "y", UP)
        upper = lax.ppermute(own, "y", DOWN)
        before = (lower, upper)
        across = [
            lax.ppermute(lower[: size // 2], "y", UP),
            lax.ppermute(upper[size // 2 :], "y", DOWN),
        ]
        rows = jnp.concatenate([own, lower, upper] + across, axis=0)
        keyval = jnp.stack(
            [
                jnp.dot(rows, whole[h], preferred_element_type=jnp.float32).astype(jnp.bfloat16)
                for h in range(2)
            ]
        )
        kept = lax.dynamic_index_in_dim(keyval, high, 0, keepdims=False)
        given = lax.dynamic_index_in_dim(keyval, 1 - high, 0, keepdims=False)
        blocks = jnp.stack([kept, lax.ppermute(given, "zh", SWAP)]).reshape(8, -1)
        outgoing = jnp.dot(selector, blocks, preferred_element_type=jnp.float32)
        outgoing = outgoing.astype(jnp.bfloat16).reshape(32, size, 2 * width)
        if at == 0:
            outgoing, old = lax.optimization_barrier((outgoing, old))
        landed_parts.append(lax.all_to_all(outgoing, SEQ, 0, 0, tiled=True))
        own_parts.append(kept)
        other_parts.append(given)

    def stats(query, parts):
        blocks = jnp.concatenate(parts, axis=0)
        scores = lax.dot_general(
            query, blocks[:, :width], (((1,), (1,)), ((), ())), preferred_element_type=jnp.float32
        ) * width ** (-0.5)
        peak = jnp.max(scores, axis=-1)
        weight = jnp.exp(scores - peak[:, None]).astype(jnp.bfloat16)
        total = jnp.sum(weight.astype(jnp.float32), axis=-1)
        acc = jnp.dot(weight, blocks[:, width:], preferred_element_type=jnp.float32)
        return pack(peak, total, acc).reshape(4, 8, 256)

    kept, given = stats(query, own_parts), stats(query_other, other_parts)
    packed = jnp.where(
        high == 0, jnp.stack([kept, given], axis=1), jnp.stack([given, kept], axis=1)
    )
    packed = jnp.stack(swap_parts(packed.reshape(8, 8, 256), OCT, 8))
    step_of = [
        lax.dynamic_index_in_dim(value, cached + request, 1, keepdims=False)
        for value in (step_peak, step_total, step_acc)
    ]
    step_packed = pack(step_of[0].reshape(32), step_of[1].reshape(32), step_of[2].reshape(32, width))
    step_packed = lax.dynamic_slice_in_dim(step_packed, quad * 8, 8, axis=0)
    new = merge(packed, step_packed)
    new = jnp.concatenate(collect(new, ("zp", "zq"), 4), axis=0)
    new = jnp.concatenate(collect(new, "x", 4), axis=0)
    new = jnp.stack(collect(new, "c", 2)).reshape(2, 4, 4, 8, width)
    new = new.transpose(1, 2, 0, 3, 4).reshape(32, 8, width)
    new = jnp.take(new, jnp.arange(32, dtype=jnp.int32) ^ shard, axis=0, mode="clip")
    new = new.reshape(8, steps, group, width)

    attended = jnp.concatenate([old, new.transpose(1, 0, 2, 3)], axis=1)
    flat_rows = attended.reshape(steps * requests, group * width)
    partial = jnp.dot(flat_rows, out_weight, preferred_element_type=jnp.float32).astype(jnp.bfloat16)
    summed = sum(part.astype(jnp.float32) for part in collect(partial, TP, 8))
    decoded = summed.astype(jnp.bfloat16).reshape(steps, requests, -1)

    landed = jnp.concatenate(landed_parts, axis=1)[:, :, None, :]
    return landed, decoded


def solution(mesh):
    fine = Mesh(mesh.devices.reshape(SIZES), NAMES)
    placed = (
        P(SEQ + TP, None),
        P(SEQ, TP),
        P(),
        P(SEQ, None, TP, None),
        P(None, SEQ),
        P(),
        P(),
        P(None, None, TP, None),
        P(None, None, TP, None),
        P(TP, SEQ),
    )
    return jax.shard_map(
        on_device,
        mesh=fine,
        in_specs=placed,
        out_specs=(P(SEQ, None, TP, None), P(None, None, SEQ)),
        check_vma=False,
    )
```

```python
import jax
import jax.numpy as jnp
from jax import lax
from jax.sharding import Mesh, PartitionSpec as P

EPSILON = 1e-05
NEGATIVE = -1e30
SIZES = (4, 2, 2, 2, 4, 2)
NAMES = ("x", "zp", "zq", "c", "y", "zh")
SEQ = ("x", "zp", "zq", "c")
TP = ("y", "zh")
RING = ("zh", "zp", "zq")
UP = [(i, (i + 1) % 4) for i in range(4)]
DOWN = [(i, (i - 1) % 4) for i in range(4)]
SWAP = [(0, 1), (1, 0)]


def row_factor(rows):
    wide = rows.astype(jnp.float32)
    return lax.rsqrt(jnp.mean(wide * wide, axis=-1, keepdims=True) + EPSILON)


def spread(values, axes, count):
    copies = jnp.broadcast_to(values[None], (count,) + values.shape)
    return lax.all_to_all(copies, axes, 0, 0, tiled=True)


def collect(values, axes, count):
    others = [
        lax.ppermute(values, axes, [(i, i ^ bits) for i in range(count)])
        for bits in range(1, count)
    ]
    return [values] + others


def paged_stats(query_matrix, keyval, usable):
    width = query_matrix.shape[-1]
    logit_scores = jnp.einsum(
        "trgd,rpbd->trgpb", query_matrix, keyval[..., :width], preferred_element_type=jnp.float32
    ) * width ** (-0.5)
    masked = jnp.where(usable, logit_scores, NEGATIVE)
    row_peak = jnp.max(masked, axis=(-1, -2))
    weight = jnp.where(usable, jnp.exp(masked - row_peak[..., None, None]), 0.0).astype(jnp.bfloat16)
    total = jnp.sum(weight.astype(jnp.float32), axis=(-1, -2))
    acc = jnp.einsum(
        "trgpb,rpbd->trgd", weight, keyval[..., width:], preferred_element_type=jnp.float32
    )
    return row_peak, total, acc


def step_stats(query_matrix, keyval):
    width = query_matrix.shape[-1]
    steps = query_matrix.shape[0]
    logit_scores = jnp.einsum(
        "trgd,urd->trgu", query_matrix, keyval[..., :width], preferred_element_type=jnp.float32
    ) * width ** (-0.5)
    usable = (jnp.arange(steps)[:, None] >= jnp.arange(steps)[None, :])[:, None, None, :]
    masked = jnp.where(usable, logit_scores, NEGATIVE)
    row_peak = jnp.max(masked, axis=-1)
    weight = jnp.where(usable, jnp.exp(masked - row_peak[..., None]), 0.0).astype(jnp.bfloat16)
    total = jnp.sum(weight.astype(jnp.float32), axis=-1)
    acc = jnp.einsum(
        "trgu,urd->trgd", weight, keyval[..., width:], preferred_element_type=jnp.float32
    )
    return row_peak, total, acc


def pack(peak, total, acc):
    rows = acc.shape[0]
    rest = jnp.zeros((rows, 126), jnp.float32)
    return jnp.concatenate([acc, peak[:, None], total[:, None], rest], axis=1)


def merge(packed, step_packed):
    parts = jnp.concatenate([packed, step_packed[None]], axis=0)
    acc, peak, total = parts[..., :128], parts[..., 128:129], parts[..., 129:130]
    factor = jnp.exp(peak - jnp.max(peak, axis=0, keepdims=True))
    return (jnp.sum(factor * acc, axis=0) / jnp.sum(factor * total, axis=0)).astype(jnp.bfloat16)


def gather_weight(mine, x_at, core):
    rows, columns = mine.shape[1:]
    lower = lax.ppermute(mine, "x", UP)
    upper = lax.ppermute(mine, "x", DOWN)
    across = jnp.concatenate(
        [lax.ppermute(lower[:4], "x", UP), lax.ppermute(upper[4:], "x", DOWN)], axis=0
    )
    whole = jnp.zeros((2, 4, 4, 2, rows, columns), mine.dtype)
    for piece, offset in ((mine, 0), (lower, 3), (upper, 1), (across, 2)):
        at = (x_at + offset) % 4
        other = lax.ppermute(piece, "c", SWAP)
        whole = lax.dynamic_update_slice(
            whole, piece.reshape(2, 1, 4, 1, rows, columns), (0, at, 0, core, 0, 0)
        )
        whole = lax.dynamic_update_slice(
            whole, other.reshape(2, 1, 4, 1, rows, columns), (0, at, 0, 1 - core, 0, 0)
        )
    return whole.reshape(2, 32 * rows, columns)


def pack_log(peak, total, acc):
    lse = peak + jnp.log(total)
    high = lax.reduce_precision(lse, 8, 7)
    mid = lax.reduce_precision(lse - high, 8, 7)
    terms = jnp.stack([high, mid, lse - high - mid])
    terms = jnp.pad(terms, ((0, 0), (0, 96)))
    return jnp.concatenate([acc / total[:, None], terms], axis=0).astype(jnp.bfloat16)


def on_device(
    prompt,
    kv_weight,
    norm_gain,
    kv_cache,
    block_table,
    context_len,
    dest_shard,
    new_query,
    new_keyval,
    out_weight,
):
    x_at, y_at, core = lax.axis_index("x"), lax.axis_index("y"), lax.axis_index("c")
    high = lax.axis_index("zh")
    shard = lax.axis_index(SEQ)
    request = shard // 4
    block_len = kv_cache.shape[1]
    width = new_query.shape[3]
    steps, requests, group = new_query.shape[:3]
    cached, own_blocks = block_table.shape
    half = prompt.shape[0] // 2

    lower = lax.ppermute(prompt, "y", UP)
    upper = lax.ppermute(prompt, "y", DOWN)
    lower_half, upper_half = lower[:half], upper[half:]
    across = [lax.ppermute(lower_half, "y", UP), lax.ppermute(upper_half, "y", DOWN)]

    gain = lax.dynamic_slice_in_dim(norm_gain, shard * kv_weight.shape[0], kv_weight.shape[0])
    scaled = kv_weight.astype(jnp.float32) * gain.astype(jnp.float32)[:, None]
    first = spread(scaled.astype(jnp.bfloat16), RING, 8)
    whole = gather_weight(first, x_at, core)

    step_peak, step_total, step_acc = step_stats(new_query, new_keyval[:, :, 0])
    cached_blocks = jnp.take(kv_cache[:, :, 0], block_table, axis=0, mode="clip")
    position = ((shard * own_blocks + jnp.arange(own_blocks, dtype=jnp.int32)) * block_len)[
        :, None
    ] + jnp.arange(block_len, dtype=jnp.int32)[None, :]
    usable = position[None, :, :] < context_len[:, None, None]
    peak, total, acc = paged_stats(new_query[:, :cached], cached_blocks, usable[None, :, None])
    packed = pack(peak.reshape(96), total.reshape(96), acc.reshape(96, width))
    packed, *_ = lax.optimization_barrier((packed, lower_half, upper_half))
    old_packed = lax.all_to_all(packed.reshape(32, 3, 256), SEQ, 0, 0, tiled=True)
    old_step = pack(
        step_peak[:, :cached].reshape(96),
        step_total[:, :cached].reshape(96),
        step_acc[:, :cached].reshape(96, width),
    )
    old_step = lax.dynamic_slice_in_dim(old_step, shard * 3, 3, axis=0)

    def project(rows):
        factor = row_factor(rows)
        return jnp.stack(
            [
                (jnp.dot(rows, whole[h], preferred_element_type=jnp.float32) * factor).astype(
                    jnp.bfloat16
                )
                for h in range(2)
            ]
        )

    early = jnp.stack([project(prompt), project(lower), project(upper)], axis=1)
    given = lax.dynamic_index_in_dim(early, 1 - high, 0, keepdims=False)
    early_got = lax.ppermute(given, "zh", SWAP)
    across, _ = lax.optimization_barrier((across, given))
    late = project(jnp.concatenate(across, axis=0))
    given = lax.dynamic_index_in_dim(late, 1 - high, 0, keepdims=False)
    late_got = lax.ppermute(given, "zh", SWAP)
    early_kept = lax.dynamic_index_in_dim(early, high, 0, keepdims=False)
    late_kept = lax.dynamic_index_in_dim(late, high, 0, keepdims=False)
    blocks = jnp.concatenate([early_kept, late_kept[None], early_got, late_got[None]], axis=0)

    query = lax.dynamic_index_in_dim(new_query, cached + request, 1, keepdims=False)
    query = query.reshape(steps * group, width)
    rows = blocks.reshape(-1, 2 * width)
    scores = lax.dot_general(
        query, rows[:, :width], (((1,), (1,)), ((), ())), preferred_element_type=jnp.float32
    ) * width ** (-0.5)
    peak = jnp.max(scores, axis=-1)
    weight = jnp.exp(scores - peak[:, None]).astype(jnp.bfloat16)
    total = jnp.sum(weight.astype(jnp.float32), axis=-1)
    acc = jnp.dot(weight, rows[:, width:], preferred_element_type=jnp.float32)
    old_packed, acc = lax.optimization_barrier((old_packed, acc))
    old = merge(old_packed, old_step)
    packed = spread(jnp.concatenate([pack_log(peak, total, acc), old, jnp.zeros((10, width), jnp.bfloat16)], axis=0), SEQ, 32)

    targets = lax.dynamic_index_in_dim(dest_shard.reshape(32, 4, 2), shard, 0, keepdims=False)
    order = (y_at + jnp.array([0, 3, 1, 2], jnp.int32)) % 4
    mine = jnp.take(targets, order, axis=0, mode="clip").T
    mine = jnp.where(high == 0, mine, mine[::-1]).reshape(8)
    selector = (mine[None, :] == jnp.arange(32, dtype=jnp.int32)[:, None]).astype(jnp.bfloat16)
    outgoing = jnp.dot(selector, blocks.reshape(8, -1), preferred_element_type=jnp.float32)
    outgoing = outgoing.astype(jnp.bfloat16).reshape(32, block_len, 2 * width)
    outgoing, packed = lax.optimization_barrier((outgoing, packed))
    landed = lax.all_to_all(outgoing, SEQ, 0, 0, tiled=True)[:, :, None, :]

    old = packed[:, 35:38].reshape(steps, cached, group, width)
    packed = packed.astype(jnp.float32).reshape(8, 4, 48, width)
    lse = packed[:, :, 32, :32] + packed[:, :, 33, :32] + packed[:, :, 34, :32]
    acc = packed[:, :, :32]
    step_peak = step_peak[:, cached:].transpose(1, 0, 2).reshape(8, 32)
    step_total = step_total[:, cached:].transpose(1, 0, 2).reshape(8, 32)
    step_acc = step_acc[:, cached:].transpose(1, 0, 2, 3).reshape(8, 32, width)
    top = jnp.maximum(jnp.max(lse, axis=1), step_peak)
    factor = jnp.exp(lse - top[:, None])
    step_factor = jnp.exp(step_peak - top)
    total = jnp.sum(factor, axis=1) + step_factor * step_total
    acc = jnp.sum(factor[..., None] * acc, axis=1) + step_factor[..., None] * step_acc
    new = (acc / total[..., None]).astype(jnp.bfloat16).reshape(8, steps, group, width)

    attended = jnp.concatenate([old, new.transpose(1, 0, 2, 3)], axis=1)
    flat_rows = attended.reshape(steps * requests, group * width)
    partial = jnp.dot(flat_rows, out_weight, preferred_element_type=jnp.float32).astype(jnp.bfloat16)
    summed = sum(part.astype(jnp.float32) for part in collect(partial, TP, 8))
    decoded = summed.astype(jnp.bfloat16).reshape(steps, requests, -1)
    return landed, decoded


def solution(mesh):
    fine = Mesh(mesh.devices.reshape(SIZES), NAMES)
    placed = (
        P(SEQ + TP, None),
        P(SEQ, TP),
        P(),
        P(SEQ, None, TP, None),
        P(None, SEQ),
        P(),
        P(),
        P(None, None, TP, None),
        P(None, None, TP, None),
        P(TP, SEQ),
    )
    return jax.shard_map(
        on_device,
        mesh=fine,
        in_specs=placed,
        out_specs=(P(SEQ, None, TP, None), P(None, None, SEQ)),
        check_vma=False,
    )
```

```python
import jax
import jax.numpy as jnp
from jax import lax
from jax.sharding import Mesh, PartitionSpec as P

EPSILON = 1e-05
NEGATIVE = -1e30
SIZES = (4, 2, 2, 2, 4, 2)
NAMES = ("x", "zp", "zq", "c", "y", "zh")
SEQ = ("x", "zp", "zq", "c")
TP = ("y", "zh")
RING = ("zh", "zp", "zq")
UP = [(i, (i + 1) % 4) for i in range(4)]
DOWN = [(i, (i - 1) % 4) for i in range(4)]
SWAP = [(0, 1), (1, 0)]


def row_factor(rows):
    wide = rows.astype(jnp.float32)
    return lax.rsqrt(jnp.mean(wide * wide, axis=-1, keepdims=True) + EPSILON)


def spread(values, axes, count):
    copies = jnp.broadcast_to(values[None], (count,) + values.shape)
    return lax.all_to_all(copies, axes, 0, 0, tiled=True)


def collect(values, axes, count):
    others = [
        lax.ppermute(values, axes, [(i, i ^ bits) for i in range(count)])
        for bits in range(1, count)
    ]
    return [values] + others


def paged_stats(query_matrix, keyval, usable):
    width = query_matrix.shape[-1]
    logit_scores = jnp.einsum(
        "trgd,rpbd->trgpb", query_matrix, keyval[..., :width], preferred_element_type=jnp.float32
    ) * width ** (-0.5)
    masked = jnp.where(usable, logit_scores, NEGATIVE)
    row_peak = jnp.max(masked, axis=(-1, -2))
    weight = jnp.where(usable, jnp.exp(masked - row_peak[..., None, None]), 0.0).astype(jnp.bfloat16)
    total = jnp.sum(weight.astype(jnp.float32), axis=(-1, -2))
    acc = jnp.einsum(
        "trgpb,rpbd->trgd", weight, keyval[..., width:], preferred_element_type=jnp.float32
    )
    return row_peak, total, acc


def step_stats(query_matrix, keyval):
    width = query_matrix.shape[-1]
    steps = query_matrix.shape[0]
    logit_scores = jnp.einsum(
        "trgd,urd->trgu", query_matrix, keyval[..., :width], preferred_element_type=jnp.float32
    ) * width ** (-0.5)
    usable = (jnp.arange(steps)[:, None] >= jnp.arange(steps)[None, :])[:, None, None, :]
    masked = jnp.where(usable, logit_scores, NEGATIVE)
    row_peak = jnp.max(masked, axis=-1)
    weight = jnp.where(usable, jnp.exp(masked - row_peak[..., None]), 0.0).astype(jnp.bfloat16)
    total = jnp.sum(weight.astype(jnp.float32), axis=-1)
    acc = jnp.einsum(
        "trgu,urd->trgd", weight, keyval[..., width:], preferred_element_type=jnp.float32
    )
    return row_peak, total, acc


def pack(peak, total, acc):
    rows = acc.shape[0]
    rest = jnp.zeros((rows, 126), jnp.float32)
    return jnp.concatenate([acc, peak[:, None], total[:, None], rest], axis=1)


def merge(packed, step_packed):
    parts = jnp.concatenate([packed, step_packed[None]], axis=0)
    acc, peak, total = parts[..., :128], parts[..., 128:129], parts[..., 129:130]
    factor = jnp.exp(peak - jnp.max(peak, axis=0, keepdims=True))
    return (jnp.sum(factor * acc, axis=0) / jnp.sum(factor * total, axis=0)).astype(jnp.bfloat16)


def gather_weight(mine, x_at, core, first):
    rows, columns = mine.shape[1:]
    lower = lax.ppermute(mine, "x", UP)
    upper = lax.ppermute(mine, "x", DOWN)
    lower, upper, *_ = lax.optimization_barrier((lower, upper) + first)
    across = jnp.concatenate(
        [lax.ppermute(lower[:4], "x", UP), lax.ppermute(upper[4:], "x", DOWN)], axis=0
    )
    whole = jnp.zeros((2, 4, 4, 2, rows, columns), mine.dtype)
    for piece, offset in ((mine, 0), (lower, 3), (upper, 1), (across, 2)):
        at = (x_at + offset) % 4
        other = lax.ppermute(piece, "c", SWAP)
        whole = lax.dynamic_update_slice(
            whole, piece.reshape(2, 1, 4, 1, rows, columns), (0, at, 0, core, 0, 0)
        )
        whole = lax.dynamic_update_slice(
            whole, other.reshape(2, 1, 4, 1, rows, columns), (0, at, 0, 1 - core, 0, 0)
        )
    return whole.reshape(2, 32 * rows, columns)


def pack_log(peak, total, acc):
    lse = peak + jnp.log(total)
    high = lax.reduce_precision(lse, 8, 7)
    mid = lax.reduce_precision(lse - high, 8, 7)
    terms = jnp.stack([high, mid, lse - high - mid])
    terms = jnp.pad(terms, ((0, 0), (0, 96)))
    return jnp.concatenate([acc / total[:, None], terms], axis=0).astype(jnp.bfloat16)


def on_device(
    prompt,
    kv_weight,
    norm_gain,
    kv_cache,
    block_table,
    context_len,
    dest_shard,
    new_query,
    new_keyval,
    out_weight,
):
    x_at, y_at, core = lax.axis_index("x"), lax.axis_index("y"), lax.axis_index("c")
    high = lax.axis_index("zh")
    shard = lax.axis_index(SEQ)
    request = shard // 4
    block_len = kv_cache.shape[1]
    width = new_query.shape[3]
    steps, requests, group = new_query.shape[:3]
    cached, own_blocks = block_table.shape
    half = prompt.shape[0] // 2

    lower = lax.ppermute(prompt, "y", UP)
    upper = lax.ppermute(prompt, "y", DOWN)
    lower_half, upper_half = lower[:half], upper[half:]
    across = [lax.ppermute(lower_half, "y", UP), lax.ppermute(upper_half, "y", DOWN)]

    gain = lax.dynamic_slice_in_dim(norm_gain, shard * kv_weight.shape[0], kv_weight.shape[0])
    scaled = kv_weight.astype(jnp.float32) * gain.astype(jnp.float32)[:, None]
    first = spread(scaled.astype(jnp.bfloat16), RING, 8)
    whole = gather_weight(first, x_at, core, (lower_half, upper_half))

    step_peak, step_total, step_acc = step_stats(new_query, new_keyval[:, :, 0])
    cached_blocks = jnp.take(kv_cache[:, :, 0], block_table, axis=0, mode="clip")
    position = ((shard * own_blocks + jnp.arange(own_blocks, dtype=jnp.int32)) * block_len)[
        :, None
    ] + jnp.arange(block_len, dtype=jnp.int32)[None, :]
    usable = position[None, :, :] < context_len[:, None, None]
    peak, total, acc = paged_stats(new_query[:, :cached], cached_blocks, usable[None, :, None])
    packed = pack(peak.reshape(96), total.reshape(96), acc.reshape(96, width))
    packed, *_ = lax.optimization_barrier((packed, lower_half, upper_half))
    old_packed = lax.all_to_all(packed.reshape(32, 3, 256), SEQ, 0, 0, tiled=True)
    old_step = pack(
        step_peak[:, :cached].reshape(96),
        step_total[:, :cached].reshape(96),
        step_acc[:, :cached].reshape(96, width),
    )
    old_step = lax.dynamic_slice_in_dim(old_step, shard * 3, 3, axis=0)

    def project(rows):
        factor = row_factor(rows)
        return jnp.stack(
            [
                (jnp.dot(rows, whole[h], preferred_element_type=jnp.float32) * factor).astype(
                    jnp.bfloat16
                )
                for h in range(2)
            ]
        )

    whole, old_packed = lax.optimization_barrier((whole, old_packed))
    early = jnp.stack([project(prompt), project(lower), project(upper)], axis=1)
    given = lax.dynamic_index_in_dim(early, 1 - high, 0, keepdims=False)
    early_got = lax.ppermute(given, "zh", SWAP)
    across, _ = lax.optimization_barrier((across, given))
    late = project(jnp.concatenate(across, axis=0))
    given = lax.dynamic_index_in_dim(late, 1 - high, 0, keepdims=False)
    late_got = lax.ppermute(given, "zh", SWAP)
    early_kept = lax.dynamic_index_in_dim(early, high, 0, keepdims=False)
    late_kept = lax.dynamic_index_in_dim(late, high, 0, keepdims=False)
    blocks = jnp.concatenate([early_kept, late_kept[None], early_got, late_got[None]], axis=0)

    query = lax.dynamic_index_in_dim(new_query, cached + request, 1, keepdims=False)
    query = query.reshape(steps * group, width)
    rows = blocks.reshape(-1, 2 * width)
    scores = lax.dot_general(
        query, rows[:, :width], (((1,), (1,)), ((), ())), preferred_element_type=jnp.float32
    ) * width ** (-0.5)
    peak = jnp.max(scores, axis=-1)
    weight = jnp.exp(scores - peak[:, None]).astype(jnp.bfloat16)
    total = jnp.sum(weight.astype(jnp.float32), axis=-1)
    acc = jnp.dot(weight, rows[:, width:], preferred_element_type=jnp.float32)
    old = merge(old_packed, old_step)
    packed = spread(jnp.concatenate([pack_log(peak, total, acc), old, jnp.zeros((10, width), jnp.bfloat16)], axis=0), SEQ, 32)

    targets = lax.dynamic_index_in_dim(dest_shard.reshape(32, 4, 2), shard, 0, keepdims=False)
    order = (y_at + jnp.array([0, 3, 1, 2], jnp.int32)) % 4
    mine = jnp.take(targets, order, axis=0, mode="clip").T
    mine = jnp.where(high == 0, mine, mine[::-1]).reshape(8)
    selector = (mine[None, :] == jnp.arange(32, dtype=jnp.int32)[:, None]).astype(jnp.bfloat16)
    outgoing = jnp.dot(selector, blocks.reshape(8, -1), preferred_element_type=jnp.float32)
    outgoing = outgoing.astype(jnp.bfloat16).reshape(32, block_len, 2 * width)
    outgoing, packed = lax.optimization_barrier((outgoing, packed))
    landed = lax.all_to_all(outgoing, SEQ, 0, 0, tiled=True)[:, :, None, :]

    old = packed[:, 35:38].reshape(steps, cached, group, width)
    packed = packed.astype(jnp.float32).reshape(8, 4, 48, width)
    lse = packed[:, :, 32, :32] + packed[:, :, 33, :32] + packed[:, :, 34, :32]
    acc = packed[:, :, :32]
    step_peak = step_peak[:, cached:].transpose(1, 0, 2).reshape(8, 32)
    step_total = step_total[:, cached:].transpose(1, 0, 2).reshape(8, 32)
    step_acc = step_acc[:, cached:].transpose(1, 0, 2, 3).reshape(8, 32, width)
    top = jnp.maximum(jnp.max(lse, axis=1), step_peak)
    factor = jnp.exp(lse - top[:, None])
    step_factor = jnp.exp(step_peak - top)
    total = jnp.sum(factor, axis=1) + step_factor * step_total
    acc = jnp.sum(factor[..., None] * acc, axis=1) + step_factor[..., None] * step_acc
    new = (acc / total[..., None]).astype(jnp.bfloat16).reshape(8, steps, group, width)

    attended = jnp.concatenate([old, new.transpose(1, 0, 2, 3)], axis=1)
    flat_rows = attended.reshape(steps * requests, group * width)
    partial = jnp.dot(flat_rows, out_weight, preferred_element_type=jnp.float32).astype(jnp.bfloat16)
    summed = sum(part.astype(jnp.float32) for part in collect(partial, TP, 8))
    decoded = summed.astype(jnp.bfloat16).reshape(steps, requests, -1)
    return landed, decoded


def solution(mesh):
    fine = Mesh(mesh.devices.reshape(SIZES), NAMES)
    placed = (
        P(SEQ + TP, None),
        P(SEQ, TP),
        P(),
        P(SEQ, None, TP, None),
        P(None, SEQ),
        P(),
        P(),
        P(None, None, TP, None),
        P(None, None, TP, None),
        P(TP, SEQ),
    )
    return jax.shard_map(
        on_device,
        mesh=fine,
        in_specs=placed,
        out_specs=(P(SEQ, None, TP, None), P(None, None, SEQ)),
        check_vma=False,
    )
```

```python
import jax
import jax.numpy as jnp
from jax import lax
from jax.experimental import pallas as pl
from jax.experimental.pallas import tpu as pltpu
from jax.sharding import Mesh, PartitionSpec as P

EPSILON = 1e-05
NEGATIVE = -1e30
SIZES = (4, 2, 2, 2, 4, 2)
NAMES = ("x", "zp", "zq", "c", "y", "zh")
SEQ = ("x", "zp", "zq", "c")
TP = ("y", "zh")
RING = ("zh", "zp", "zq")
UP = [(i, (i + 1) % 4) for i in range(4)]
DOWN = [(i, (i - 1) % 4) for i in range(4)]
SWAP = [(0, 1), (1, 0)]


def spread(values, axes, count):
    copies = jnp.broadcast_to(values[None], (count,) + values.shape)
    return lax.all_to_all(copies, axes, 0, 0, tiled=True)


def collect(values, axes, count):
    others = [
        lax.ppermute(values, axes, [(i, i ^ bits) for i in range(count)])
        for bits in range(1, count)
    ]
    return [values] + others


def paged_stats(query_matrix, keyval, usable):
    width = query_matrix.shape[-1]
    logit_scores = jnp.einsum(
        "trgd,rpbd->trgpb", query_matrix, keyval[..., :width], preferred_element_type=jnp.float32
    ) * width ** (-0.5)
    masked = jnp.where(usable, logit_scores, NEGATIVE)
    row_peak = jnp.max(masked, axis=(-1, -2))
    weight = jnp.where(usable, jnp.exp(masked - row_peak[..., None, None]), 0.0).astype(jnp.bfloat16)
    total = jnp.sum(weight.astype(jnp.float32), axis=(-1, -2))
    acc = jnp.einsum(
        "trgpb,rpbd->trgd", weight, keyval[..., width:], preferred_element_type=jnp.float32
    )
    return row_peak, total, acc


def step_stats(query_matrix, keyval):
    width = query_matrix.shape[-1]
    steps = query_matrix.shape[0]
    logit_scores = jnp.einsum(
        "trgd,urd->trgu", query_matrix, keyval[..., :width], preferred_element_type=jnp.float32
    ) * width ** (-0.5)
    usable = (jnp.arange(steps)[:, None] >= jnp.arange(steps)[None, :])[:, None, None, :]
    masked = jnp.where(usable, logit_scores, NEGATIVE)
    row_peak = jnp.max(masked, axis=-1)
    weight = jnp.where(usable, jnp.exp(masked - row_peak[..., None]), 0.0).astype(jnp.bfloat16)
    total = jnp.sum(weight.astype(jnp.float32), axis=-1)
    acc = jnp.einsum(
        "trgu,urd->trgd", weight, keyval[..., width:], preferred_element_type=jnp.float32
    )
    return row_peak, total, acc


def pack(peak, total, acc):
    rows = acc.shape[0]
    rest = jnp.zeros((rows, 126), jnp.float32)
    return jnp.concatenate([acc, peak[:, None], total[:, None], rest], axis=1)


def merge(packed, step_packed):
    parts = jnp.concatenate([packed, step_packed[None]], axis=0)
    acc, peak, total = parts[..., :128], parts[..., 128:129], parts[..., 129:130]
    factor = jnp.exp(peak - jnp.max(peak, axis=0, keepdims=True))
    return (jnp.sum(factor * acc, axis=0) / jnp.sum(factor * total, axis=0)).astype(jnp.bfloat16)


def gather_weight(mine, first):
    lower = lax.ppermute(mine, "x", UP)
    upper = lax.ppermute(mine, "x", DOWN)
    lower, upper, *_ = lax.optimization_barrier((lower, upper) + first)
    across = jnp.concatenate(
        [lax.ppermute(lower[:4], "x", UP), lax.ppermute(upper[4:], "x", DOWN)], axis=0
    )
    near = jnp.concatenate([mine, lower, upper], axis=0)
    return [near, lax.ppermute(near, "c", SWAP), across, lax.ppermute(across, "c", SWAP)]


def project_kernel(at, *refs):
    rows_in, weights_in, query = refs[:5], refs[5:9], refs[9]
    kept, given, kept_stats, given_stats = refs[10:14]
    rows, weights, acc, squares, sems = refs[14:]
    copies, start = [], 0
    for k, ref in enumerate(rows_in):
        copies.append(
            pltpu.make_async_copy(ref, rows.at[pl.ds(start, ref.shape[0])], sems.at[8 + k])
        )
        start += ref.shape[0]

    def piece(p):
        source = weights_in[(0, 0, 0, 1, 1, 1, 2, 3)[p]]
        offset = (0, 8, 16, 0, 8, 16, 0, 0)[p]
        return pltpu.make_async_copy(
            source.at[pl.ds(offset, 8)], weights.at[pl.ds(8 * p, 8)], sems.at[p]
        )

    piece(0).start()
    for copy in copies:
        copy.start()
    for p in range(1, 8):
        piece(p).start()
    acc[...] = jnp.zeros_like(acc)
    squares[...] = jnp.zeros_like(squares)
    for copy in copies:
        copy.wait()
    high = at[8]
    for p in range(8):
        piece(p).wait()
        base = at[p]
        columns = [
            rows[:, pl.ds(pl.multiple_of(base + 512 * zl, 256), 256)] for zl in range(4)
        ]
        total = squares[...]
        for column in columns:
            wide = column.astype(jnp.float32)
            wide = wide * wide
            total += wide[:, :128] + wide[:, 128:]
        squares[...] = total
        joined = jnp.concatenate(columns, axis=1)
        for j in range(2):
            at_head = 8 * p + 4 * (high if j == 0 else 1 - high)
            tile = weights[pl.ds(at_head, 4)].reshape(1024, 256)
            acc[j] += jnp.dot(joined, tile, preferred_element_type=jnp.float32)
    mean = jnp.sum(squares[...], axis=-1, keepdims=True) / rows.shape[1]
    factor = lax.rsqrt(mean + EPSILON)
    for j, (out, stats) in enumerate(((kept, kept_stats), (given, given_stats))):
        keyval = (acc[j] * factor).astype(jnp.bfloat16)
        out[...] = keyval
        scores = lax.dot_general(
            query[j],
            keyval[:, :128],
            (((1,), (1,)), ((), ())),
            preferred_element_type=jnp.float32,
        ) * 128 ** (-0.5)
        peak = jnp.max(scores, axis=-1, keepdims=True)
        weight = jnp.exp(scores - peak).astype(jnp.bfloat16)
        total = jnp.sum(weight.astype(jnp.float32), axis=-1, keepdims=True)
        value = jnp.dot(weight, keyval[:, 128:], preferred_element_type=jnp.float32)
        stats[:, :128] = value / total
        stats[:, 128:] = jnp.broadcast_to(peak + jnp.log(total), (32, 128))


def project(at, rows, weights, query):
    count = sum(part.shape[0] for part in rows)
    anywhere = pl.BlockSpec(memory_space=pl.ANY)
    inside = pl.BlockSpec(memory_space=pltpu.VMEM)
    keyval = jax.ShapeDtypeStruct((count, 256), jnp.bfloat16)
    stats = jax.ShapeDtypeStruct((32, 256), jnp.float32)
    return pl.pallas_call(
        project_kernel,
        out_shape=(keyval, keyval, stats, stats),
        in_specs=[pl.BlockSpec(memory_space=pltpu.SMEM)] + [anywhere] * 9 + [inside],
        out_specs=(inside,) * 4,
        scratch_shapes=[
            pltpu.VMEM((count, 8192), jnp.bfloat16),
            pltpu.VMEM((64, 256, 256), jnp.bfloat16),
            pltpu.VMEM((2, count, 256), jnp.float32),
            pltpu.VMEM((count, 128), jnp.float32),
            pltpu.SemaphoreType.DMA((13,)),
        ],
        compiler_params=pltpu.CompilerParams(vmem_limit_bytes=32 * 1024 * 1024),
        cost_estimate=pl.CostEstimate(
            flops=2 * count * 8192 * 512, bytes_accessed=17 * 1024 * 1024, transcendentals=0
        ),
    )(at, *rows, *weights, query)


def pack_log(mine, other):
    top = jnp.maximum(mine[:, 128], other[:, 128])
    mine_factor, other_factor = jnp.exp(mine[:, 128] - top), jnp.exp(other[:, 128] - top)
    both = mine_factor + other_factor
    lse = top + jnp.log(both)
    acc = mine_factor[:, None] * mine[:, :128] + other_factor[:, None] * other[:, :128]
    high = lax.reduce_precision(lse, 8, 7)
    mid = lax.reduce_precision(lse - high, 8, 7)
    terms = jnp.stack([high, mid, lse - high - mid])
    terms = jnp.pad(terms, ((0, 0), (0, 96)))
    return jnp.concatenate([acc / both[:, None], terms], axis=0).astype(jnp.bfloat16)


def on_device(
    prompt,
    kv_weight,
    norm_gain,
    kv_cache,
    block_table,
    context_len,
    dest_shard,
    new_query,
    new_keyval,
    out_weight,
):
    x_at, y_at, core = lax.axis_index("x"), lax.axis_index("y"), lax.axis_index("c")
    high = lax.axis_index("zh")
    shard = lax.axis_index(SEQ)
    request = shard // 4
    block_len = kv_cache.shape[1]
    width = new_query.shape[3]
    steps, requests, group = new_query.shape[:3]
    cached, own_blocks = block_table.shape
    half = prompt.shape[0] // 2

    lower = lax.ppermute(prompt, "y", UP)
    upper = lax.ppermute(prompt, "y", DOWN)
    lower_half, upper_half = lower[:half], upper[half:]
    across = [lax.ppermute(lower_half, "y", UP), lax.ppermute(upper_half, "y", DOWN)]

    gain = lax.dynamic_slice_in_dim(norm_gain, shard * kv_weight.shape[0], kv_weight.shape[0])
    scaled = kv_weight.astype(jnp.float32) * gain.astype(jnp.float32)[:, None]
    first = spread(scaled.astype(jnp.bfloat16), RING, 8)
    weights = gather_weight(first, (lower_half, upper_half))

    step_peak, step_total, step_acc = step_stats(new_query, new_keyval[:, :, 0])
    cached_blocks = jnp.take(kv_cache[:, :, 0], block_table, axis=0, mode="clip")
    position = ((shard * own_blocks + jnp.arange(own_blocks, dtype=jnp.int32)) * block_len)[
        :, None
    ] + jnp.arange(block_len, dtype=jnp.int32)[None, :]
    usable = position[None, :, :] < context_len[:, None, None]
    peak, total, acc = paged_stats(new_query[:, :cached], cached_blocks, usable[None, :, None])
    packed = pack(peak.reshape(96), total.reshape(96), acc.reshape(96, width))
    packed, *_ = lax.optimization_barrier((packed, lower_half, upper_half))
    old_packed = lax.all_to_all(packed.reshape(32, 3, 256), SEQ, 0, 0, tiled=True)
    old_step = pack(
        step_peak[:, :cached].reshape(96),
        step_total[:, :cached].reshape(96),
        step_acc[:, :cached].reshape(96, width),
    )
    old_step = lax.dynamic_slice_in_dim(old_step, shard * 3, 3, axis=0)

    query = lax.dynamic_index_in_dim(new_query, cached + request, 1, keepdims=False)
    query = query.reshape(steps * group, width)
    query = jnp.stack([query, lax.ppermute(query, "zh", SWAP)])
    x_of = (x_at + jnp.array([0, 3, 1, 0, 3, 1, 2, 2], jnp.int32)) % 4
    core_of = core ^ jnp.array([0, 0, 0, 1, 1, 1, 0, 1], jnp.int32)
    at = jnp.concatenate([x_of * 2048 + core_of * 256, high[None]]).astype(jnp.int32)
    across, old_packed = lax.optimization_barrier((across, old_packed))
    kept, given, kept_stats, given_stats = project(
        at, [prompt, lower, upper] + across, weights, query
    )
    got_stats = lax.ppermute(given_stats, "zh", SWAP)
    given, _ = lax.optimization_barrier((given, given_stats))
    got = lax.ppermute(given, "zh", SWAP)
    old = merge(old_packed, old_step)
    packed = jnp.concatenate(
        [pack_log(kept_stats, got_stats), old, jnp.zeros((10, width), jnp.bfloat16)], axis=0
    )
    packed = spread(packed, SEQ, 32)
    blocks = jnp.concatenate([kept, got], axis=0).reshape(8, -1)

    targets = lax.dynamic_index_in_dim(dest_shard.reshape(32, 4, 2), shard, 0, keepdims=False)
    order = (y_at + jnp.array([0, 3, 1, 2], jnp.int32)) % 4
    mine = jnp.take(targets, order, axis=0, mode="clip").T
    mine = jnp.where(high == 0, mine, mine[::-1]).reshape(8)
    selector = (mine[None, :] == jnp.arange(32, dtype=jnp.int32)[:, None]).astype(jnp.bfloat16)
    outgoing = jnp.dot(selector, blocks, preferred_element_type=jnp.float32)
    outgoing = outgoing.astype(jnp.bfloat16).reshape(32, block_len, 2 * width)
    outgoing, packed = lax.optimization_barrier((outgoing, packed))
    landed = lax.all_to_all(outgoing, SEQ, 0, 0, tiled=True)[:, :, None, :]

    old = packed[:, 35:38].reshape(steps, cached, group, width)
    packed = packed.astype(jnp.float32).reshape(8, 4, 48, width)
    lse = packed[:, :, 32, :32] + packed[:, :, 33, :32] + packed[:, :, 34, :32]
    acc = packed[:, :, :32]
    step_peak = step_peak[:, cached:].transpose(1, 0, 2).reshape(8, 32)
    step_total = step_total[:, cached:].transpose(1, 0, 2).reshape(8, 32)
    step_acc = step_acc[:, cached:].transpose(1, 0, 2, 3).reshape(8, 32, width)
    top = jnp.maximum(jnp.max(lse, axis=1), step_peak)
    factor = jnp.exp(lse - top[:, None])
    step_factor = jnp.exp(step_peak - top)
    total = jnp.sum(factor, axis=1) + step_factor * step_total
    acc = jnp.sum(factor[..., None] * acc, axis=1) + step_factor[..., None] * step_acc
    new = (acc / total[..., None]).astype(jnp.bfloat16).reshape(8, steps, group, width)

    attended = jnp.concatenate([old, new.transpose(1, 0, 2, 3)], axis=1)
    flat_rows = attended.reshape(steps * requests, group * width)
    partial = jnp.dot(flat_rows, out_weight, preferred_element_type=jnp.float32).astype(jnp.bfloat16)
    summed = sum(part.astype(jnp.float32) for part in collect(partial, "y", 4))
    summed = summed + lax.ppermute(summed, "zh", SWAP)
    decoded = summed.astype(jnp.bfloat16).reshape(steps, requests, -1)
    return landed, decoded


def solution(mesh):
    fine = Mesh(mesh.devices.reshape(SIZES), NAMES)
    placed = (
        P(SEQ + TP, None),
        P(SEQ, TP),
        P(),
        P(SEQ, None, TP, None),
        P(None, SEQ),
        P(),
        P(),
        P(None, None, TP, None),
        P(None, None, TP, None),
        P(TP, SEQ),
    )
    return jax.shard_map(
        on_device,
        mesh=fine,
        in_specs=placed,
        out_specs=(P(SEQ, None, TP, None), P(None, None, SEQ)),
        check_vma=False,
    )
```

```python
import jax
import jax.numpy as jnp
from jax import lax
from jax.experimental import pallas as pl
from jax.experimental.pallas import tpu as pltpu
from jax.sharding import Mesh, PartitionSpec as P

EPSILON = 1e-05
NEGATIVE = -1e30
SIZES = (4, 2, 2, 2, 4, 2)
NAMES = ("x", "zp", "zq", "c", "y", "zh")
SEQ = ("x", "zp", "zq", "c")
TP = ("y", "zh")
RING = ("zh", "zp", "zq")
UP = [(i, (i + 1) % 4) for i in range(4)]
DOWN = [(i, (i - 1) % 4) for i in range(4)]
SWAP = [(0, 1), (1, 0)]


def spread(values, axes, count):
    copies = jnp.broadcast_to(values[None], (count,) + values.shape)
    return lax.all_to_all(copies, axes, 0, 0, tiled=True)


def collect(values, axes, count):
    others = [
        lax.ppermute(values, axes, [(i, i ^ bits) for i in range(count)])
        for bits in range(1, count)
    ]
    return [values] + others


def paged_stats(query_matrix, keyval, usable):
    width = query_matrix.shape[-1]
    logit_scores = jnp.einsum(
        "trgd,rpbd->trgpb", query_matrix, keyval[..., :width], preferred_element_type=jnp.float32
    ) * width ** (-0.5)
    masked = jnp.where(usable, logit_scores, NEGATIVE)
    row_peak = jnp.max(masked, axis=(-1, -2))
    weight = jnp.where(usable, jnp.exp(masked - row_peak[..., None, None]), 0.0).astype(jnp.bfloat16)
    total = jnp.sum(weight.astype(jnp.float32), axis=(-1, -2))
    acc = jnp.einsum(
        "trgpb,rpbd->trgd", weight, keyval[..., width:], preferred_element_type=jnp.float32
    )
    return row_peak, total, acc


def step_stats(query_matrix, keyval):
    width = query_matrix.shape[-1]
    steps = query_matrix.shape[0]
    logit_scores = jnp.einsum(
        "trgd,urd->trgu", query_matrix, keyval[..., :width], preferred_element_type=jnp.float32
    ) * width ** (-0.5)
    usable = (jnp.arange(steps)[:, None] >= jnp.arange(steps)[None, :])[:, None, None, :]
    masked = jnp.where(usable, logit_scores, NEGATIVE)
    row_peak = jnp.max(masked, axis=-1)
    weight = jnp.where(usable, jnp.exp(masked - row_peak[..., None]), 0.0).astype(jnp.bfloat16)
    total = jnp.sum(weight.astype(jnp.float32), axis=-1)
    acc = jnp.einsum(
        "trgu,urd->trgd", weight, keyval[..., width:], preferred_element_type=jnp.float32
    )
    return row_peak, total, acc


def pack(peak, total, acc):
    rows = acc.shape[0]
    rest = jnp.zeros((rows, 126), jnp.float32)
    return jnp.concatenate([acc, peak[:, None], total[:, None], rest], axis=1)


def merge(packed, step_packed):
    parts = jnp.concatenate([packed, step_packed[None]], axis=0)
    acc, peak, total = parts[..., :128], parts[..., 128:129], parts[..., 129:130]
    factor = jnp.exp(peak - jnp.max(peak, axis=0, keepdims=True))
    return (jnp.sum(factor * acc, axis=0) / jnp.sum(factor * total, axis=0)).astype(jnp.bfloat16)


def gather_weight(mine, packed):
    lower = lax.ppermute(mine, "x", UP)
    upper = lax.ppermute(mine, "x", DOWN)
    lower_half, upper_half = lower[:4], upper[4:]
    lower_half, upper_half, lower, upper, packed = lax.optimization_barrier(
        (lower_half, upper_half, lower, upper, packed)
    )
    pieces = [
        mine,
        lower,
        upper,
        lax.ppermute(lower_half, "x", UP),
        lax.ppermute(upper_half, "x", DOWN),
    ]
    return pieces + [lax.ppermute(piece, "c", SWAP) for piece in pieces], packed


def project_kernel(at, *refs):
    rows_in, weights_in, query = refs[0], refs[1:11], refs[11]
    kept, given, kept_stats = refs[12:15]
    rows, weights, acc, squares, sems = refs[15:]
    count = rows.shape[0]
    rows_copy = pltpu.make_async_copy(rows_in, rows, sems.at[10])

    order = (0, 1, 2, 5, 6, 7, 3, 4, 8, 9)
    place = (0, 8, 16, 24, 32, 40, 48, 52, 56, 60)
    copies = [
        pltpu.make_async_copy(
            weights_in[k], weights.at[pl.ds(start, weights_in[k].shape[0])], sems.at[n]
        )
        for n, (k, start) in enumerate(zip(order, place))
    ]
    copies[0].start()
    rows_copy.start()
    for copy in copies[1:]:
        copy.start()
    acc[...] = jnp.zeros_like(acc)
    squares[...] = jnp.zeros_like(squares)
    rows_copy.wait()
    high = at[8]
    for p in range(8):
        for copy in copies[p : p + 1] if p < 6 else copies[2 * p - 6 : 2 * p - 4]:
            copy.wait()
        base = at[p]
        columns = [
            rows[:, pl.ds(pl.multiple_of(base + 512 * zl, 256), 256)] for zl in range(4)
        ]
        total = squares[...]
        for column in columns:
            wide = column.astype(jnp.float32)
            wide = wide * wide
            total += wide[:, :128] + wide[:, 128:]
        squares[...] = total
        joined = jnp.concatenate(columns, axis=1)
        for j in range(2):
            at_head = 8 * p + 4 * (high if j == 0 else 1 - high)
            tile = weights[pl.ds(at_head, 4)].reshape(1024, 256)
            acc[j] += jnp.dot(joined, tile, preferred_element_type=jnp.float32)
    mean = jnp.sum(squares[...], axis=-1, keepdims=True) / rows.shape[1]
    factor = lax.rsqrt(mean + EPSILON)
    lane = lax.broadcasted_iota(jnp.int32, (32, 128), 1)
    for j, out in enumerate((kept, given)):
        keyval = (acc[j] * factor).astype(jnp.bfloat16)
        out[:count] = keyval
        scores = lax.dot_general(
            query[j],
            keyval[:, :128],
            (((1,), (1,)), ((), ())),
            preferred_element_type=jnp.float32,
        ) * 128 ** (-0.5)
        peak = jnp.max(scores, axis=-1, keepdims=True)
        weight = jnp.exp(scores - peak).astype(jnp.bfloat16)
        total = jnp.sum(weight.astype(jnp.float32), axis=-1, keepdims=True)
        value = jnp.dot(weight, keyval[:, 128:], preferred_element_type=jnp.float32)
        lse = jnp.broadcast_to(peak + jnp.log(total), (32, 128))
        if j == 0:
            kept_stats[:, :128] = value / total
            kept_stats[:, 128:] = lse
        else:
            first = lse.astype(jnp.bfloat16).astype(jnp.float32)
            second = (lse - first).astype(jnp.bfloat16).astype(jnp.float32)
            third = lse - first - second
            terms = jnp.where(lane == 0, first, jnp.where(lane == 1, second, third))
            packed = jnp.concatenate([value / total, terms], axis=1)
            given[count:] = packed.astype(jnp.bfloat16)


def project(at, rows, weights, query):
    count = rows.shape[0]
    anywhere = pl.BlockSpec(memory_space=pl.ANY)
    inside = pl.BlockSpec(memory_space=pltpu.VMEM)
    return pl.pallas_call(
        project_kernel,
        out_shape=(
            jax.ShapeDtypeStruct((count, 256), jnp.bfloat16),
            jax.ShapeDtypeStruct((count + 32, 256), jnp.bfloat16),
            jax.ShapeDtypeStruct((32, 256), jnp.float32),
        ),
        in_specs=[pl.BlockSpec(memory_space=pltpu.SMEM)] + [anywhere] * 11 + [inside],
        out_specs=(inside,) * 3,
        scratch_shapes=[
            pltpu.VMEM((count, 8192), jnp.bfloat16),
            pltpu.VMEM((64, 256, 256), jnp.bfloat16),
            pltpu.VMEM((2, count, 256), jnp.float32),
            pltpu.VMEM((count, 128), jnp.float32),
            pltpu.SemaphoreType.DMA((11,)),
        ],
        compiler_params=pltpu.CompilerParams(vmem_limit_bytes=32 * 1024 * 1024),
        cost_estimate=pl.CostEstimate(
            flops=2 * count * 8192 * 512, bytes_accessed=17 * 1024 * 1024, transcendentals=0
        ),
    )(at, rows, *weights, query)


def pack_log(mine, other, other_lse):
    mine_lse = mine[:, 128]
    top = jnp.maximum(mine_lse, other_lse)
    mine_factor, other_factor = jnp.exp(mine_lse - top), jnp.exp(other_lse - top)
    both = mine_factor + other_factor
    lse = top + jnp.log(both)
    acc = mine_factor[:, None] * mine[:, :128] + other_factor[:, None] * other[:, :128]
    high = lax.reduce_precision(lse, 8, 7)
    mid = lax.reduce_precision(lse - high, 8, 7)
    terms = jnp.stack([high, mid, lse - high - mid])
    terms = jnp.pad(terms, ((0, 0), (0, 96)))
    return jnp.concatenate([acc / both[:, None], terms], axis=0).astype(jnp.bfloat16)


def on_device(
    prompt,
    kv_weight,
    norm_gain,
    kv_cache,
    block_table,
    context_len,
    dest_shard,
    new_query,
    new_keyval,
    out_weight,
):
    x_at, core = lax.axis_index("x"), lax.axis_index("c")
    high = lax.axis_index("zh")
    shard = lax.axis_index(SEQ)
    request = shard // 4
    block_len = kv_cache.shape[1]
    width = new_query.shape[3]
    steps, requests, group = new_query.shape[:3]
    cached, own_blocks = block_table.shape

    rows = lax.all_gather(prompt, "y", axis=0, tiled=True)
    query = lax.dynamic_index_in_dim(new_query, cached + request, 1, keepdims=False)
    query = query.reshape(steps * group, width)
    query = jnp.stack([query, lax.ppermute(query, "zh", SWAP)])

    gain = lax.dynamic_slice_in_dim(norm_gain, shard * kv_weight.shape[0], kv_weight.shape[0])
    scaled = kv_weight.astype(jnp.float32) * gain.astype(jnp.float32)[:, None]
    first = spread(scaled.astype(jnp.bfloat16), RING, 8)

    step_peak, step_total, step_acc = step_stats(new_query, new_keyval[:, :, 0])
    cached_blocks = jnp.take(kv_cache[:, :, 0], block_table, axis=0, mode="clip")
    position = ((shard * own_blocks + jnp.arange(own_blocks, dtype=jnp.int32)) * block_len)[
        :, None
    ] + jnp.arange(block_len, dtype=jnp.int32)[None, :]
    usable = position[None, :, :] < context_len[:, None, None]
    peak, total, acc = paged_stats(new_query[:, :cached], cached_blocks, usable[None, :, None])
    packed = pack(peak.reshape(96), total.reshape(96), acc.reshape(96, width))
    first, packed, query = lax.optimization_barrier((first, packed, query))
    weights, packed = gather_weight(first, packed)
    old_packed = lax.all_to_all(packed.reshape(32, 3, 256), SEQ, 0, 0, tiled=True)
    old_step = pack(
        step_peak[:, :cached].reshape(96),
        step_total[:, :cached].reshape(96),
        step_acc[:, :cached].reshape(96, width),
    )
    old_step = lax.dynamic_slice_in_dim(old_step, shard * 3, 3, axis=0)

    x_of = (x_at + jnp.array([0, 3, 1, 0, 3, 1, 2, 2], jnp.int32)) % 4
    core_of = core ^ jnp.array([0, 0, 0, 1, 1, 1, 0, 1], jnp.int32)
    at = jnp.concatenate([x_of * 2048 + core_of * 256, high[None]]).astype(jnp.int32)
    rows, old_packed = lax.optimization_barrier((rows, old_packed))
    kept, given, kept_stats = project(at, rows, weights, query)
    got = lax.ppermute(given, "zh", SWAP)
    got_stats = got[-32:].astype(jnp.float32)
    got_lse = jnp.sum(got_stats[:, width : width + 3], axis=1)
    old = merge(old_packed, old_step)
    packed = jnp.concatenate(
        [pack_log(kept_stats, got_stats, got_lse), old, jnp.zeros((10, width), jnp.bfloat16)], axis=0
    )
    packed = spread(packed, SEQ, 32)
    blocks = jnp.concatenate([kept, got[:-32]], axis=0).reshape(8, -1)

    targets = lax.dynamic_index_in_dim(dest_shard.reshape(32, 4, 2), shard, 0, keepdims=False)
    mine = targets.T
    mine = jnp.where(high == 0, mine, mine[::-1]).reshape(8)
    selector = (mine[None, :] == jnp.arange(32, dtype=jnp.int32)[:, None]).astype(jnp.bfloat16)
    outgoing = jnp.dot(selector, blocks, preferred_element_type=jnp.float32)
    outgoing = outgoing.astype(jnp.bfloat16).reshape(32, block_len, 2 * width)
    outgoing, packed = lax.optimization_barrier((outgoing, packed))
    landed = lax.all_to_all(outgoing, SEQ, 0, 0, tiled=True)[:, :, None, :]

    old = packed[:, 35:38].reshape(steps, cached, group, width)
    packed = packed.astype(jnp.float32).reshape(8, 4, 48, width)
    lse = packed[:, :, 32, :32] + packed[:, :, 33, :32] + packed[:, :, 34, :32]
    acc = packed[:, :, :32]
    step_peak = step_peak[:, cached:].transpose(1, 0, 2).reshape(8, 32)
    step_total = step_total[:, cached:].transpose(1, 0, 2).reshape(8, 32)
    step_acc = step_acc[:, cached:].transpose(1, 0, 2, 3).reshape(8, 32, width)
    top = jnp.maximum(jnp.max(lse, axis=1), step_peak)
    factor = jnp.exp(lse - top[:, None])
    step_factor = jnp.exp(step_peak - top)
    total = jnp.sum(factor, axis=1) + step_factor * step_total
    acc = jnp.sum(factor[..., None] * acc, axis=1) + step_factor[..., None] * step_acc
    new = (acc / total[..., None]).astype(jnp.bfloat16).reshape(8, steps, group, width)

    attended = jnp.concatenate([old, new.transpose(1, 0, 2, 3)], axis=1)
    flat_rows = attended.reshape(steps * requests, group * width)
    partial = jnp.dot(flat_rows, out_weight, preferred_element_type=jnp.float32).astype(jnp.bfloat16)
    summed = sum(part.astype(jnp.float32) for part in collect(partial, "y", 4))
    summed = summed + lax.ppermute(summed, "zh", SWAP)
    decoded = summed.astype(jnp.bfloat16).reshape(steps, requests, -1)
    return landed, decoded


def solution(mesh):
    fine = Mesh(mesh.devices.reshape(SIZES), NAMES)
    placed = (
        P(SEQ + TP, None),
        P(SEQ, TP),
        P(),
        P(SEQ, None, TP, None),
        P(None, SEQ),
        P(),
        P(),
        P(None, None, TP, None),
        P(None, None, TP, None),
        P(TP, SEQ),
    )
    return jax.shard_map(
        on_device,
        mesh=fine,
        in_specs=placed,
        out_specs=(P(SEQ, None, TP, None), P(None, None, SEQ)),
        check_vma=False,
    )
```

```python
import jax
import jax.numpy as jnp
from jax import lax
from jax.experimental import pallas as pl
from jax.experimental.pallas import tpu as pltpu
from jax.sharding import Mesh, PartitionSpec as P

EPSILON = 1e-05
NEGATIVE = -1e30
SIZES = (4, 2, 2, 2, 4, 2)
NAMES = ("x", "zp", "zq", "c", "y", "zh")
SEQ = ("x", "zp", "zq", "c")
TP = ("y", "zh")
RING = ("zh", "zp", "zq")
UP = [(i, (i + 1) % 4) for i in range(4)]
DOWN = [(i, (i - 1) % 4) for i in range(4)]
OVER = [(i, (i + 2) % 4) for i in range(4)]
SWAP = [(0, 1), (1, 0)]


def spread(values, axes, count):
    copies = jnp.broadcast_to(values[None], (count,) + values.shape)
    return lax.all_to_all(copies, axes, 0, 0, tiled=True)


def collect(values, axes, count):
    others = [
        lax.ppermute(values, axes, [(i, i ^ bits) for i in range(count)])
        for bits in range(1, count)
    ]
    return [values] + others


def paged_stats(query_matrix, keyval, usable):
    width = query_matrix.shape[-1]
    logit_scores = jnp.einsum(
        "trgd,rpbd->trgpb", query_matrix, keyval[..., :width], preferred_element_type=jnp.float32
    ) * width ** (-0.5)
    masked = jnp.where(usable, logit_scores, NEGATIVE)
    row_peak = jnp.max(masked, axis=(-1, -2))
    weight = jnp.where(usable, jnp.exp(masked - row_peak[..., None, None]), 0.0).astype(jnp.bfloat16)
    total = jnp.sum(weight.astype(jnp.float32), axis=(-1, -2))
    acc = jnp.einsum(
        "trgpb,rpbd->trgd", weight, keyval[..., width:], preferred_element_type=jnp.float32
    )
    return row_peak, total, acc


def step_stats(query_matrix, keyval):
    width = query_matrix.shape[-1]
    steps = query_matrix.shape[0]
    logit_scores = jnp.einsum(
        "trgd,urd->trgu", query_matrix, keyval[..., :width], preferred_element_type=jnp.float32
    ) * width ** (-0.5)
    usable = (jnp.arange(steps)[:, None] >= jnp.arange(steps)[None, :])[:, None, None, :]
    masked = jnp.where(usable, logit_scores, NEGATIVE)
    row_peak = jnp.max(masked, axis=-1)
    weight = jnp.where(usable, jnp.exp(masked - row_peak[..., None]), 0.0).astype(jnp.bfloat16)
    total = jnp.sum(weight.astype(jnp.float32), axis=-1)
    acc = jnp.einsum(
        "trgu,urd->trgd", weight, keyval[..., width:], preferred_element_type=jnp.float32
    )
    return row_peak, total, acc


def pack(peak, total, acc):
    rows = acc.shape[0]
    rest = jnp.zeros((rows, 126), jnp.float32)
    return jnp.concatenate([acc, peak[:, None], total[:, None], rest], axis=1)


def merge(packed, step_packed):
    parts = jnp.concatenate([packed, step_packed[None]], axis=0)
    acc, peak, total = parts[..., :128], parts[..., 128:129], parts[..., 129:130]
    factor = jnp.exp(peak - jnp.max(peak, axis=0, keepdims=True))
    return (jnp.sum(factor * acc, axis=0) / jnp.sum(factor * total, axis=0)).astype(jnp.bfloat16)


def gather_weight(mine):
    pieces = [mine, lax.ppermute(mine, "x", UP), lax.ppermute(mine, "x", DOWN)]
    return pieces + [lax.ppermute(mine, "x", OVER)]


def project_kernel(at, *refs):
    rows_in, weights_in, query = refs[:5], refs[5:13], refs[13]
    kept, given, kept_stats = refs[14:17]
    rows, weights, acc, squares, sems = refs[17:]
    count = rows.shape[0]
    order = (0, 1, 2, 4, 5, 6, 3, 7)
    copies = [
        pltpu.make_async_copy(weights_in[k], weights.at[pl.ds(8 * n, 8)], sems.at[n])
        for n, k in enumerate(order)
    ]
    row_copies, start = [], 0
    for n, ref in enumerate(rows_in):
        row_copies.append(
            pltpu.make_async_copy(ref, rows.at[pl.ds(start, ref.shape[0])], sems.at[8 + n])
        )
        start += ref.shape[0]
    copies[0].start()
    for copy in row_copies + copies[1:]:
        copy.start()
    acc[...] = jnp.zeros_like(acc)
    squares[...] = jnp.zeros_like(squares)
    for copy in row_copies:
        copy.wait()
    high = at[8]
    for p in range(8):
        copies[p].wait()
        base = at[p]
        columns = [
            rows[:, pl.ds(pl.multiple_of(base + 512 * zl, 256), 256)] for zl in range(4)
        ]
        total = squares[...]
        for column in columns:
            wide = column.astype(jnp.float32)
            wide = wide * wide
            total += wide[:, :128] + wide[:, 128:]
        squares[...] = total
        joined = jnp.concatenate(columns, axis=1)
        for j in range(2):
            at_head = 8 * p + 4 * (high if j == 0 else 1 - high)
            tile = weights[pl.ds(at_head, 4)].reshape(1024, 256)
            acc[j] += jnp.dot(joined, tile, preferred_element_type=jnp.float32)
    mean = jnp.sum(squares[...], axis=-1, keepdims=True) / rows.shape[1]
    factor = lax.rsqrt(mean + EPSILON)
    lane = lax.broadcasted_iota(jnp.int32, (32, 128), 1)
    for j, out in enumerate((kept, given)):
        keyval = (acc[j] * factor).astype(jnp.bfloat16)
        out[:count] = keyval
        scores = lax.dot_general(
            query[j],
            keyval[:, :128],
            (((1,), (1,)), ((), ())),
            preferred_element_type=jnp.float32,
        ) * 128 ** (-0.5)
        peak = jnp.max(scores, axis=-1, keepdims=True)
        weight = jnp.exp(scores - peak).astype(jnp.bfloat16)
        total = jnp.sum(weight.astype(jnp.float32), axis=-1, keepdims=True)
        value = jnp.dot(weight, keyval[:, 128:], preferred_element_type=jnp.float32)
        lse = jnp.broadcast_to(peak + jnp.log(total), (32, 128))
        if j == 0:
            kept_stats[:, :128] = value / total
            kept_stats[:, 128:] = lse
        else:
            first = lse.astype(jnp.bfloat16).astype(jnp.float32)
            second = (lse - first).astype(jnp.bfloat16).astype(jnp.float32)
            third = lse - first - second
            terms = jnp.where(lane == 0, first, jnp.where(lane == 1, second, third))
            packed = jnp.concatenate([value / total, terms], axis=1)
            given[count:] = packed.astype(jnp.bfloat16)


def project(at, rows, weights, query):
    count = sum(part.shape[0] for part in rows)
    anywhere = pl.BlockSpec(memory_space=pl.ANY)
    inside = pl.BlockSpec(memory_space=pltpu.VMEM)
    return pl.pallas_call(
        project_kernel,
        out_shape=(
            jax.ShapeDtypeStruct((count, 256), jnp.bfloat16),
            jax.ShapeDtypeStruct((count + 32, 256), jnp.bfloat16),
            jax.ShapeDtypeStruct((32, 256), jnp.float32),
        ),
        in_specs=[pl.BlockSpec(memory_space=pltpu.SMEM)] + [anywhere] * 13 + [inside],
        out_specs=(inside,) * 3,
        scratch_shapes=[
            pltpu.VMEM((count, 8192), jnp.bfloat16),
            pltpu.VMEM((64, 256, 256), jnp.bfloat16),
            pltpu.VMEM((2, count, 256), jnp.float32),
            pltpu.VMEM((count, 128), jnp.float32),
            pltpu.SemaphoreType.DMA((13,)),
        ],
        compiler_params=pltpu.CompilerParams(vmem_limit_bytes=32 * 1024 * 1024),
        cost_estimate=pl.CostEstimate(
            flops=2 * count * 8192 * 512, bytes_accessed=17 * 1024 * 1024, transcendentals=0
        ),
    )(at, *rows, *weights, query)


def pack_log(mine, other, other_lse):
    mine_lse = mine[:, 128]
    top = jnp.maximum(mine_lse, other_lse)
    mine_factor, other_factor = jnp.exp(mine_lse - top), jnp.exp(other_lse - top)
    both = mine_factor + other_factor
    lse = top + jnp.log(both)
    acc = mine_factor[:, None] * mine[:, :128] + other_factor[:, None] * other[:, :128]
    high = lax.reduce_precision(lse, 8, 7)
    mid = lax.reduce_precision(lse - high, 8, 7)
    terms = jnp.stack([high, mid, lse - high - mid])
    terms = jnp.pad(terms, ((0, 0), (0, 96)))
    return jnp.concatenate([acc / both[:, None], terms], axis=0).astype(jnp.bfloat16)


def on_device(
    prompt,
    kv_weight,
    norm_gain,
    kv_cache,
    block_table,
    context_len,
    dest_shard,
    new_query,
    new_keyval,
    out_weight,
):
    x_at, y_at, core = lax.axis_index("x"), lax.axis_index("y"), lax.axis_index("c")
    high = lax.axis_index("zh")
    shard = lax.axis_index(SEQ)
    request = shard // 4
    block_len = kv_cache.shape[1]
    width = new_query.shape[3]
    steps, requests, group = new_query.shape[:3]
    cached, own_blocks = block_table.shape

    half = prompt.shape[0] // 2
    lower = lax.ppermute(prompt, "y", UP)
    upper = lax.ppermute(prompt, "y", DOWN)
    lower_half, upper_half = lower[:half], upper[half:]
    query = lax.dynamic_index_in_dim(new_query, cached + request, 1, keepdims=False)
    query = query.reshape(steps * group, width)
    query = jnp.stack([query, lax.ppermute(query, "zh", SWAP)])

    gain = lax.dynamic_slice_in_dim(norm_gain, shard * kv_weight.shape[0], kv_weight.shape[0])
    scaled = kv_weight.astype(jnp.float32) * gain.astype(jnp.float32)[:, None]
    first = spread(scaled.astype(jnp.bfloat16), RING, 8)

    step_peak, step_total, step_acc = step_stats(new_query, new_keyval[:, :, 0])
    cached_blocks = jnp.take(kv_cache[:, :, 0], block_table, axis=0, mode="clip")
    position = ((shard * own_blocks + jnp.arange(own_blocks, dtype=jnp.int32)) * block_len)[
        :, None
    ] + jnp.arange(block_len, dtype=jnp.int32)[None, :]
    usable = position[None, :, :] < context_len[:, None, None]
    peak, total, acc = paged_stats(new_query[:, :cached], cached_blocks, usable[None, :, None])
    packed = pack(peak.reshape(96), total.reshape(96), acc.reshape(96, width))
    first, packed, query = lax.optimization_barrier((first, packed, query))
    weights = gather_weight(first)
    lower_half, upper_half, packed = lax.optimization_barrier((lower_half, upper_half, packed))
    across = [lax.ppermute(lower_half, "y", UP), lax.ppermute(upper_half, "y", DOWN)]
    old_packed = lax.all_to_all(packed.reshape(32, 3, 256), SEQ, 0, 0, tiled=True)
    weights, across, old_packed = lax.optimization_barrier((weights, across, old_packed))
    weights = weights + [lax.ppermute(piece, "c", SWAP) for piece in weights]
    old_step = pack(
        step_peak[:, :cached].reshape(96),
        step_total[:, :cached].reshape(96),
        step_acc[:, :cached].reshape(96, width),
    )
    old_step = lax.dynamic_slice_in_dim(old_step, shard * 3, 3, axis=0)

    x_of = (x_at + jnp.array([0, 3, 1, 0, 3, 1, 2, 2], jnp.int32)) % 4
    core_of = core ^ jnp.array([0, 0, 0, 1, 1, 1, 0, 1], jnp.int32)
    at = jnp.concatenate([x_of * 2048 + core_of * 256, high[None]]).astype(jnp.int32)
    kept, given, kept_stats = project(at, [prompt, lower, upper] + across, weights, query)
    got = lax.ppermute(given, "zh", SWAP)
    got_stats = got[-32:].astype(jnp.float32)
    got_lse = jnp.sum(got_stats[:, width : width + 3], axis=1)
    old = merge(old_packed, old_step)
    packed = jnp.concatenate(
        [pack_log(kept_stats, got_stats, got_lse), old, jnp.zeros((10, width), jnp.bfloat16)], axis=0
    )
    packed = spread(packed, SEQ, 32)
    blocks = jnp.concatenate([kept, got[:-32]], axis=0).reshape(8, -1)

    targets = lax.dynamic_index_in_dim(dest_shard.reshape(32, 4, 2), shard, 0, keepdims=False)
    order = (y_at + jnp.array([0, 3, 1, 2], jnp.int32)) % 4
    mine = jnp.take(targets, order, axis=0, mode="clip").T
    mine = jnp.where(high == 0, mine, mine[::-1]).reshape(8)
    selector = (mine[None, :] == jnp.arange(32, dtype=jnp.int32)[:, None]).astype(jnp.bfloat16)
    outgoing = jnp.dot(selector, blocks, preferred_element_type=jnp.float32)
    outgoing = outgoing.astype(jnp.bfloat16).reshape(32, block_len, 2 * width)
    outgoing, packed = lax.optimization_barrier((outgoing, packed))
    landed = lax.all_to_all(outgoing, SEQ, 0, 0, tiled=True)[:, :, None, :]

    old = packed[:, 35:38].reshape(steps, cached, group, width)
    packed = packed.astype(jnp.float32).reshape(8, 4, 48, width)
    lse = packed[:, :, 32, :32] + packed[:, :, 33, :32] + packed[:, :, 34, :32]
    acc = packed[:, :, :32]
    step_peak = step_peak[:, cached:].transpose(1, 0, 2).reshape(8, 32)
    step_total = step_total[:, cached:].transpose(1, 0, 2).reshape(8, 32)
    step_acc = step_acc[:, cached:].transpose(1, 0, 2, 3).reshape(8, 32, width)
    top = jnp.maximum(jnp.max(lse, axis=1), step_peak)
    factor = jnp.exp(lse - top[:, None])
    step_factor = jnp.exp(step_peak - top)
    total = jnp.sum(factor, axis=1) + step_factor * step_total
    acc = jnp.sum(factor[..., None] * acc, axis=1) + step_factor[..., None] * step_acc
    new = (acc / total[..., None]).astype(jnp.bfloat16).reshape(8, steps, group, width)

    attended = jnp.concatenate([old, new.transpose(1, 0, 2, 3)], axis=1)
    flat_rows = attended.reshape(steps * requests, group * width)
    partial = jnp.dot(flat_rows, out_weight, preferred_element_type=jnp.float32).astype(jnp.bfloat16)
    summed = sum(part.astype(jnp.float32) for part in collect(partial, "y", 4))
    summed = summed + lax.ppermute(summed, "zh", SWAP)
    decoded = summed.astype(jnp.bfloat16).reshape(steps, requests, -1)
    return landed, decoded


def solution(mesh):
    fine = Mesh(mesh.devices.reshape(SIZES), NAMES)
    placed = (
        P(SEQ + TP, None),
        P(SEQ, TP),
        P(),
        P(SEQ, None, TP, None),
        P(None, SEQ),
        P(),
        P(),
        P(None, None, TP, None),
        P(None, None, TP, None),
        P(TP, SEQ),
    )
    return jax.shard_map(
        on_device,
        mesh=fine,
        in_specs=placed,
        out_specs=(P(SEQ, None, TP, None), P(None, None, SEQ)),
        check_vma=False,
    )
```

```python
import jax
import jax.numpy as jnp
from jax import lax
from jax.experimental import pallas as pl
from jax.experimental.pallas import tpu as pltpu
from jax.sharding import Mesh, PartitionSpec as P

EPSILON = 1e-05
NEGATIVE = -1e30
SIZES = (4, 2, 2, 2, 4, 2)
NAMES = ("x", "zp", "zq", "c", "y", "zh")
SEQ = ("x", "zp", "zq", "c")
TP = ("y", "zh")
RING = ("zh", "zp", "zq")
UP = [(i, (i + 1) % 4) for i in range(4)]
DOWN = [(i, (i - 1) % 4) for i in range(4)]
OVER = [(i, (i + 2) % 4) for i in range(4)]
SWAP = [(0, 1), (1, 0)]


def spread(values, axes, count):
    copies = jnp.broadcast_to(values[None], (count,) + values.shape)
    return lax.all_to_all(copies, axes, 0, 0, tiled=True)


def collect(values, axes, count):
    others = [
        lax.ppermute(values, axes, [(i, i ^ bits) for i in range(count)])
        for bits in range(1, count)
    ]
    return [values] + others


def paged_stats(query_matrix, keyval, usable):
    width = query_matrix.shape[-1]
    logit_scores = jnp.einsum(
        "trgd,rpbd->trgpb", query_matrix, keyval[..., :width], preferred_element_type=jnp.float32
    ) * width ** (-0.5)
    masked = jnp.where(usable, logit_scores, NEGATIVE)
    row_peak = jnp.max(masked, axis=(-1, -2))
    weight = jnp.where(usable, jnp.exp(masked - row_peak[..., None, None]), 0.0).astype(jnp.bfloat16)
    total = jnp.sum(weight.astype(jnp.float32), axis=(-1, -2))
    acc = jnp.einsum(
        "trgpb,rpbd->trgd", weight, keyval[..., width:], preferred_element_type=jnp.float32
    )
    return row_peak, total, acc


def step_stats(query_matrix, keyval):
    width = query_matrix.shape[-1]
    steps = query_matrix.shape[0]
    logit_scores = jnp.einsum(
        "trgd,urd->trgu", query_matrix, keyval[..., :width], preferred_element_type=jnp.float32
    ) * width ** (-0.5)
    usable = (jnp.arange(steps)[:, None] >= jnp.arange(steps)[None, :])[:, None, None, :]
    masked = jnp.where(usable, logit_scores, NEGATIVE)
    row_peak = jnp.max(masked, axis=-1)
    weight = jnp.where(usable, jnp.exp(masked - row_peak[..., None]), 0.0).astype(jnp.bfloat16)
    total = jnp.sum(weight.astype(jnp.float32), axis=-1)
    acc = jnp.einsum(
        "trgu,urd->trgd", weight, keyval[..., width:], preferred_element_type=jnp.float32
    )
    return row_peak, total, acc


def pack(peak, total, acc):
    rows = acc.shape[0]
    rest = jnp.zeros((rows, 126), jnp.float32)
    return jnp.concatenate([acc, peak[:, None], total[:, None], rest], axis=1)


def merge(packed, step_packed):
    parts = jnp.concatenate([packed, step_packed[None]], axis=0)
    acc, peak, total = parts[..., :128], parts[..., 128:129], parts[..., 129:130]
    factor = jnp.exp(peak - jnp.max(peak, axis=0, keepdims=True))
    return (jnp.sum(factor * acc, axis=0) / jnp.sum(factor * total, axis=0)).astype(jnp.bfloat16)


def gather_weight(mine):
    pieces = [mine, lax.ppermute(mine, "x", UP), lax.ppermute(mine, "x", DOWN)]
    return pieces + [lax.ppermute(mine, "x", OVER)]


def project_kernel(at, *refs):
    rows_in, weights_in, query = refs[:5], refs[5:13], refs[13]
    out, stats = refs[14:16]
    rows, weights, acc, squares, sems = refs[16:]
    count = rows.shape[0]
    head = at[8]
    order = (0, 1, 2, 4, 5, 6, 3, 7)
    copies = [
        pltpu.make_async_copy(
            weights_in[k].at[pl.ds(4 * head, 4)], weights.at[pl.ds(4 * n, 4)], sems.at[n]
        )
        for n, k in enumerate(order)
    ]
    row_copies, start = [], 0
    for n, ref in enumerate(rows_in):
        row_copies.append(
            pltpu.make_async_copy(ref, rows.at[pl.ds(start, ref.shape[0])], sems.at[8 + n])
        )
        start += ref.shape[0]
    copies[0].start()
    for copy in row_copies + copies[1:]:
        copy.start()
    acc[...] = jnp.zeros_like(acc)
    squares[...] = jnp.zeros_like(squares)
    for copy in row_copies:
        copy.wait()
    for p in range(8):
        copies[p].wait()
        base = at[p]
        columns = [
            rows[:, pl.ds(pl.multiple_of(base + 512 * zl, 256), 256)] for zl in range(4)
        ]
        total = squares[...]
        for column in columns:
            wide = column.astype(jnp.float32)
            wide = wide * wide
            total += wide[:, :128] + wide[:, 128:]
        squares[...] = total
        joined = jnp.concatenate(columns, axis=1)
        tile = weights[4 * p : 4 * p + 4].reshape(1024, 256)
        acc[...] += jnp.dot(joined, tile, preferred_element_type=jnp.float32)
    mean = jnp.sum(squares[...], axis=-1, keepdims=True) / rows.shape[1]
    keyval = (acc[...] * lax.rsqrt(mean + EPSILON)).astype(jnp.bfloat16)
    out[:count] = keyval
    scores = lax.dot_general(
        query[...], keyval[:, :128], (((1,), (1,)), ((), ())), preferred_element_type=jnp.float32
    ) * 128 ** (-0.5)
    peak = jnp.max(scores, axis=-1, keepdims=True)
    weight = jnp.exp(scores - peak).astype(jnp.bfloat16)
    total = jnp.sum(weight.astype(jnp.float32), axis=-1, keepdims=True)
    value = jnp.dot(weight, keyval[:, 128:], preferred_element_type=jnp.float32) / total
    lse = jnp.broadcast_to(peak + jnp.log(total), (32, 128))
    stats[:, :128] = value
    stats[:, 128:] = lse
    first = lse.astype(jnp.bfloat16).astype(jnp.float32)
    second = (lse - first).astype(jnp.bfloat16).astype(jnp.float32)
    third = lse - first - second
    lane = lax.broadcasted_iota(jnp.int32, (32, 128), 1)
    terms = jnp.where(lane == 0, first, jnp.where(lane == 1, second, third))
    out[count:] = jnp.concatenate([value, terms], axis=1).astype(jnp.bfloat16)


def project(at, rows, weights, query):
    count = sum(part.shape[0] for part in rows)
    anywhere = pl.BlockSpec(memory_space=pl.ANY)
    inside = pl.BlockSpec(memory_space=pltpu.VMEM)
    return pl.pallas_call(
        project_kernel,
        out_shape=(
            jax.ShapeDtypeStruct((count + 32, 256), jnp.bfloat16),
            jax.ShapeDtypeStruct((32, 256), jnp.float32),
        ),
        in_specs=[pl.BlockSpec(memory_space=pltpu.SMEM)] + [anywhere] * 13 + [inside],
        out_specs=(inside,) * 2,
        scratch_shapes=[
            pltpu.VMEM((count, 8192), jnp.bfloat16),
            pltpu.VMEM((32, 256, 256), jnp.bfloat16),
            pltpu.VMEM((count, 256), jnp.float32),
            pltpu.VMEM((count, 128), jnp.float32),
            pltpu.SemaphoreType.DMA((13,)),
        ],
        compiler_params=pltpu.CompilerParams(vmem_limit_bytes=28 * 1024 * 1024),
        cost_estimate=pl.CostEstimate(
            flops=2 * count * 8192 * 256, bytes_accessed=13 * 1024 * 1024, transcendentals=0
        ),
    )(at, *rows, *weights, query)


def pack_log(mine, other, other_lse):
    mine_lse = mine[:, 128]
    top = jnp.maximum(mine_lse, other_lse)
    mine_factor, other_factor = jnp.exp(mine_lse - top), jnp.exp(other_lse - top)
    both = mine_factor + other_factor
    lse = top + jnp.log(both)
    acc = mine_factor[:, None] * mine[:, :128] + other_factor[:, None] * other[:, :128]
    high = lax.reduce_precision(lse, 8, 7)
    mid = lax.reduce_precision(lse - high, 8, 7)
    terms = jnp.stack([high, mid, lse - high - mid])
    terms = jnp.pad(terms, ((0, 0), (0, 96)))
    return jnp.concatenate([acc / both[:, None], terms], axis=0).astype(jnp.bfloat16)


def on_device(
    prompt,
    kv_weight,
    norm_gain,
    kv_cache,
    block_table,
    context_len,
    dest_shard,
    new_query,
    new_keyval,
    out_weight,
):
    x_at, y_at, core = lax.axis_index("x"), lax.axis_index("y"), lax.axis_index("c")
    high = lax.axis_index("zh")
    shard = lax.axis_index(SEQ)
    request = shard // 4
    block_len = kv_cache.shape[1]
    width = new_query.shape[3]
    steps, requests, group = new_query.shape[:3]
    cached, own_blocks = block_table.shape

    half = prompt.shape[0] // 2
    lower = lax.ppermute(prompt, "y", UP)
    upper = lax.ppermute(prompt, "y", DOWN)
    lower_half, upper_half = lower[:half], upper[half:]
    query = lax.dynamic_index_in_dim(new_query, cached + request, 1, keepdims=False)
    query = query.reshape(steps * group, width)

    gain = lax.dynamic_slice_in_dim(norm_gain, shard * kv_weight.shape[0], kv_weight.shape[0])
    scaled = kv_weight.astype(jnp.float32) * gain.astype(jnp.float32)[:, None]
    first = spread(scaled.astype(jnp.bfloat16), RING, 8)

    step_peak, step_total, step_acc = step_stats(new_query, new_keyval[:, :, 0])
    cached_blocks = jnp.take(kv_cache[:, :, 0], block_table, axis=0, mode="clip")
    position = ((shard * own_blocks + jnp.arange(own_blocks, dtype=jnp.int32)) * block_len)[
        :, None
    ] + jnp.arange(block_len, dtype=jnp.int32)[None, :]
    usable = position[None, :, :] < context_len[:, None, None]
    peak, total, acc = paged_stats(new_query[:, :cached], cached_blocks, usable[None, :, None])
    packed = pack(peak.reshape(96), total.reshape(96), acc.reshape(96, width))
    first, packed = lax.optimization_barrier((first, packed))
    weights = gather_weight(first)
    lower_half, upper_half, packed = lax.optimization_barrier((lower_half, upper_half, packed))
    across = [lax.ppermute(lower_half, "y", UP), lax.ppermute(upper_half, "y", DOWN)]
    old_packed = lax.all_to_all(packed.reshape(32, 3, 256), SEQ, 0, 0, tiled=True)
    weights, across, old_packed, query = lax.optimization_barrier(
        (weights, across, old_packed, query)
    )
    query_other = lax.ppermute(query, "zh", SWAP)
    weights = weights + [lax.ppermute(piece, "c", SWAP) for piece in weights]
    old_step = pack(
        step_peak[:, :cached].reshape(96),
        step_total[:, :cached].reshape(96),
        step_acc[:, :cached].reshape(96, width),
    )
    old_step = lax.dynamic_slice_in_dim(old_step, shard * 3, 3, axis=0)

    x_of = (x_at + jnp.array([0, 3, 1, 0, 3, 1, 2, 2], jnp.int32)) % 4
    core_of = core ^ jnp.array([0, 0, 0, 1, 1, 1, 0, 1], jnp.int32)
    at = x_of * 2048 + core_of * 256
    rows = [prompt, lower, upper] + across
    at_other = jnp.concatenate([at, 1 - high[None]]).astype(jnp.int32)
    given, _ = project(at_other, rows, weights, query_other)
    got = lax.ppermute(given, "zh", SWAP)
    at, _ = lax.optimization_barrier((at, given))
    at = jnp.concatenate([at, high[None]]).astype(jnp.int32)
    kept, kept_stats = project(at, rows, weights, query)
    got_stats = got[-32:].astype(jnp.float32)
    got_lse = jnp.sum(got_stats[:, width : width + 3], axis=1)
    old = merge(old_packed, old_step)
    packed = jnp.concatenate(
        [pack_log(kept_stats, got_stats, got_lse), old, jnp.zeros((10, width), jnp.bfloat16)], axis=0
    )
    packed = spread(packed, SEQ, 32)
    blocks = jnp.concatenate([kept[:-32], got[:-32]], axis=0).reshape(8, -1)

    targets = lax.dynamic_index_in_dim(dest_shard.reshape(32, 4, 2), shard, 0, keepdims=False)
    order = (y_at + jnp.array([0, 3, 1, 2], jnp.int32)) % 4
    mine = jnp.take(targets, order, axis=0, mode="clip").T
    mine = jnp.where(high == 0, mine, mine[::-1]).reshape(8)
    selector = (mine[None, :] == jnp.arange(32, dtype=jnp.int32)[:, None]).astype(jnp.bfloat16)
    outgoing = jnp.dot(selector, blocks, preferred_element_type=jnp.float32)
    outgoing = outgoing.astype(jnp.bfloat16).reshape(32, block_len, 2 * width)
    outgoing, packed = lax.optimization_barrier((outgoing, packed))
    landed = lax.all_to_all(outgoing, SEQ, 0, 0, tiled=True)[:, :, None, :]

    old = packed[:, 35:38].reshape(steps, cached, group, width)
    packed = packed.astype(jnp.float32).reshape(8, 4, 48, width)
    lse = packed[:, :, 32, :32] + packed[:, :, 33, :32] + packed[:, :, 34, :32]
    acc = packed[:, :, :32]
    step_peak = step_peak[:, cached:].transpose(1, 0, 2).reshape(8, 32)
    step_total = step_total[:, cached:].transpose(1, 0, 2).reshape(8, 32)
    step_acc = step_acc[:, cached:].transpose(1, 0, 2, 3).reshape(8, 32, width)
    top = jnp.maximum(jnp.max(lse, axis=1), step_peak)
    factor = jnp.exp(lse - top[:, None])
    step_factor = jnp.exp(step_peak - top)
    total = jnp.sum(factor, axis=1) + step_factor * step_total
    acc = jnp.sum(factor[..., None] * acc, axis=1) + step_factor[..., None] * step_acc
    new = (acc / total[..., None]).astype(jnp.bfloat16).reshape(8, steps, group, width)

    attended = jnp.concatenate([old, new.transpose(1, 0, 2, 3)], axis=1)
    flat_rows = attended.reshape(steps * requests, group * width)
    partial = jnp.dot(flat_rows, out_weight, preferred_element_type=jnp.float32).astype(jnp.bfloat16)
    summed = sum(part.astype(jnp.float32) for part in collect(partial, "y", 4))
    summed = summed + lax.ppermute(summed, "zh", SWAP)
    decoded = summed.astype(jnp.bfloat16).reshape(steps, requests, -1)
    return landed, decoded


def solution(mesh):
    fine = Mesh(mesh.devices.reshape(SIZES), NAMES)
    placed = (
        P(SEQ + TP, None),
        P(SEQ, TP),
        P(),
        P(SEQ, None, TP, None),
        P(None, SEQ),
        P(),
        P(),
        P(None, None, TP, None),
        P(None, None, TP, None),
        P(TP, SEQ),
    )
    return jax.shard_map(
        on_device,
        mesh=fine,
        in_specs=placed,
        out_specs=(P(SEQ, None, TP, None), P(None, None, SEQ)),
        check_vma=False,
    )
```

```python
import jax
import jax.numpy as jnp
from jax import lax
from jax.experimental import pallas as pl
from jax.experimental.pallas import tpu as pltpu
from jax.sharding import Mesh, PartitionSpec as P

EPSILON = 1e-05
NEGATIVE = -1e30
SIZES = (4, 2, 2, 2, 4, 2)
NAMES = ("x", "zp", "zq", "c", "y", "zh")
SEQ = ("x", "zp", "zq", "c")
TP = ("y", "zh")
RING = ("zh", "zp", "zq")
UP = [(i, (i + 1) % 4) for i in range(4)]
DOWN = [(i, (i - 1) % 4) for i in range(4)]
SWAP = [(0, 1), (1, 0)]


def spread(values, axes, count):
    copies = jnp.broadcast_to(values[None], (count,) + values.shape)
    return lax.all_to_all(copies, axes, 0, 0, tiled=True)


def collect(values, axes, count):
    others = [
        lax.ppermute(values, axes, [(i, i ^ bits) for i in range(count)])
        for bits in range(1, count)
    ]
    return [values] + others


def paged_stats(query_matrix, keyval, usable):
    width = query_matrix.shape[-1]
    logit_scores = jnp.einsum(
        "trgd,rpbd->trgpb", query_matrix, keyval[..., :width], preferred_element_type=jnp.float32
    ) * width ** (-0.5)
    masked = jnp.where(usable, logit_scores, NEGATIVE)
    row_peak = jnp.max(masked, axis=(-1, -2))
    weight = jnp.where(usable, jnp.exp(masked - row_peak[..., None, None]), 0.0).astype(jnp.bfloat16)
    total = jnp.sum(weight.astype(jnp.float32), axis=(-1, -2))
    acc = jnp.einsum(
        "trgpb,rpbd->trgd", weight, keyval[..., width:], preferred_element_type=jnp.float32
    )
    return row_peak, total, acc


def step_stats(query_matrix, keyval):
    width = query_matrix.shape[-1]
    steps = query_matrix.shape[0]
    logit_scores = jnp.einsum(
        "trgd,urd->trgu", query_matrix, keyval[..., :width], preferred_element_type=jnp.float32
    ) * width ** (-0.5)
    usable = (jnp.arange(steps)[:, None] >= jnp.arange(steps)[None, :])[:, None, None, :]
    masked = jnp.where(usable, logit_scores, NEGATIVE)
    row_peak = jnp.max(masked, axis=-1)
    weight = jnp.where(usable, jnp.exp(masked - row_peak[..., None]), 0.0).astype(jnp.bfloat16)
    total = jnp.sum(weight.astype(jnp.float32), axis=-1)
    acc = jnp.einsum(
        "trgu,urd->trgd", weight, keyval[..., width:], preferred_element_type=jnp.float32
    )
    return row_peak, total, acc


def pack(peak, total, acc):
    rows = acc.shape[0]
    rest = jnp.zeros((rows, 126), jnp.float32)
    return jnp.concatenate([acc, peak[:, None], total[:, None], rest], axis=1)


def merge(packed, step_packed):
    parts = jnp.concatenate([packed, step_packed[None]], axis=0)
    acc, peak, total = parts[..., :128], parts[..., 128:129], parts[..., 129:130]
    factor = jnp.exp(peak - jnp.max(peak, axis=0, keepdims=True))
    return (jnp.sum(factor * acc, axis=0) / jnp.sum(factor * total, axis=0)).astype(jnp.bfloat16)


def project_kernel(at, *refs):
    rows_in, weights_in, query = refs[:5], refs[5:15], refs[15]
    kept, given, kept_stats = refs[16:19]
    rows, weights, acc, squares, sems = refs[19:]
    count = rows.shape[0]
    order = (0, 1, 2, 5, 6, 7, 3, 4, 8, 9)
    place = (0, 8, 16, 24, 32, 40, 48, 52, 56, 60)
    copies = [
        pltpu.make_async_copy(
            weights_in[k], weights.at[pl.ds(start, weights_in[k].shape[0])], sems.at[n]
        )
        for n, (k, start) in enumerate(zip(order, place))
    ]
    row_copies, start = [], 0
    for n, ref in enumerate(rows_in):
        row_copies.append(
            pltpu.make_async_copy(ref, rows.at[pl.ds(start, ref.shape[0])], sems.at[10 + n])
        )
        start += ref.shape[0]
    copies[0].start()
    for copy in row_copies + copies[1:]:
        copy.start()
    acc[...] = jnp.zeros_like(acc)
    squares[...] = jnp.zeros_like(squares)
    for copy in row_copies:
        copy.wait()
    high = at[8]
    for p in range(8):
        for copy in copies[p : p + 1] if p < 6 else copies[2 * p - 6 : 2 * p - 4]:
            copy.wait()
        base = at[p]
        columns = [
            rows[:, pl.ds(pl.multiple_of(base + 512 * zl, 256), 256)] for zl in range(4)
        ]
        total = squares[...]
        for column in columns:
            wide = column.astype(jnp.float32)
            wide = wide * wide
            total += wide[:, :128] + wide[:, 128:]
        squares[...] = total
        joined = jnp.concatenate(columns, axis=1)
        for j in range(2):
            at_head = 8 * p + 4 * (high if j == 0 else 1 - high)
            tile = weights[pl.ds(at_head, 4)].reshape(1024, 256)
            acc[j] += jnp.dot(joined, tile, preferred_element_type=jnp.float32)
    mean = jnp.sum(squares[...], axis=-1, keepdims=True) / rows.shape[1]
    factor = lax.rsqrt(mean + EPSILON)
    lane = lax.broadcasted_iota(jnp.int32, (32, 128), 1)
    for j, out in enumerate((kept, given)):
        keyval = (acc[j] * factor).astype(jnp.bfloat16)
        out[:count] = keyval
        scores = lax.dot_general(
            query[j],
            keyval[:, :128],
            (((1,), (1,)), ((), ())),
            preferred_element_type=jnp.float32,
        ) * 128 ** (-0.5)
        peak = jnp.max(scores, axis=-1, keepdims=True)
        weight = jnp.exp(scores - peak).astype(jnp.bfloat16)
        total = jnp.sum(weight.astype(jnp.float32), axis=-1, keepdims=True)
        value = jnp.dot(weight, keyval[:, 128:], preferred_element_type=jnp.float32)
        lse = jnp.broadcast_to(peak + jnp.log(total), (32, 128))
        if j == 0:
            kept_stats[:, :128] = value / total
            kept_stats[:, 128:] = lse
        else:
            first = lse.astype(jnp.bfloat16).astype(jnp.float32)
            second = (lse - first).astype(jnp.bfloat16).astype(jnp.float32)
            third = lse - first - second
            terms = jnp.where(lane == 0, first, jnp.where(lane == 1, second, third))
            packed = jnp.concatenate([value / total, terms], axis=1)
            given[count:] = packed.astype(jnp.bfloat16)


def project(at, rows, weights, query):
    count = sum(part.shape[0] for part in rows)
    anywhere = pl.BlockSpec(memory_space=pl.ANY)
    inside = pl.BlockSpec(memory_space=pltpu.VMEM)
    return pl.pallas_call(
        project_kernel,
        out_shape=(
            jax.ShapeDtypeStruct((count, 256), jnp.bfloat16),
            jax.ShapeDtypeStruct((count + 32, 256), jnp.bfloat16),
            jax.ShapeDtypeStruct((32, 256), jnp.float32),
        ),
        in_specs=[pl.BlockSpec(memory_space=pltpu.SMEM)] + [anywhere] * 15 + [inside],
        out_specs=(inside,) * 3,
        scratch_shapes=[
            pltpu.VMEM((count, 8192), jnp.bfloat16),
            pltpu.VMEM((64, 256, 256), jnp.bfloat16),
            pltpu.VMEM((2, count, 256), jnp.float32),
            pltpu.VMEM((count, 128), jnp.float32),
            pltpu.SemaphoreType.DMA((15,)),
        ],
        compiler_params=pltpu.CompilerParams(vmem_limit_bytes=32 * 1024 * 1024),
        cost_estimate=pl.CostEstimate(
            flops=2 * count * 8192 * 512, bytes_accessed=17 * 1024 * 1024, transcendentals=0
        ),
    )(at, *rows, *weights, query)


def pack_log(mine, other, other_lse):
    mine_lse = mine[:, 128]
    top = jnp.maximum(mine_lse, other_lse)
    mine_factor, other_factor = jnp.exp(mine_lse - top), jnp.exp(other_lse - top)
    both = mine_factor + other_factor
    lse = top + jnp.log(both)
    acc = mine_factor[:, None] * mine[:, :128] + other_factor[:, None] * other[:, :128]
    high = lax.reduce_precision(lse, 8, 7)
    mid = lax.reduce_precision(lse - high, 8, 7)
    terms = jnp.stack([high, mid, lse - high - mid])
    terms = jnp.pad(terms, ((0, 0), (0, 96)))
    return jnp.concatenate([acc / both[:, None], terms], axis=0).astype(jnp.bfloat16)


def on_device(
    prompt,
    kv_weight,
    norm_gain,
    kv_cache,
    block_table,
    context_len,
    dest_shard,
    new_query,
    new_keyval,
    out_weight,
):
    x_at, y_at, core = lax.axis_index("x"), lax.axis_index("y"), lax.axis_index("c")
    high = lax.axis_index("zh")
    shard = lax.axis_index(SEQ)
    request = shard // 4
    block_len = kv_cache.shape[1]
    width = new_query.shape[3]
    steps, requests, group = new_query.shape[:3]
    cached, own_blocks = block_table.shape

    half = prompt.shape[0] // 2
    lower = lax.ppermute(prompt, "y", UP)
    upper = lax.ppermute(prompt, "y", DOWN)
    lower_half, upper_half = lower[:half], upper[half:]
    query = lax.dynamic_index_in_dim(new_query, cached + request, 1, keepdims=False)
    query = query.reshape(steps * group, width)

    gain = lax.dynamic_slice_in_dim(norm_gain, shard * kv_weight.shape[0], kv_weight.shape[0])
    scaled = kv_weight.astype(jnp.float32) * gain.astype(jnp.float32)[:, None]
    first = spread(scaled.astype(jnp.bfloat16), RING, 8)

    step_peak, step_total, step_acc = step_stats(new_query, new_keyval[:, :, 0])
    cached_blocks = jnp.take(kv_cache[:, :, 0], block_table, axis=0, mode="clip")
    position = ((shard * own_blocks + jnp.arange(own_blocks, dtype=jnp.int32)) * block_len)[
        :, None
    ] + jnp.arange(block_len, dtype=jnp.int32)[None, :]
    usable = position[None, :, :] < context_len[:, None, None]
    peak, total, acc = paged_stats(new_query[:, :cached], cached_blocks, usable[None, :, None])
    packed = pack(peak.reshape(96), total.reshape(96), acc.reshape(96, width))
    first, packed, query = lax.optimization_barrier((first, packed, query))
    query = jnp.stack([query, lax.ppermute(query, "zh", SWAP)])
    x_lower = lax.ppermute(first, "x", UP)
    x_upper = lax.ppermute(first, "x", DOWN)
    lower_half, upper_half, packed = lax.optimization_barrier((lower_half, upper_half, packed))
    across = [lax.ppermute(lower_half, "y", UP), lax.ppermute(upper_half, "y", DOWN)]
    x_lower, x_upper, *_ = lax.optimization_barrier((x_lower, x_upper, lower_half, upper_half))
    far = [lax.ppermute(x_lower[:4], "x", UP), lax.ppermute(x_upper[4:], "x", DOWN)]
    old_packed = lax.all_to_all(packed.reshape(32, 3, 256), SEQ, 0, 0, tiled=True)
    weights, across, old_packed = lax.optimization_barrier(
        ([first, x_lower, x_upper] + far, across, old_packed)
    )
    weights = weights + [lax.ppermute(piece, "c", SWAP) for piece in weights]
    old_step = pack(
        step_peak[:, :cached].reshape(96),
        step_total[:, :cached].reshape(96),
        step_acc[:, :cached].reshape(96, width),
    )
    old_step = lax.dynamic_slice_in_dim(old_step, shard * 3, 3, axis=0)

    x_of = (x_at + jnp.array([0, 3, 1, 0, 3, 1, 2, 2], jnp.int32)) % 4
    core_of = core ^ jnp.array([0, 0, 0, 1, 1, 1, 0, 1], jnp.int32)
    at = jnp.concatenate([x_of * 2048 + core_of * 256, high[None]]).astype(jnp.int32)
    kept, given, kept_stats = project(at, [prompt, lower, upper] + across, weights, query)
    got = lax.ppermute(given, "zh", SWAP)
    got_stats = got[-32:].astype(jnp.float32)
    got_lse = jnp.sum(got_stats[:, width : width + 3], axis=1)
    old = merge(old_packed, old_step)
    packed = jnp.concatenate(
        [pack_log(kept_stats, got_stats, got_lse), old, jnp.zeros((10, width), jnp.bfloat16)], axis=0
    )
    packed = spread(packed, SEQ, 32)
    blocks = jnp.concatenate([kept, got[:-32]], axis=0).reshape(8, -1)

    targets = lax.dynamic_index_in_dim(dest_shard.reshape(32, 4, 2), shard, 0, keepdims=False)
    order = (y_at + jnp.array([0, 3, 1, 2], jnp.int32)) % 4
    mine = jnp.take(targets, order, axis=0, mode="clip").T
    mine = jnp.where(high == 0, mine, mine[::-1]).reshape(8)
    selector = (mine[None, :] == jnp.arange(32, dtype=jnp.int32)[:, None]).astype(jnp.bfloat16)
    outgoing = jnp.dot(selector, blocks, preferred_element_type=jnp.float32)
    outgoing = outgoing.astype(jnp.bfloat16).reshape(32, block_len, 2 * width)
    outgoing, packed = lax.optimization_barrier((outgoing, packed))
    landed = lax.all_to_all(outgoing, SEQ, 0, 0, tiled=True)[:, :, None, :]

    old = packed[:, 35:38].reshape(steps, cached, group, width)
    packed = packed.astype(jnp.float32).reshape(8, 4, 48, width)
    lse = packed[:, :, 32, :32] + packed[:, :, 33, :32] + packed[:, :, 34, :32]
    acc = packed[:, :, :32]
    step_peak = step_peak[:, cached:].transpose(1, 0, 2).reshape(8, 32)
    step_total = step_total[:, cached:].transpose(1, 0, 2).reshape(8, 32)
    step_acc = step_acc[:, cached:].transpose(1, 0, 2, 3).reshape(8, 32, width)
    top = jnp.maximum(jnp.max(lse, axis=1), step_peak)
    factor = jnp.exp(lse - top[:, None])
    step_factor = jnp.exp(step_peak - top)
    total = jnp.sum(factor, axis=1) + step_factor * step_total
    acc = jnp.sum(factor[..., None] * acc, axis=1) + step_factor[..., None] * step_acc
    new = (acc / total[..., None]).astype(jnp.bfloat16).reshape(8, steps, group, width)

    attended = jnp.concatenate([old, new.transpose(1, 0, 2, 3)], axis=1)
    flat_rows = attended.reshape(steps * requests, group * width)
    partial = jnp.dot(flat_rows, out_weight, preferred_element_type=jnp.float32).astype(jnp.bfloat16)
    summed = sum(part.astype(jnp.float32) for part in collect(partial, "y", 4))
    summed = summed + lax.ppermute(summed, "zh", SWAP)
    decoded = summed.astype(jnp.bfloat16).reshape(steps, requests, -1)
    return landed, decoded


def solution(mesh):
    fine = Mesh(mesh.devices.reshape(SIZES), NAMES)
    placed = (
        P(SEQ + TP, None),
        P(SEQ, TP),
        P(),
        P(SEQ, None, TP, None),
        P(None, SEQ),
        P(),
        P(),
        P(None, None, TP, None),
        P(None, None, TP, None),
        P(TP, SEQ),
    )
    return jax.shard_map(
        on_device,
        mesh=fine,
        in_specs=placed,
        out_specs=(P(SEQ, None, TP, None), P(None, None, SEQ)),
        check_vma=False,
    )
```

```python
import jax
import jax.numpy as jnp
from jax import lax
from jax.experimental import pallas as pl
from jax.experimental.pallas import tpu as pltpu
from jax.sharding import Mesh, PartitionSpec as P

EPSILON = 1e-05
NEGATIVE = -1e30
SIZES = (4, 2, 2, 2, 4, 2)
NAMES = ("x", "zp", "zq", "c", "y", "zh")
SEQ = ("x", "zp", "zq", "c")
TP = ("y", "zh")
RING = ("zh", "zp", "zq")
UP = [(i, (i + 1) % 4) for i in range(4)]
DOWN = [(i, (i - 1) % 4) for i in range(4)]
SWAP = [(0, 1), (1, 0)]


def spread(values, axes, count):
    copies = jnp.broadcast_to(values[None], (count,) + values.shape)
    return lax.all_to_all(copies, axes, 0, 0, tiled=True)


def collect(values, axes, count):
    others = [
        lax.ppermute(values, axes, [(i, i ^ bits) for i in range(count)])
        for bits in range(1, count)
    ]
    return [values] + others


def paged_stats(query_matrix, keyval, usable):
    width = query_matrix.shape[-1]
    logit_scores = jnp.einsum(
        "trgd,rpbd->trgpb", query_matrix, keyval[..., :width], preferred_element_type=jnp.float32
    ) * width ** (-0.5)
    masked = jnp.where(usable, logit_scores, NEGATIVE)
    row_peak = jnp.max(masked, axis=(-1, -2))
    weight = jnp.where(usable, jnp.exp(masked - row_peak[..., None, None]), 0.0).astype(jnp.bfloat16)
    total = jnp.sum(weight.astype(jnp.float32), axis=(-1, -2))
    acc = jnp.einsum(
        "trgpb,rpbd->trgd", weight, keyval[..., width:], preferred_element_type=jnp.float32
    )
    return row_peak, total, acc


def step_stats(query_matrix, keyval):
    width = query_matrix.shape[-1]
    steps = query_matrix.shape[0]
    logit_scores = jnp.einsum(
        "trgd,urd->trgu", query_matrix, keyval[..., :width], preferred_element_type=jnp.float32
    ) * width ** (-0.5)
    usable = (jnp.arange(steps)[:, None] >= jnp.arange(steps)[None, :])[:, None, None, :]
    masked = jnp.where(usable, logit_scores, NEGATIVE)
    row_peak = jnp.max(masked, axis=-1)
    weight = jnp.where(usable, jnp.exp(masked - row_peak[..., None]), 0.0).astype(jnp.bfloat16)
    total = jnp.sum(weight.astype(jnp.float32), axis=-1)
    acc = jnp.einsum(
        "trgu,urd->trgd", weight, keyval[..., width:], preferred_element_type=jnp.float32
    )
    return row_peak, total, acc


def pack(peak, total, acc):
    rows = acc.shape[0]
    rest = jnp.zeros((rows, 126), jnp.float32)
    return jnp.concatenate([acc, peak[:, None], total[:, None], rest], axis=1)


def merge(packed, step_packed):
    parts = jnp.concatenate([packed, step_packed[None]], axis=0)
    acc, peak, total = parts[..., :128], parts[..., 128:129], parts[..., 129:130]
    factor = jnp.exp(peak - jnp.max(peak, axis=0, keepdims=True))
    return (jnp.sum(factor * acc, axis=0) / jnp.sum(factor * total, axis=0)).astype(jnp.bfloat16)


def project_kernel(at, *refs):
    rows_in, weights_in, query = refs[:5], refs[5:15], refs[15]
    kept, given, kept_stats = refs[16:19]
    rows, weights, acc, squares, sems = refs[19:]
    count = rows.shape[0]
    order = (0, 1, 2, 5, 6, 7, 3, 4, 8, 9)
    place = (0, 8, 16, 24, 32, 40, 48, 52, 56, 60)
    copies = [
        pltpu.make_async_copy(
            weights_in[k], weights.at[pl.ds(start, weights_in[k].shape[0])], sems.at[n]
        )
        for n, (k, start) in enumerate(zip(order, place))
    ]
    row_copies, start = [], 0
    for n, ref in enumerate(rows_in):
        row_copies.append(
            pltpu.make_async_copy(ref, rows.at[pl.ds(start, ref.shape[0])], sems.at[10 + n])
        )
        start += ref.shape[0]
    copies[0].start()
    for copy in row_copies + copies[1:]:
        copy.start()
    acc[...] = jnp.zeros_like(acc)
    squares[...] = jnp.zeros_like(squares)
    for copy in row_copies:
        copy.wait()
    high = at[8]
    for p in range(8):
        for copy in copies[p : p + 1] if p < 6 else copies[2 * p - 6 : 2 * p - 4]:
            copy.wait()
        base = at[p]
        columns = [
            rows[:, pl.ds(pl.multiple_of(base + 512 * zl, 256), 256)] for zl in range(4)
        ]
        total = squares[...]
        for column in columns:
            wide = column.astype(jnp.float32)
            wide = wide * wide
            total += wide[:, :128] + wide[:, 128:]
        squares[...] = total
        joined = jnp.concatenate(columns, axis=1)
        for j in range(2):
            at_head = 8 * p + 4 * (high if j == 0 else 1 - high)
            tile = weights[pl.ds(at_head, 4)].reshape(1024, 256)
            acc[j] += jnp.dot(joined, tile, preferred_element_type=jnp.float32)
    mean = jnp.sum(squares[...], axis=-1, keepdims=True) / rows.shape[1]
    factor = lax.rsqrt(mean + EPSILON)
    lane = lax.broadcasted_iota(jnp.int32, (32, 128), 1)
    for j, out in enumerate((kept, given)):
        keyval = (acc[j] * factor).astype(jnp.bfloat16)
        out[:count] = keyval
        scores = lax.dot_general(
            query[j],
            keyval[:, :128],
            (((1,), (1,)), ((), ())),
            preferred_element_type=jnp.float32,
        ) * 128 ** (-0.5)
        peak = jnp.max(scores, axis=-1, keepdims=True)
        weight = jnp.exp(scores - peak).astype(jnp.bfloat16)
        total = jnp.sum(weight.astype(jnp.float32), axis=-1, keepdims=True)
        value = jnp.dot(weight, keyval[:, 128:], preferred_element_type=jnp.float32)
        lse = jnp.broadcast_to(peak + jnp.log(total), (32, 128))
        if j == 0:
            kept_stats[:, :128] = value / total
            kept_stats[:, 128:] = lse
        else:
            first = lse.astype(jnp.bfloat16).astype(jnp.float32)
            second = (lse - first).astype(jnp.bfloat16).astype(jnp.float32)
            third = lse - first - second
            terms = jnp.where(lane == 0, first, jnp.where(lane == 1, second, third))
            packed = jnp.concatenate([value / total, terms], axis=1)
            given[count:] = packed.astype(jnp.bfloat16)


def project(at, rows, weights, query):
    count = sum(part.shape[0] for part in rows)
    anywhere = pl.BlockSpec(memory_space=pl.ANY)
    inside = pl.BlockSpec(memory_space=pltpu.VMEM)
    return pl.pallas_call(
        project_kernel,
        out_shape=(
            jax.ShapeDtypeStruct((count, 256), jnp.bfloat16),
            jax.ShapeDtypeStruct((count + 32, 256), jnp.bfloat16),
            jax.ShapeDtypeStruct((32, 256), jnp.float32),
        ),
        in_specs=[pl.BlockSpec(memory_space=pltpu.SMEM)] + [anywhere] * 15 + [inside],
        out_specs=(inside,) * 3,
        scratch_shapes=[
            pltpu.VMEM((count, 8192), jnp.bfloat16),
            pltpu.VMEM((64, 256, 256), jnp.bfloat16),
            pltpu.VMEM((2, count, 256), jnp.float32),
            pltpu.VMEM((count, 128), jnp.float32),
            pltpu.SemaphoreType.DMA((15,)),
        ],
        compiler_params=pltpu.CompilerParams(vmem_limit_bytes=32 * 1024 * 1024),
        cost_estimate=pl.CostEstimate(
            flops=2 * count * 8192 * 512, bytes_accessed=17 * 1024 * 1024, transcendentals=0
        ),
    )(at, *rows, *weights, query)


def pack_log(mine, other, other_lse):
    mine_lse = mine[:, 128]
    top = jnp.maximum(mine_lse, other_lse)
    mine_factor, other_factor = jnp.exp(mine_lse - top), jnp.exp(other_lse - top)
    both = mine_factor + other_factor
    lse = top + jnp.log(both)
    acc = mine_factor[:, None] * mine[:, :128] + other_factor[:, None] * other[:, :128]
    high = lax.reduce_precision(lse, 8, 7)
    mid = lax.reduce_precision(lse - high, 8, 7)
    terms = jnp.stack([high, mid, lse - high - mid])
    terms = jnp.pad(terms, ((0, 0), (0, 96)))
    return jnp.concatenate([acc / both[:, None], terms], axis=0).astype(jnp.bfloat16)


def on_device(
    prompt,
    kv_weight,
    norm_gain,
    kv_cache,
    block_table,
    context_len,
    dest_shard,
    new_query,
    new_keyval,
    out_weight,
):
    x_at, y_at, core = lax.axis_index("x"), lax.axis_index("y"), lax.axis_index("c")
    high = lax.axis_index("zh")
    shard = lax.axis_index(SEQ)
    request = shard // 4
    block_len = kv_cache.shape[1]
    width = new_query.shape[3]
    steps, requests, group = new_query.shape[:3]
    cached, own_blocks = block_table.shape

    half = prompt.shape[0] // 2
    lower = lax.ppermute(prompt, "y", UP)
    upper = lax.ppermute(prompt, "y", DOWN)
    lower_half, upper_half = lower[:half], upper[half:]
    query = lax.dynamic_index_in_dim(new_query, cached + request, 1, keepdims=False)
    query = query.reshape(steps * group, width)

    gain = lax.dynamic_slice_in_dim(norm_gain, shard * kv_weight.shape[0], kv_weight.shape[0])
    scaled = kv_weight.astype(jnp.float32) * gain.astype(jnp.float32)[:, None]
    first = spread(scaled.astype(jnp.bfloat16), RING, 8)

    step_peak, step_total, step_acc = step_stats(new_query, new_keyval[:, :, 0])
    cached_blocks = jnp.take(kv_cache[:, :, 0], block_table, axis=0, mode="clip")
    position = ((shard * own_blocks + jnp.arange(own_blocks, dtype=jnp.int32)) * block_len)[
        :, None
    ] + jnp.arange(block_len, dtype=jnp.int32)[None, :]
    usable = position[None, :, :] < context_len[:, None, None]
    peak, total, acc = paged_stats(new_query[:, :cached], cached_blocks, usable[None, :, None])
    packed = pack(peak.reshape(96), total.reshape(96), acc.reshape(96, width))
    old_step = pack(
        step_peak[:, :cached].reshape(96),
        step_total[:, :cached].reshape(96),
        step_acc[:, :cached].reshape(96, width),
    )
    old_step = lax.dynamic_slice_in_dim(old_step, shard * 3, 3, axis=0)
    step_peak = step_peak[:, cached:].transpose(1, 0, 2).reshape(8, 32)
    step_total = step_total[:, cached:].transpose(1, 0, 2).reshape(8, 32)
    step_acc = step_acc[:, cached:].transpose(1, 0, 2, 3).reshape(8, 32, width)
    x_of = (x_at + jnp.array([0, 3, 1, 0, 3, 1, 2, 2], jnp.int32)) % 4
    core_of = core ^ jnp.array([0, 0, 0, 1, 1, 1, 0, 1], jnp.int32)
    at = jnp.concatenate([x_of * 2048 + core_of * 256, high[None]]).astype(jnp.int32)
    first, packed, query, at, old_step, step_peak, step_total, step_acc = (
        lax.optimization_barrier(
            (first, packed, query, at, old_step, step_peak, step_total, step_acc)
        )
    )
    query = jnp.stack([query, lax.ppermute(query, "zh", SWAP)])
    x_lower = lax.ppermute(first, "x", UP)
    x_upper = lax.ppermute(first, "x", DOWN)

    lower_half, upper_half, packed = lax.optimization_barrier((lower_half, upper_half, packed))
    across = [lax.ppermute(lower_half, "y", UP), lax.ppermute(upper_half, "y", DOWN)]
    x_lower, x_upper, *_ = lax.optimization_barrier((x_lower, x_upper, lower_half, upper_half))
    far = [lax.ppermute(x_lower[:4], "x", UP), lax.ppermute(x_upper[4:], "x", DOWN)]
    old_packed = lax.all_to_all(packed.reshape(32, 3, 256), SEQ, 0, 0, tiled=True)
    weights, across, old_packed = lax.optimization_barrier(
        ([first, x_lower, x_upper] + far, across, old_packed)
    )
    weights = weights + [lax.ppermute(piece, "c", SWAP) for piece in weights]
    kept, given, kept_stats = project(at, [prompt, lower, upper] + across, weights, query)
    got = lax.ppermute(given, "zh", SWAP)
    got_stats = got[-32:].astype(jnp.float32)
    got_lse = jnp.sum(got_stats[:, width : width + 3], axis=1)
    old_packed, dest_shard, _ = lax.optimization_barrier((old_packed, dest_shard, given))
    old = merge(old_packed, old_step)
    packed = jnp.concatenate(
        [pack_log(kept_stats, got_stats, got_lse), old, jnp.zeros((10, width), jnp.bfloat16)], axis=0
    )
    packed = spread(packed, SEQ, 32)
    blocks = jnp.concatenate([kept, got[:-32]], axis=0).reshape(8, -1)

    targets = lax.dynamic_index_in_dim(dest_shard.reshape(32, 4, 2), shard, 0, keepdims=False)
    order = (y_at + jnp.array([0, 3, 1, 2], jnp.int32)) % 4
    mine = jnp.take(targets, order, axis=0, mode="clip").T
    mine = jnp.where(high == 0, mine, mine[::-1]).reshape(8)
    selector = (mine[None, :] == jnp.arange(32, dtype=jnp.int32)[:, None]).astype(jnp.bfloat16)
    outgoing = jnp.dot(selector, blocks, preferred_element_type=jnp.float32)
    outgoing = outgoing.astype(jnp.bfloat16).reshape(32, block_len, 2 * width)
    outgoing, packed = lax.optimization_barrier((outgoing, packed))
    landed = lax.all_to_all(outgoing, SEQ, 0, 0, tiled=True)[:, :, None, :]

    old = packed[:, 35:38].reshape(steps, cached, group, width)
    packed = packed.astype(jnp.float32).reshape(8, 4, 48, width)
    lse = packed[:, :, 32, :32] + packed[:, :, 33, :32] + packed[:, :, 34, :32]
    acc = packed[:, :, :32]
    top = jnp.maximum(jnp.max(lse, axis=1), step_peak)
    factor = jnp.exp(lse - top[:, None])
    step_factor = jnp.exp(step_peak - top)
    total = jnp.sum(factor, axis=1) + step_factor * step_total
    acc = jnp.sum(factor[..., None] * acc, axis=1) + step_factor[..., None] * step_acc
    new = (acc / total[..., None]).astype(jnp.bfloat16).reshape(8, steps, group, width)

    attended = jnp.concatenate([old, new.transpose(1, 0, 2, 3)], axis=1)
    flat_rows = attended.reshape(steps * requests, group * width)
    partial = jnp.dot(flat_rows, out_weight, preferred_element_type=jnp.float32).astype(jnp.bfloat16)
    summed = sum(part.astype(jnp.float32) for part in collect(partial, "y", 4))
    summed = summed + lax.ppermute(summed, "zh", SWAP)
    decoded = summed.astype(jnp.bfloat16).reshape(steps, requests, -1)
    return landed, decoded


def solution(mesh):
    fine = Mesh(mesh.devices.reshape(SIZES), NAMES)
    placed = (
        P(SEQ + TP, None),
        P(SEQ, TP),
        P(),
        P(SEQ, None, TP, None),
        P(None, SEQ),
        P(),
        P(),
        P(None, None, TP, None),
        P(None, None, TP, None),
        P(TP, SEQ),
    )
    return jax.shard_map(
        on_device,
        mesh=fine,
        in_specs=placed,
        out_specs=(P(SEQ, None, TP, None), P(None, None, SEQ)),
        check_vma=False,
    )
```

```python
import jax
import jax.numpy as jnp
from jax import lax
from jax.experimental import pallas as pl
from jax.experimental.pallas import tpu as pltpu
from jax.sharding import Mesh, PartitionSpec as P

EPSILON = 1e-05
NEGATIVE = -1e30
SIZES = (4, 2, 2, 2, 4, 2)
NAMES = ("x", "zp", "zq", "c", "y", "zh")
SEQ = ("x", "zp", "zq", "c")
TP = ("y", "zh")
RING = ("zh", "zp", "zq")
UP = [(i, (i + 1) % 4) for i in range(4)]
DOWN = [(i, (i - 1) % 4) for i in range(4)]
SWAP = [(0, 1), (1, 0)]


def spread(values, axes, count):
    copies = jnp.broadcast_to(values[None], (count,) + values.shape)
    return lax.all_to_all(copies, axes, 0, 0, tiled=True)


def collect(values, axes, count):
    others = [
        lax.ppermute(values, axes, [(i, i ^ bits) for i in range(count)])
        for bits in range(1, count)
    ]
    return [values] + others


def paged_stats(query_matrix, keyval, usable):
    width = query_matrix.shape[-1]
    logit_scores = jnp.einsum(
        "trgd,rpbd->trgpb", query_matrix, keyval[..., :width], preferred_element_type=jnp.float32
    ) * width ** (-0.5)
    masked = jnp.where(usable, logit_scores, NEGATIVE)
    row_peak = jnp.max(masked, axis=(-1, -2))
    weight = jnp.where(usable, jnp.exp(masked - row_peak[..., None, None]), 0.0).astype(jnp.bfloat16)
    total = jnp.sum(weight.astype(jnp.float32), axis=(-1, -2))
    acc = jnp.einsum(
        "trgpb,rpbd->trgd", weight, keyval[..., width:], preferred_element_type=jnp.float32
    )
    return row_peak, total, acc


def step_stats(query_matrix, keyval):
    width = query_matrix.shape[-1]
    steps = query_matrix.shape[0]
    logit_scores = jnp.einsum(
        "trgd,urd->trgu", query_matrix, keyval[..., :width], preferred_element_type=jnp.float32
    ) * width ** (-0.5)
    usable = (jnp.arange(steps)[:, None] >= jnp.arange(steps)[None, :])[:, None, None, :]
    masked = jnp.where(usable, logit_scores, NEGATIVE)
    row_peak = jnp.max(masked, axis=-1)
    weight = jnp.where(usable, jnp.exp(masked - row_peak[..., None]), 0.0).astype(jnp.bfloat16)
    total = jnp.sum(weight.astype(jnp.float32), axis=-1)
    acc = jnp.einsum(
        "trgu,urd->trgd", weight, keyval[..., width:], preferred_element_type=jnp.float32
    )
    return row_peak, total, acc


def pack(peak, total, acc):
    rows = acc.shape[0]
    rest = jnp.zeros((rows, 126), jnp.float32)
    return jnp.concatenate([acc, peak[:, None], total[:, None], rest], axis=1)


def merge(packed, step_packed):
    parts = jnp.concatenate([packed, step_packed[None]], axis=0)
    acc, peak, total = parts[..., :128], parts[..., 128:129], parts[..., 129:130]
    factor = jnp.exp(peak - jnp.max(peak, axis=0, keepdims=True))
    return (jnp.sum(factor * acc, axis=0) / jnp.sum(factor * total, axis=0)).astype(jnp.bfloat16)


def project_kernel(at, *refs):
    rows_in, weights_in, query = refs[:5], refs[5:15], refs[15]
    kept, given, kept_stats = refs[16:19]
    rows, weights, acc, squares, sems = refs[19:]
    count = rows.shape[0]
    order = (0, 1, 2, 5, 6, 7, 3, 4, 8, 9)
    place = (0, 8, 16, 24, 32, 40, 48, 52, 56, 60)
    copies = [
        pltpu.make_async_copy(
            weights_in[k], weights.at[pl.ds(start, weights_in[k].shape[0])], sems.at[n]
        )
        for n, (k, start) in enumerate(zip(order, place))
    ]
    row_copies, start = [], 0
    for n, ref in enumerate(rows_in):
        row_copies.append(
            pltpu.make_async_copy(ref, rows.at[pl.ds(start, ref.shape[0])], sems.at[10 + n])
        )
        start += ref.shape[0]
    copies[0].start()
    for copy in row_copies + copies[1:]:
        copy.start()
    acc[...] = jnp.zeros_like(acc)
    squares[...] = jnp.zeros_like(squares)
    for copy in row_copies:
        copy.wait()
    high = at[8]
    for p in range(8):
        for copy in copies[p : p + 1] if p < 6 else copies[2 * p - 6 : 2 * p - 4]:
            copy.wait()
        base = at[p]
        columns = [
            rows[:, pl.ds(pl.multiple_of(base + 512 * zl, 256), 256)] for zl in range(4)
        ]
        total = squares[...]
        for column in columns:
            wide = column.astype(jnp.float32)
            wide = wide * wide
            total += wide[:, :128] + wide[:, 128:]
        squares[...] = total
        joined = jnp.concatenate(columns, axis=1)
        for j in range(2):
            at_head = 8 * p + 4 * (high if j == 0 else 1 - high)
            tile = weights[pl.ds(at_head, 4)].reshape(1024, 256)
            acc[j] += jnp.dot(joined, tile, preferred_element_type=jnp.float32)
    mean = jnp.sum(squares[...], axis=-1, keepdims=True) / rows.shape[1]
    factor = lax.rsqrt(mean + EPSILON)
    lane = lax.broadcasted_iota(jnp.int32, (32, 128), 1)
    for j, out in enumerate((kept, given)):
        keyval = (acc[j] * factor).astype(jnp.bfloat16)
        out[:count] = keyval
        scores = lax.dot_general(
            query[j],
            keyval[:, :128],
            (((1,), (1,)), ((), ())),
            preferred_element_type=jnp.float32,
        ) * 128 ** (-0.5)
        peak = jnp.max(scores, axis=-1, keepdims=True)
        weight = jnp.exp(scores - peak).astype(jnp.bfloat16)
        total = jnp.sum(weight.astype(jnp.float32), axis=-1, keepdims=True)
        value = jnp.dot(weight, keyval[:, 128:], preferred_element_type=jnp.float32)
        lse = jnp.broadcast_to(peak + jnp.log(total), (32, 128))
        if j == 0:
            kept_stats[:, :128] = value / total
            kept_stats[:, 128:] = lse
        else:
            first = lse.astype(jnp.bfloat16).astype(jnp.float32)
            second = (lse - first).astype(jnp.bfloat16).astype(jnp.float32)
            third = lse - first - second
            terms = jnp.where(lane == 0, first, jnp.where(lane == 1, second, third))
            packed = jnp.concatenate([value / total, terms], axis=1)
            given[count:] = packed.astype(jnp.bfloat16)


def project(at, rows, weights, query):
    count = sum(part.shape[0] for part in rows)
    outside = pl.BlockSpec(memory_space=pl.ANY)
    inside = pl.BlockSpec(memory_space=pltpu.VMEM)
    return pl.pallas_call(
        project_kernel,
        out_shape=(
            jax.ShapeDtypeStruct((count, 256), jnp.bfloat16),
            jax.ShapeDtypeStruct((count + 32, 256), jnp.bfloat16),
            jax.ShapeDtypeStruct((32, 256), jnp.float32),
        ),
        in_specs=[pl.BlockSpec(memory_space=pltpu.SMEM)] + [outside] * 15 + [inside],
        out_specs=(inside,) * 3,
        scratch_shapes=[
            pltpu.VMEM((count, 8192), jnp.bfloat16),
            pltpu.VMEM((64, 256, 256), jnp.bfloat16),
            pltpu.VMEM((2, count, 256), jnp.float32),
            pltpu.VMEM((count, 128), jnp.float32),
            pltpu.SemaphoreType.DMA((15,)),
        ],
        compiler_params=pltpu.CompilerParams(vmem_limit_bytes=24 * 1024 * 1024),
        cost_estimate=pl.CostEstimate(
            flops=2 * count * 8192 * 512, bytes_accessed=17 * 1024 * 1024, transcendentals=0
        ),
    )(at, *rows, *weights, query)


def pack_log(mine, other, other_lse):
    mine_lse = mine[:, 128]
    top = jnp.maximum(mine_lse, other_lse)
    mine_factor, other_factor = jnp.exp(mine_lse - top), jnp.exp(other_lse - top)
    both = mine_factor + other_factor
    lse = top + jnp.log(both)
    acc = mine_factor[:, None] * mine[:, :128] + other_factor[:, None] * other[:, :128]
    high = lax.reduce_precision(lse, 8, 7)
    mid = lax.reduce_precision(lse - high, 8, 7)
    terms = jnp.stack([high, mid, lse - high - mid])
    terms = jnp.pad(terms, ((0, 0), (0, 96)))
    return jnp.concatenate([acc / both[:, None], terms], axis=0).astype(jnp.bfloat16)


def on_device(
    prompt,
    kv_weight,
    norm_gain,
    kv_cache,
    block_table,
    context_len,
    dest_shard,
    new_query,
    new_keyval,
    out_weight,
):
    x_at, y_at, core = lax.axis_index("x"), lax.axis_index("y"), lax.axis_index("c")
    high = lax.axis_index("zh")
    shard = lax.axis_index(SEQ)
    request = shard // 4
    block_len = kv_cache.shape[1]
    width = new_query.shape[3]
    steps, requests, group = new_query.shape[:3]
    cached, own_blocks = block_table.shape

    half = prompt.shape[0] // 2
    lower = lax.ppermute(prompt, "y", UP)
    upper = lax.ppermute(prompt, "y", DOWN)
    lower_half, upper_half = lower[:half], upper[half:]
    query = lax.dynamic_index_in_dim(new_query, cached + request, 1, keepdims=False)
    query = query.reshape(steps * group, width)

    gain = lax.dynamic_slice_in_dim(norm_gain, shard * kv_weight.shape[0], kv_weight.shape[0])
    scaled = kv_weight.astype(jnp.float32) * gain.astype(jnp.float32)[:, None]
    first = spread(scaled.astype(jnp.bfloat16), RING, 8)

    step_peak, step_total, step_acc = step_stats(new_query, new_keyval[:, :, 0])
    cached_blocks = jnp.take(kv_cache[:, :, 0], block_table, axis=0, mode="clip")
    position = ((shard * own_blocks + jnp.arange(own_blocks, dtype=jnp.int32)) * block_len)[
        :, None
    ] + jnp.arange(block_len, dtype=jnp.int32)[None, :]
    usable = position[None, :, :] < context_len[:, None, None]
    peak, total, acc = paged_stats(new_query[:, :cached], cached_blocks, usable[None, :, None])
    packed = pack(peak.reshape(96), total.reshape(96), acc.reshape(96, width))
    old_step = pack(
        step_peak[:, :cached].reshape(96),
        step_total[:, :cached].reshape(96),
        step_acc[:, :cached].reshape(96, width),
    )
    old_step = lax.dynamic_slice_in_dim(old_step, shard * 3, 3, axis=0)
    step_peak = step_peak[:, cached:].transpose(1, 0, 2).reshape(8, 32)
    step_total = step_total[:, cached:].transpose(1, 0, 2).reshape(8, 32)
    step_acc = step_acc[:, cached:].transpose(1, 0, 2, 3).reshape(8, 32, width)
    x_of = (x_at + jnp.array([0, 3, 1, 0, 3, 1, 2, 2], jnp.int32)) % 4
    core_of = core ^ jnp.array([0, 0, 0, 1, 1, 1, 0, 1], jnp.int32)
    at = jnp.concatenate([x_of * 2048 + core_of * 256, high[None]]).astype(jnp.int32)
    first, packed, query, at, old_step, step_peak, step_total, step_acc = (
        lax.optimization_barrier(
            (first, packed, query, at, old_step, step_peak, step_total, step_acc)
        )
    )
    query = jnp.stack([query, lax.ppermute(query, "zh", SWAP)])
    x_lower = lax.ppermute(first, "x", UP)
    x_upper = lax.ppermute(first, "x", DOWN)

    lower_half, upper_half, packed = lax.optimization_barrier((lower_half, upper_half, packed))
    across = [lax.ppermute(lower_half, "y", UP), lax.ppermute(upper_half, "y", DOWN)]
    x_lower, x_upper, *_ = lax.optimization_barrier((x_lower, x_upper, lower_half, upper_half))
    far = [lax.ppermute(x_lower[:4], "x", UP), lax.ppermute(x_upper[4:], "x", DOWN)]
    old_packed = lax.all_to_all(packed.reshape(32, 3, 256), SEQ, 0, 0, tiled=True)
    weights, across, old_packed, query = lax.optimization_barrier(
        ([first, x_lower, x_upper] + far, across, old_packed, query)
    )
    weights = weights + [lax.ppermute(piece, "c", SWAP) for piece in weights]
    kept, given, kept_stats = project(at, [prompt, lower, upper] + across, weights, query)
    got = lax.ppermute(given, "zh", SWAP)
    got_stats = got[-32:].astype(jnp.float32)
    got_lse = jnp.sum(got_stats[:, width : width + 3], axis=1)
    old_packed, dest_shard, _ = lax.optimization_barrier((old_packed, dest_shard, given))
    old = merge(old_packed, old_step)
    packed = jnp.concatenate(
        [pack_log(kept_stats, got_stats, got_lse), old, jnp.zeros((10, width), jnp.bfloat16)], axis=0
    )
    packed = spread(packed, SEQ, 32)
    blocks = jnp.concatenate([kept, got[:-32]], axis=0).reshape(8, -1)

    targets = lax.dynamic_index_in_dim(dest_shard.reshape(32, 4, 2), shard, 0, keepdims=False)
    order = (y_at + jnp.array([0, 3, 1, 2], jnp.int32)) % 4
    mine = jnp.take(targets, order, axis=0, mode="clip").T
    mine = jnp.where(high == 0, mine, mine[::-1]).reshape(8)
    selector = (mine[None, :] == jnp.arange(32, dtype=jnp.int32)[:, None]).astype(jnp.bfloat16)
    outgoing = jnp.dot(selector, blocks, preferred_element_type=jnp.float32)
    outgoing = outgoing.astype(jnp.bfloat16).reshape(32, block_len, 2 * width)
    outgoing, packed = lax.optimization_barrier((outgoing, packed))
    landed = lax.all_to_all(outgoing, SEQ, 0, 0, tiled=True)[:, :, None, :]

    old = packed[:, 35:38].reshape(steps, cached, group, width)
    packed = packed.astype(jnp.float32).reshape(8, 4, 48, width)
    lse = packed[:, :, 32, :32] + packed[:, :, 33, :32] + packed[:, :, 34, :32]
    acc = packed[:, :, :32]
    top = jnp.maximum(jnp.max(lse, axis=1), step_peak)
    factor = jnp.exp(lse - top[:, None])
    step_factor = jnp.exp(step_peak - top)
    total = jnp.sum(factor, axis=1) + step_factor * step_total
    acc = jnp.sum(factor[..., None] * acc, axis=1) + step_factor[..., None] * step_acc
    new = (acc / total[..., None]).astype(jnp.bfloat16).reshape(8, steps, group, width)

    attended = jnp.concatenate([old, new.transpose(1, 0, 2, 3)], axis=1)
    flat_rows = attended.reshape(steps * requests, group * width)
    partial = jnp.dot(flat_rows, out_weight, preferred_element_type=jnp.float32).astype(jnp.bfloat16)
    summed = sum(part.astype(jnp.float32) for part in collect(partial, "y", 4))
    summed = summed + lax.ppermute(summed, "zh", SWAP)
    decoded = summed.astype(jnp.bfloat16).reshape(steps, requests, -1)
    return landed, decoded


def solution(mesh):
    fine = Mesh(mesh.devices.reshape(SIZES), NAMES)
    placed = (
        P(SEQ + TP, None),
        P(SEQ, TP),
        P(),
        P(SEQ, None, TP, None),
        P(None, SEQ),
        P(),
        P(),
        P(None, None, TP, None),
        P(None, None, TP, None),
        P(TP, SEQ),
    )
    return jax.shard_map(
        on_device,
        mesh=fine,
        in_specs=placed,
        out_specs=(P(SEQ, None, TP, None), P(None, None, SEQ)),
        check_vma=False,
    )
```

```python
import jax
import jax.numpy as jnp
from jax import lax
from jax.experimental import pallas as pl
from jax.experimental.pallas import tpu as pltpu
from jax.sharding import Mesh, PartitionSpec as P

EPSILON = 1e-05
NEGATIVE = -1e30
SIZES = (4, 2, 2, 2, 4, 2)
NAMES = ("x", "zp", "zq", "c", "y", "zh")
SEQ = ("x", "zp", "zq", "c")
TP = ("y", "zh")
RING = ("zh", "zp", "zq")
UP = [(i, (i + 1) % 4) for i in range(4)]
DOWN = [(i, (i - 1) % 4) for i in range(4)]
SWAP = [(0, 1), (1, 0)]


def spread(values, axes, count):
    copies = jnp.broadcast_to(values[None], (count,) + values.shape)
    return lax.all_to_all(copies, axes, 0, 0, tiled=True)


def collect(values, axes, count):
    others = [
        lax.ppermute(values, axes, [(i, i ^ bits) for i in range(count)])
        for bits in range(1, count)
    ]
    return [values] + others


def paged_stats(query_matrix, keyval, usable):
    width = query_matrix.shape[-1]
    logit_scores = jnp.einsum(
        "trgd,rpbd->trgpb", query_matrix, keyval[..., :width], preferred_element_type=jnp.float32
    ) * width ** (-0.5)
    masked = jnp.where(usable, logit_scores, NEGATIVE)
    row_peak = jnp.max(masked, axis=(-1, -2))
    weight = jnp.where(usable, jnp.exp(masked - row_peak[..., None, None]), 0.0).astype(jnp.bfloat16)
    total = jnp.sum(weight.astype(jnp.float32), axis=(-1, -2))
    acc = jnp.einsum(
        "trgpb,rpbd->trgd", weight, keyval[..., width:], preferred_element_type=jnp.float32
    )
    return row_peak, total, acc


def step_stats(query_matrix, keyval):
    width = query_matrix.shape[-1]
    steps = query_matrix.shape[0]
    logit_scores = jnp.einsum(
        "trgd,urd->trgu", query_matrix, keyval[..., :width], preferred_element_type=jnp.float32
    ) * width ** (-0.5)
    usable = (jnp.arange(steps)[:, None] >= jnp.arange(steps)[None, :])[:, None, None, :]
    masked = jnp.where(usable, logit_scores, NEGATIVE)
    row_peak = jnp.max(masked, axis=-1)
    weight = jnp.where(usable, jnp.exp(masked - row_peak[..., None]), 0.0).astype(jnp.bfloat16)
    total = jnp.sum(weight.astype(jnp.float32), axis=-1)
    acc = jnp.einsum(
        "trgu,urd->trgd", weight, keyval[..., width:], preferred_element_type=jnp.float32
    )
    return row_peak, total, acc


def pack(peak, total, acc):
    rows = acc.shape[0]
    rest = jnp.zeros((rows, 126), jnp.float32)
    return jnp.concatenate([acc, peak[:, None], total[:, None], rest], axis=1)


def merge(packed, step_packed):
    parts = jnp.concatenate([packed, step_packed[None]], axis=0)
    acc, peak, total = parts[..., :128], parts[..., 128:129], parts[..., 129:130]
    factor = jnp.exp(peak - jnp.max(peak, axis=0, keepdims=True))
    return (jnp.sum(factor * acc, axis=0) / jnp.sum(factor * total, axis=0)).astype(jnp.bfloat16)


def project_kernel(at, *refs):
    rows_in, weights_in, query = refs[:5], refs[5:15], refs[15]
    kept, given, kept_stats = refs[16:19]
    rows, weights, acc, squares, sems = refs[19:]
    count = rows.shape[0]
    order = (0, 1, 2, 5, 6, 7, 3, 4, 8, 9)
    place = (0, 8, 16, 24, 32, 40, 48, 52, 56, 60)
    copies = [
        pltpu.make_async_copy(
            weights_in[k], weights.at[pl.ds(start, weights_in[k].shape[0])], sems.at[n]
        )
        for n, (k, start) in enumerate(zip(order, place))
    ]
    count = rows.shape[0]
    row_copies = []
    for quarter in range(4):
        span = pl.ds(pl.multiple_of(at[9 + quarter], 2048), 2048)
        start, part = 0, []
        for n, ref in enumerate(rows_in):
            part.append(
                pltpu.make_async_copy(
                    ref.at[:, span],
                    rows.at[pl.ds(start, ref.shape[0]), span],
                    sems.at[10 + 5 * quarter + n],
                )
            )
            start += ref.shape[0]
        row_copies.append(part)
    piece_copies = [copies[:1] + copies[3:4], copies[1:2] + copies[4:5], copies[2:3] + copies[5:6], copies[6:]]
    for quarter in range(4):
        for copy in row_copies[quarter] + piece_copies[quarter]:
            copy.start()
    acc[...] = jnp.zeros_like(acc)
    squares[...] = jnp.zeros_like(squares)
    high = at[8]
    for step, p in enumerate((0, 3, 1, 4, 2, 5, 6, 7)):
        if step % 2 == 0:
            for copy in row_copies[step // 2] + piece_copies[step // 2]:
                copy.wait()
        base = at[p]
        columns = [
            rows[:, pl.ds(pl.multiple_of(base + 512 * zl, 256), 256)] for zl in range(4)
        ]
        total = squares[...]
        for column in columns:
            wide = column.astype(jnp.float32)
            wide = wide * wide
            total += wide[:, :128] + wide[:, 128:]
        squares[...] = total
        joined = jnp.concatenate(columns, axis=1)
        for j in range(2):
            at_head = 8 * p + 4 * (high if j == 0 else 1 - high)
            tile = weights[pl.ds(at_head, 4)].reshape(1024, 256)
            acc[j] += jnp.dot(joined, tile, preferred_element_type=jnp.float32)
    mean = jnp.sum(squares[...], axis=-1, keepdims=True) / rows.shape[1]
    factor = lax.rsqrt(mean + EPSILON)
    lane = lax.broadcasted_iota(jnp.int32, (32, 128), 1)
    for j, out in enumerate((kept, given)):
        keyval = (acc[j] * factor).astype(jnp.bfloat16)
        out[:count] = keyval
        scores = lax.dot_general(
            query[j],
            keyval[:, :128],
            (((1,), (1,)), ((), ())),
            preferred_element_type=jnp.float32,
        ) * 128 ** (-0.5)
        peak = jnp.max(scores, axis=-1, keepdims=True)
        weight = jnp.exp(scores - peak).astype(jnp.bfloat16)
        total = jnp.sum(weight.astype(jnp.float32), axis=-1, keepdims=True)
        value = jnp.dot(weight, keyval[:, 128:], preferred_element_type=jnp.float32)
        lse = jnp.broadcast_to(peak + jnp.log(total), (32, 128))
        if j == 0:
            kept_stats[:, :128] = value / total
            kept_stats[:, 128:] = lse
        else:
            first = lse.astype(jnp.bfloat16).astype(jnp.float32)
            second = (lse - first).astype(jnp.bfloat16).astype(jnp.float32)
            third = lse - first - second
            terms = jnp.where(lane == 0, first, jnp.where(lane == 1, second, third))
            packed = jnp.concatenate([value / total, terms], axis=1)
            given[count:] = packed.astype(jnp.bfloat16)


def project(at, rows, weights, query):
    count = sum(part.shape[0] for part in rows)
    outside = pl.BlockSpec(memory_space=pl.ANY)
    inside = pl.BlockSpec(memory_space=pltpu.VMEM)
    return pl.pallas_call(
        project_kernel,
        out_shape=(
            jax.ShapeDtypeStruct((count, 256), jnp.bfloat16),
            jax.ShapeDtypeStruct((count + 32, 256), jnp.bfloat16),
            jax.ShapeDtypeStruct((32, 256), jnp.float32),
        ),
        in_specs=[pl.BlockSpec(memory_space=pltpu.SMEM)] + [outside] * 15 + [inside],
        out_specs=(inside,) * 3,
        scratch_shapes=[
            pltpu.VMEM((count, 8192), jnp.bfloat16),
            pltpu.VMEM((64, 256, 256), jnp.bfloat16),
            pltpu.VMEM((2, count, 256), jnp.float32),
            pltpu.VMEM((count, 128), jnp.float32),
            pltpu.SemaphoreType.DMA((30,)),
        ],
        compiler_params=pltpu.CompilerParams(vmem_limit_bytes=24 * 1024 * 1024),
        cost_estimate=pl.CostEstimate(
            flops=2 * count * 8192 * 512, bytes_accessed=17 * 1024 * 1024, transcendentals=0
        ),
    )(at, *rows, *weights, query)


def pack_log(mine, other, other_lse):
    mine_lse = mine[:, 128]
    top = jnp.maximum(mine_lse, other_lse)
    mine_factor, other_factor = jnp.exp(mine_lse - top), jnp.exp(other_lse - top)
    both = mine_factor + other_factor
    lse = top + jnp.log(both)
    acc = mine_factor[:, None] * mine[:, :128] + other_factor[:, None] * other[:, :128]
    high = lax.reduce_precision(lse, 8, 7)
    mid = lax.reduce_precision(lse - high, 8, 7)
    terms = jnp.stack([high, mid, lse - high - mid])
    terms = jnp.pad(terms, ((0, 0), (0, 96)))
    return jnp.concatenate([acc / both[:, None], terms], axis=0).astype(jnp.bfloat16)


def on_device(
    prompt,
    kv_weight,
    norm_gain,
    kv_cache,
    block_table,
    context_len,
    dest_shard,
    new_query,
    new_keyval,
    out_weight,
):
    x_at, y_at, core = lax.axis_index("x"), lax.axis_index("y"), lax.axis_index("c")
    high = lax.axis_index("zh")
    shard = lax.axis_index(SEQ)
    request = shard // 4
    block_len = kv_cache.shape[1]
    width = new_query.shape[3]
    steps, requests, group = new_query.shape[:3]
    cached, own_blocks = block_table.shape

    half = prompt.shape[0] // 2
    lower = lax.ppermute(prompt, "y", UP)
    upper = lax.ppermute(prompt, "y", DOWN)
    lower_half, upper_half = lower[:half], upper[half:]
    query = lax.dynamic_index_in_dim(new_query, cached + request, 1, keepdims=False)
    query = query.reshape(steps * group, width)

    gain = lax.dynamic_slice_in_dim(norm_gain, shard * kv_weight.shape[0], kv_weight.shape[0])
    scaled = kv_weight.astype(jnp.float32) * gain.astype(jnp.float32)[:, None]
    first = spread(scaled.astype(jnp.bfloat16), RING, 8)

    step_peak, step_total, step_acc = step_stats(new_query, new_keyval[:, :, 0])
    cached_blocks = jnp.take(kv_cache[:, :, 0], block_table, axis=0, mode="clip")
    position = ((shard * own_blocks + jnp.arange(own_blocks, dtype=jnp.int32)) * block_len)[
        :, None
    ] + jnp.arange(block_len, dtype=jnp.int32)[None, :]
    usable = position[None, :, :] < context_len[:, None, None]
    peak, total, acc = paged_stats(new_query[:, :cached], cached_blocks, usable[None, :, None])
    packed = pack(peak.reshape(96), total.reshape(96), acc.reshape(96, width))
    old_step = pack(
        step_peak[:, :cached].reshape(96),
        step_total[:, :cached].reshape(96),
        step_acc[:, :cached].reshape(96, width),
    )
    old_step = lax.dynamic_slice_in_dim(old_step, shard * 3, 3, axis=0)
    step_peak = step_peak[:, cached:].transpose(1, 0, 2).reshape(8, 32)
    step_total = step_total[:, cached:].transpose(1, 0, 2).reshape(8, 32)
    step_acc = step_acc[:, cached:].transpose(1, 0, 2, 3).reshape(8, 32, width)
    x_of = (x_at + jnp.array([0, 3, 1, 0, 3, 1, 2, 2], jnp.int32)) % 4
    core_of = core ^ jnp.array([0, 0, 0, 1, 1, 1, 0, 1], jnp.int32)
    quarters = x_of[jnp.array([0, 1, 2, 6])] * 2048
    at = jnp.concatenate([x_of * 2048 + core_of * 256, high[None], quarters]).astype(jnp.int32)
    first, packed, query, at, old_step, step_peak, step_total, step_acc = (
        lax.optimization_barrier(
            (first, packed, query, at, old_step, step_peak, step_total, step_acc)
        )
    )
    query = jnp.stack([query, lax.ppermute(query, "zh", SWAP)])
    x_lower = lax.ppermute(first, "x", UP)
    x_upper = lax.ppermute(first, "x", DOWN)

    lower_half, upper_half, packed = lax.optimization_barrier((lower_half, upper_half, packed))
    across = [lax.ppermute(lower_half, "y", UP), lax.ppermute(upper_half, "y", DOWN)]
    x_lower, x_upper, *_ = lax.optimization_barrier((x_lower, x_upper, lower_half, upper_half))
    far = [lax.ppermute(x_lower[:4], "x", UP), lax.ppermute(x_upper[4:], "x", DOWN)]
    old_packed = lax.all_to_all(packed.reshape(32, 3, 256), SEQ, 0, 0, tiled=True)
    weights, across, old_packed, query = lax.optimization_barrier(
        ([first, x_lower, x_upper] + far, across, old_packed, query)
    )
    weights = weights + [lax.ppermute(piece, "c", SWAP) for piece in weights]
    rows = [pltpu.with_memory_space_constraint(prompt, pltpu.HBM), lower, upper] + across
    weights[1:3] = [pltpu.with_memory_space_constraint(part, pltpu.HBM) for part in weights[1:3]]
    kept, given, kept_stats = project(at, rows, weights, query)
    got = lax.ppermute(given, "zh", SWAP)
    got_stats = got[-32:].astype(jnp.float32)
    got_lse = jnp.sum(got_stats[:, width : width + 3], axis=1)
    old_packed, dest_shard, _ = lax.optimization_barrier((old_packed, dest_shard, given))
    old = merge(old_packed, old_step)
    packed = jnp.concatenate(
        [pack_log(kept_stats, got_stats, got_lse), old, jnp.zeros((10, width), jnp.bfloat16)], axis=0
    )
    packed = spread(packed, SEQ, 32)
    blocks = jnp.concatenate([kept, got[:-32]], axis=0).reshape(8, -1)

    targets = lax.dynamic_index_in_dim(dest_shard.reshape(32, 4, 2), shard, 0, keepdims=False)
    order = (y_at + jnp.array([0, 3, 1, 2], jnp.int32)) % 4
    mine = jnp.take(targets, order, axis=0, mode="clip").T
    mine = jnp.where(high == 0, mine, mine[::-1]).reshape(8)
    selector = (mine[None, :] == jnp.arange(32, dtype=jnp.int32)[:, None]).astype(jnp.bfloat16)
    outgoing = jnp.dot(selector, blocks, preferred_element_type=jnp.float32)
    outgoing = outgoing.astype(jnp.bfloat16).reshape(32, block_len, 2 * width)
    outgoing, packed = lax.optimization_barrier((outgoing, packed))
    landed = lax.all_to_all(outgoing, SEQ, 0, 0, tiled=True)[:, :, None, :]

    old = packed[:, 35:38].reshape(steps, cached, group, width)
    packed = packed.astype(jnp.float32).reshape(8, 4, 48, width)
    lse = packed[:, :, 32, :32] + packed[:, :, 33, :32] + packed[:, :, 34, :32]
    acc = packed[:, :, :32]
    top = jnp.maximum(jnp.max(lse, axis=1), step_peak)
    factor = jnp.exp(lse - top[:, None])
    step_factor = jnp.exp(step_peak - top)
    total = jnp.sum(factor, axis=1) + step_factor * step_total
    acc = jnp.sum(factor[..., None] * acc, axis=1) + step_factor[..., None] * step_acc
    new = (acc / total[..., None]).astype(jnp.bfloat16).reshape(8, steps, group, width)

    attended = jnp.concatenate([old, new.transpose(1, 0, 2, 3)], axis=1)
    flat_rows = attended.reshape(steps * requests, group * width)
    partial = jnp.dot(flat_rows, out_weight, preferred_element_type=jnp.float32).astype(jnp.bfloat16)
    summed = sum(part.astype(jnp.float32) for part in collect(partial, "y", 4))
    summed = summed + lax.ppermute(summed, "zh", SWAP)
    decoded = summed.astype(jnp.bfloat16).reshape(steps, requests, -1)
    return landed, decoded


def solution(mesh):
    fine = Mesh(mesh.devices.reshape(SIZES), NAMES)
    placed = (
        P(SEQ + TP, None),
        P(SEQ, TP),
        P(),
        P(SEQ, None, TP, None),
        P(None, SEQ),
        P(),
        P(),
        P(None, None, TP, None),
        P(None, None, TP, None),
        P(TP, SEQ),
    )
    return jax.shard_map(
        on_device,
        mesh=fine,
        in_specs=placed,
        out_specs=(P(SEQ, None, TP, None), P(None, None, SEQ)),
        check_vma=False,
    )
```

```python
import jax
import jax.numpy as jnp
from jax import lax
from jax.experimental import pallas as pl
from jax.experimental.pallas import tpu as pltpu
from jax.sharding import Mesh, PartitionSpec as P

EPSILON = 1e-05
NEGATIVE = -1e30
SIZES = (4, 2, 2, 2, 4, 2)
NAMES = ("x", "zp", "zq", "c", "y", "zh")
SEQ = ("x", "zp", "zq", "c")
TP = ("y", "zh")
RING = ("zh", "zp", "zq")
UP = [(i, (i + 1) % 4) for i in range(4)]
DOWN = [(i, (i - 1) % 4) for i in range(4)]
SWAP = [(0, 1), (1, 0)]


def spread(values, axes, count):
    copies = jnp.broadcast_to(values[None], (count,) + values.shape)
    return lax.all_to_all(copies, axes, 0, 0, tiled=True)


def collect(values, axes, count):
    others = [
        lax.ppermute(values, axes, [(i, i ^ bits) for i in range(count)])
        for bits in range(1, count)
    ]
    return [values] + others


def paged_stats(query_matrix, keyval, usable):
    width = query_matrix.shape[-1]
    logit_scores = jnp.einsum(
        "trgd,rpbd->trgpb", query_matrix, keyval[..., :width], preferred_element_type=jnp.float32
    ) * width ** (-0.5)
    masked = jnp.where(usable, logit_scores, NEGATIVE)
    row_peak = jnp.max(masked, axis=(-1, -2))
    weight = jnp.where(usable, jnp.exp(masked - row_peak[..., None, None]), 0.0).astype(jnp.bfloat16)
    total = jnp.sum(weight.astype(jnp.float32), axis=(-1, -2))
    acc = jnp.einsum(
        "trgpb,rpbd->trgd", weight, keyval[..., width:], preferred_element_type=jnp.float32
    )
    return row_peak, total, acc


def step_stats(query_matrix, keyval):
    width = query_matrix.shape[-1]
    steps = query_matrix.shape[0]
    logit_scores = jnp.einsum(
        "trgd,urd->trgu", query_matrix, keyval[..., :width], preferred_element_type=jnp.float32
    ) * width ** (-0.5)
    usable = (jnp.arange(steps)[:, None] >= jnp.arange(steps)[None, :])[:, None, None, :]
    masked = jnp.where(usable, logit_scores, NEGATIVE)
    row_peak = jnp.max(masked, axis=-1)
    weight = jnp.where(usable, jnp.exp(masked - row_peak[..., None]), 0.0).astype(jnp.bfloat16)
    total = jnp.sum(weight.astype(jnp.float32), axis=-1)
    acc = jnp.einsum(
        "trgu,urd->trgd", weight, keyval[..., width:], preferred_element_type=jnp.float32
    )
    return row_peak, total, acc


def pack(peak, total, acc):
    rows = acc.shape[0]
    rest = jnp.zeros((rows, 126), jnp.float32)
    return jnp.concatenate([acc, peak[:, None], total[:, None], rest], axis=1)


def merge(packed, step_packed):
    parts = jnp.concatenate([packed, step_packed[None]], axis=0)
    acc, peak, total = parts[..., :128], parts[..., 128:129], parts[..., 129:130]
    factor = jnp.exp(peak - jnp.max(peak, axis=0, keepdims=True))
    return (jnp.sum(factor * acc, axis=0) / jnp.sum(factor * total, axis=0)).astype(jnp.bfloat16)


def project_kernel(at, *refs):
    rows_in, weights_in, query = refs[:5], refs[5:15], refs[15]
    kept, given, kept_stats = refs[16:19]
    rows, weights, acc, squares, sems = refs[19:]
    count = rows.shape[0]
    order = (0, 1, 2, 5, 6, 7, 3, 4, 8, 9)
    place = (0, 8, 16, 24, 32, 40, 48, 52, 56, 60)
    copies = [
        pltpu.make_async_copy(
            weights_in[k], weights.at[pl.ds(start, weights_in[k].shape[0])], sems.at[n]
        )
        for n, (k, start) in enumerate(zip(order, place))
    ]
    count = rows.shape[0]
    row_copies = []
    for quarter in range(4):
        span = pl.ds(pl.multiple_of(at[9 + quarter], 2048), 2048)
        start, part = 0, []
        for n, ref in enumerate(rows_in):
            part.append(
                pltpu.make_async_copy(
                    ref.at[:, span],
                    rows.at[pl.ds(start, ref.shape[0]), span],
                    sems.at[10 + 5 * quarter + n],
                )
            )
            start += ref.shape[0]
        row_copies.append(part)
    piece_copies = [copies[:1] + copies[3:4], copies[1:2] + copies[4:5], copies[2:3] + copies[5:6], copies[6:]]
    for quarter in range(4):
        for copy in row_copies[quarter] + piece_copies[quarter]:
            copy.start()
    acc[...] = jnp.zeros_like(acc)
    squares[...] = jnp.zeros_like(squares)
    high = at[8]
    for step, p in enumerate((0, 3, 1, 4, 2, 5, 6, 7)):
        if step % 2 == 0:
            for copy in row_copies[step // 2] + piece_copies[step // 2]:
                copy.wait()
        base = at[p]
        columns = [
            rows[:, pl.ds(pl.multiple_of(base + 512 * zl, 256), 256)] for zl in range(4)
        ]
        total = squares[...]
        for column in columns:
            wide = column.astype(jnp.float32)
            wide = wide * wide
            total += wide[:, :128] + wide[:, 128:]
        squares[...] = total
        joined = jnp.concatenate(columns, axis=1)
        for j in range(2):
            at_head = 8 * p + 4 * (high if j == 0 else 1 - high)
            tile = weights[pl.ds(at_head, 4)].reshape(1024, 256)
            acc[j] += jnp.dot(joined, tile, preferred_element_type=jnp.float32)
    mean = jnp.sum(squares[...], axis=-1, keepdims=True) / rows.shape[1]
    factor = lax.rsqrt(mean + EPSILON)
    lane = lax.broadcasted_iota(jnp.int32, (32, 128), 1)
    for j, out in enumerate((kept, given)):
        keyval = (acc[j] * factor).astype(jnp.bfloat16)
        out[:count] = keyval
        scores = lax.dot_general(
            query[j],
            keyval[:, :128],
            (((1,), (1,)), ((), ())),
            preferred_element_type=jnp.float32,
        ) * 128 ** (-0.5)
        peak = jnp.max(scores, axis=-1, keepdims=True)
        weight = jnp.exp(scores - peak).astype(jnp.bfloat16)
        total = jnp.sum(weight.astype(jnp.float32), axis=-1, keepdims=True)
        value = jnp.dot(weight, keyval[:, 128:], preferred_element_type=jnp.float32)
        lse = jnp.broadcast_to(peak + jnp.log(total), (32, 128))
        if j == 0:
            kept_stats[:, :128] = value / total
            kept_stats[:, 128:] = lse
        else:
            first = lse.astype(jnp.bfloat16).astype(jnp.float32)
            second = (lse - first).astype(jnp.bfloat16).astype(jnp.float32)
            third = lse - first - second
            terms = jnp.where(lane == 0, first, jnp.where(lane == 1, second, third))
            packed = jnp.concatenate([value / total, terms], axis=1)
            given[count:] = packed.astype(jnp.bfloat16)


def project(at, rows, weights, query):
    count = sum(part.shape[0] for part in rows)
    outside = pl.BlockSpec(memory_space=pl.ANY)
    inside = pl.BlockSpec(memory_space=pltpu.VMEM)
    return pl.pallas_call(
        project_kernel,
        out_shape=(
            jax.ShapeDtypeStruct((count, 256), jnp.bfloat16),
            jax.ShapeDtypeStruct((count + 32, 256), jnp.bfloat16),
            jax.ShapeDtypeStruct((32, 256), jnp.float32),
        ),
        in_specs=[pl.BlockSpec(memory_space=pltpu.SMEM)] + [outside] * 15 + [inside],
        out_specs=(inside,) * 3,
        scratch_shapes=[
            pltpu.VMEM((count, 8192), jnp.bfloat16),
            pltpu.VMEM((64, 256, 256), jnp.bfloat16),
            pltpu.VMEM((2, count, 256), jnp.float32),
            pltpu.VMEM((count, 128), jnp.float32),
            pltpu.SemaphoreType.DMA((30,)),
        ],
        compiler_params=pltpu.CompilerParams(vmem_limit_bytes=24 * 1024 * 1024),
        cost_estimate=pl.CostEstimate(
            flops=2 * count * 8192 * 512, bytes_accessed=17 * 1024 * 1024, transcendentals=0
        ),
    )(at, *rows, *weights, query)


def pack_log(mine, other, other_lse):
    mine_lse = mine[:, 128]
    top = jnp.maximum(mine_lse, other_lse)
    mine_factor, other_factor = jnp.exp(mine_lse - top), jnp.exp(other_lse - top)
    both = mine_factor + other_factor
    lse = top + jnp.log(both)
    acc = mine_factor[:, None] * mine[:, :128] + other_factor[:, None] * other[:, :128]
    high = lax.reduce_precision(lse, 8, 7)
    mid = lax.reduce_precision(lse - high, 8, 7)
    terms = jnp.stack([high, mid, lse - high - mid])
    terms = jnp.pad(terms, ((0, 0), (0, 96)))
    return jnp.concatenate([acc / both[:, None], terms], axis=0).astype(jnp.bfloat16)


def on_device(
    prompt,
    kv_weight,
    norm_gain,
    kv_cache,
    block_table,
    context_len,
    dest_shard,
    new_query,
    new_keyval,
    out_weight,
):
    x_at, y_at, core = lax.axis_index("x"), lax.axis_index("y"), lax.axis_index("c")
    high = lax.axis_index("zh")
    shard = lax.axis_index(SEQ)
    request = shard // 4
    block_len = kv_cache.shape[1]
    width = new_query.shape[3]
    steps, requests, group = new_query.shape[:3]
    cached, own_blocks = block_table.shape

    half = prompt.shape[0] // 2
    lower = lax.ppermute(prompt, "y", UP)
    upper = lax.ppermute(prompt, "y", DOWN)
    lower_half, upper_half = lower[:half], upper[half:]
    query = lax.dynamic_index_in_dim(new_query, cached + request, 1, keepdims=False)
    query = query.reshape(steps * group, width)

    gain = lax.dynamic_slice_in_dim(norm_gain, shard * kv_weight.shape[0], kv_weight.shape[0])
    scaled = kv_weight.astype(jnp.float32) * gain.astype(jnp.float32)[:, None]
    first = spread(scaled.astype(jnp.bfloat16), RING, 8)

    step_peak, step_total, step_acc = step_stats(new_query, new_keyval[:, :, 0])
    cached_blocks = jnp.take(kv_cache[:, :, 0], block_table, axis=0, mode="clip")
    position = ((shard * own_blocks + jnp.arange(own_blocks, dtype=jnp.int32)) * block_len)[
        :, None
    ] + jnp.arange(block_len, dtype=jnp.int32)[None, :]
    usable = position[None, :, :] < context_len[:, None, None]
    peak, total, acc = paged_stats(new_query[:, :cached], cached_blocks, usable[None, :, None])
    packed = pack(peak.reshape(96), total.reshape(96), acc.reshape(96, width))
    old_step = pack(
        step_peak[:, :cached].reshape(96),
        step_total[:, :cached].reshape(96),
        step_acc[:, :cached].reshape(96, width),
    )
    old_step = lax.dynamic_slice_in_dim(old_step, shard * 3, 3, axis=0)
    step_peak = step_peak[:, cached:].transpose(1, 0, 2).reshape(8, 32)
    step_total = step_total[:, cached:].transpose(1, 0, 2).reshape(8, 32)
    step_acc = step_acc[:, cached:].transpose(1, 0, 2, 3).reshape(8, 32, width)
    x_of = (x_at + jnp.array([0, 3, 1, 0, 3, 1, 2, 2], jnp.int32)) % 4
    core_of = core ^ jnp.array([0, 0, 0, 1, 1, 1, 0, 1], jnp.int32)
    quarters = x_of[jnp.array([0, 1, 2, 6])] * 2048
    at = jnp.concatenate([x_of * 2048 + core_of * 256, high[None], quarters]).astype(jnp.int32)
    first, packed, query, at, old_step, step_peak, step_total, step_acc = (
        lax.optimization_barrier(
            (first, packed, query, at, old_step, step_peak, step_total, step_acc)
        )
    )
    query = jnp.stack([query, lax.ppermute(query, "zh", SWAP)])
    x_lower = lax.ppermute(first, "x", UP)
    x_upper = lax.ppermute(first, "x", DOWN)

    lower_half, upper_half, packed = lax.optimization_barrier((lower_half, upper_half, packed))
    across = [lax.ppermute(lower_half, "y", UP), lax.ppermute(upper_half, "y", DOWN)]
    x_lower, x_upper, *_ = lax.optimization_barrier((x_lower, x_upper, lower_half, upper_half))
    far = [lax.ppermute(x_lower[:4], "x", UP), lax.ppermute(x_upper[4:], "x", DOWN)]
    old_packed = lax.all_to_all(packed.reshape(32, 3, 256), SEQ, 0, 0, tiled=True)
    weights, across, old_packed, query = lax.optimization_barrier(
        ([first, x_lower, x_upper] + far, across, old_packed, query)
    )
    weights = weights + [lax.ppermute(piece, "c", SWAP) for piece in weights]
    rows = [pltpu.with_memory_space_constraint(prompt, pltpu.HBM), lower, upper] + across
    weights[1:3] = [pltpu.with_memory_space_constraint(part, pltpu.HBM) for part in weights[1:3]]
    kept, given, kept_stats = project(at, rows, weights, query)
    got = lax.ppermute(given, "zh", SWAP)
    got_stats = got[-32:].astype(jnp.float32)
    got_lse = jnp.sum(got_stats[:, width : width + 3], axis=1)
    old_packed, dest_shard, _ = lax.optimization_barrier((old_packed, dest_shard, given))
    old = merge(old_packed, old_step)
    packed = jnp.concatenate(
        [pack_log(kept_stats, got_stats, got_lse), old, jnp.zeros((2, width), jnp.bfloat16)], axis=0
    )
    packed = spread(packed, SEQ, 32)
    blocks = jnp.concatenate([kept, got[:-32]], axis=0).reshape(8, -1)

    targets = lax.dynamic_index_in_dim(dest_shard.reshape(32, 4, 2), shard, 0, keepdims=False)
    order = (y_at + jnp.array([0, 3, 1, 2], jnp.int32)) % 4
    mine = jnp.take(targets, order, axis=0, mode="clip").T
    mine = jnp.where(high == 0, mine, mine[::-1]).reshape(8)
    selector = (mine[None, :] == jnp.arange(32, dtype=jnp.int32)[:, None]).astype(jnp.bfloat16)
    outgoing = jnp.dot(selector, blocks, preferred_element_type=jnp.float32)
    outgoing = outgoing.astype(jnp.bfloat16).reshape(32, block_len, 2 * width)
    outgoing, packed = lax.optimization_barrier((outgoing, packed))
    landed = lax.all_to_all(outgoing, SEQ, 0, 0, tiled=True)[:, :, None, :]

    old = packed[:, 35:38].reshape(steps, cached, group, width)
    packed = packed.astype(jnp.float32).reshape(8, 4, 40, width)
    lse = packed[:, :, 32, :32] + packed[:, :, 33, :32] + packed[:, :, 34, :32]
    acc = packed[:, :, :32]
    top = jnp.maximum(jnp.max(lse, axis=1), step_peak)
    factor = jnp.exp(lse - top[:, None])
    step_factor = jnp.exp(step_peak - top)
    total = jnp.sum(factor, axis=1) + step_factor * step_total
    acc = jnp.sum(factor[..., None] * acc, axis=1) + step_factor[..., None] * step_acc
    new = (acc / total[..., None]).astype(jnp.bfloat16).reshape(8, steps, group, width)

    attended = jnp.concatenate([old, new.transpose(1, 0, 2, 3)], axis=1)
    flat_rows = attended.reshape(steps * requests, group * width)
    partial = jnp.dot(flat_rows, out_weight, preferred_element_type=jnp.float32).astype(jnp.bfloat16)
    summed = sum(part.astype(jnp.float32) for part in collect(partial, "y", 4))
    summed = summed + lax.ppermute(summed, "zh", SWAP)
    decoded = summed.astype(jnp.bfloat16).reshape(steps, requests, -1)
    return landed, decoded


def solution(mesh):
    fine = Mesh(mesh.devices.reshape(SIZES), NAMES)
    placed = (
        P(SEQ + TP, None),
        P(SEQ, TP),
        P(),
        P(SEQ, None, TP, None),
        P(None, SEQ),
        P(),
        P(),
        P(None, None, TP, None),
        P(None, None, TP, None),
        P(TP, SEQ),
    )
    return jax.shard_map(
        on_device,
        mesh=fine,
        in_specs=placed,
        out_specs=(P(SEQ, None, TP, None), P(None, None, SEQ)),
        check_vma=False,
    )
```
